128 devices in a mesh: ctx: 16 (over z, x), fsdp: 8 (over y, core).
Axes of the slice: x: 4, y: 4, z: 4, core: 2. Of those that a mesh axis runs over, the one named last changes fastest.
Arguments:
- tokens: bfloat16 [8, 2048, 768], P('fsdp', 'ctx'), may hold values from -6 to 6
- cotangent: bfloat16 [8, 2048, 768], P('fsdp', 'ctx'), may hold values from -6 to 6
- pair_order: int32 [16], replicated, may hold values from 0 to 15, each once
- first_gain: bfloat16 [768], P('fsdp'), may hold values from 0.5 to 1.5
- first_shift: bfloat16 [768], P('fsdp'), may hold values from -1.5 to 1.5
- qkv_weight: bfloat16 [768, 2304], P('fsdp'), may hold values from -0.3125 to 0.3125
- qv_bias: bfloat16 [1536], P('fsdp'), may hold values from -2.5 to 2.5
- out_weight: bfloat16 [768, 768], P('fsdp'), may hold values from -0.625 to 0.625
- out_bias: bfloat16 [768], P('fsdp'), may hold values from -1.5 to 1.5
- second_gain: bfloat16 [768], P('fsdp'), may hold values from 0.5 to 1.5
- second_shift: bfloat16 [768], P('fsdp'), may hold values from -1.5 to 1.5
- up_weight: bfloat16 [768, 3072], P('fsdp'), may hold values from -0.21875 to 0.21875
- up_bias: bfloat16 [3072], P('fsdp'), may hold values from -2.5 to 2.5
- down_weight: bfloat16 [3072, 768], P('fsdp'), may hold values from -0.15625 to 0.15625
- down_bias: bfloat16 [768], P('fsdp'), may hold values from -1.5 to 1.5
Outputs:
- mixed: bfloat16 [8, 2048, 768], P('fsdp', 'ctx')
- tokens_grad: float32 [8, 2048, 768], P('fsdp', 'ctx')
- first_gain_grad: float32 [768], P('fsdp')
- first_shift_grad: float32 [768], P('fsdp')
- qkv_weight_grad: float32 [768, 2304], P('fsdp')
- qv_bias_grad: float32 [1536], P('fsdp')
- out_weight_grad: float32 [768, 768], P('fsdp')
- out_bias_grad: float32 [768], P('fsdp')
- second_gain_grad: float32 [768], P('fsdp')
- second_shift_grad: float32 [768], P('fsdp')
- up_weight_grad: float32 [768, 3072], P('fsdp')
- up_bias_grad: float32 [3072], P('fsdp')
- down_weight_grad: float32 [3072, 768], P('fsdp')
- down_bias_grad: float32 [768], P('fsdp')
The draws below stay inside these ranges and needn't reach their ends.
Inputs may be any that keep to these rules, and one draw needn't show every extreme that they name: A permutation of 0 to 15; the blocks at stored block pair i are position blocks pair_order[i] and 31 - pair_order[i].
All inputs are finite; a program needn't handle non-finite values.
Results may differ from the reference program's by a relative error of at most 0.025.
Values may be sent and summed in bfloat16 or wider, within the bound.
No kernel may reach another device: no remote copies, remote signals or barrier semaphores. Data moves between devices by JAX's collectives and lax.ppermute only.
A program may use at most 128 MiB of HBM per device.

```python
import jax
import jax.numpy as jnp
from jax import lax

D = 768
HEADS = 12
FF = 3072
TOK_DEV = 128
HEAD_DIM = 64
SEQ = 2048
SEQS = 8
BLOCK_PAIRS = 16


def block_scale(rng, dims, cuts, low, top_value):
    loudness = 1.0
    for dim, parts in cuts:
        heights = jax.random.uniform(jax.random.fold_in(jax.random.fold_in(rng, 6), dim), (parts,), jnp.float32, low / len(cuts), top_value / len(cuts))
        loudness = loudness * jnp.repeat(jnp.exp(heights), dims[dim] // parts).reshape((-1,) + (1,) * (len(dims) - 1 - dim))
    return loudness


def bell_draw(stream_key, shape, width, most, shards=(), kind=jnp.bfloat16):
    array = jax.random.normal(stream_key, shape, jnp.float32) * width
    if len(shards) > 0:
        array = block_scale(stream_key, shape, shards, -0.22, 0.18) * array
    return jnp.clip(array, min=-most, max=most).astype(kind)


def setup_inputs(seed: int = 0) -> dict:
    seeds = jax.random.split(jax.random.key(seed), 16)
    return {
        "tokens": bell_draw(seeds[0], (SEQS, SEQ, D), 1.0, 6.0, ((0, 8), (1, 16))),
        "cotangent": bell_draw(seeds[1], (SEQS, SEQ, D), 1.0, 6.0, ((0, 8), (1, 16))),
        "pair_order": jax.random.permutation(seeds[2], BLOCK_PAIRS).astype(jnp.int32),
        "first_gain": jnp.clip(1.0 + 0.1 * jax.random.normal(seeds[3], (D,), jnp.float32), 0.5, 1.5).astype(jnp.bfloat16),
        "first_shift": bell_draw(seeds[4], (D,), 0.3, 1.5, ((0, 8),)),
        "qkv_weight": bell_draw(seeds[5], (D, 3 * D), (D // 2) ** -0.5, 0.3125, ((0, 8),)),
        "qv_bias": bell_draw(seeds[6], (2 * D,), 0.5, 2.5, ((0, 8),)),
        "out_weight": bell_draw(seeds[7], (D, D), (D // 8) ** -0.5, 0.625, ((0, 8),)),
        "out_bias": bell_draw(seeds[8], (D,), 0.3, 1.5, ((0, 8),)),
        "second_gain": jnp.clip(1.0 + 0.1 * jax.random.normal(seeds[9], (D,), jnp.float32), 0.5, 1.5).astype(jnp.bfloat16),
        "second_shift": bell_draw(seeds[10], (D,), 0.3, 1.5, ((0, 8),)),
        "up_weight": bell_draw(seeds[11], (D, FF), D ** -0.5, 0.21875, ((0, 8),)),
        "up_bias": bell_draw(seeds[12], (FF,), 0.5, 2.5, ((0, 8),)),
        "down_weight": bell_draw(seeds[13], (FF, D), (FF // 2) ** -0.5, 0.15625, ((0, 8),)),
        "down_bias": bell_draw(seeds[14], (D,), 0.3, 1.5, ((0, 8),)),
    }


EPSILON = 1e-05
NEGATIVE = -1e+30
HIGHEST = lax.Precision.HIGHEST

@jax.custom_vjp
def low(v):
    return lax.optimization_barrier(v.astype(jnp.bfloat16)).astype(jnp.float32)

@jax.custom_vjp
def low_back(v):
    return v

def low_keep(v):
    return (low(v), None)

def low_pass(kept, grad):
    return (grad,)

def back_keep(v):
    return (v, None)

def back_low(kept, grad):
    return (low(grad),)
low.defvjp(low_keep, low_pass)
low_back.defvjp(back_keep, back_low)

def layer_norm(values, scale_row, shift_row):
    center = values - lax.optimization_barrier(jnp.mean(values, axis=-1, keepdims=True))
    spread = lax.optimization_barrier(jnp.mean(center * center, axis=-1, keepdims=True))
    return center * lax.rsqrt(spread + EPSILON) * scale_row + shift_row

def positions_of(pair_order, row_count):
    pair_count = pair_order.shape[0]
    half_rows = row_count // 2
    stored = jnp.arange(pair_count * row_count, dtype=jnp.int32)
    device_of = stored // row_count
    inside = stored % row_count
    chosen = lax.optimization_barrier(jnp.sum(jnp.where(device_of[:, None] == jnp.arange(pair_count, dtype=jnp.int32)[None, :], pair_order[None, :], 0), axis=1)).astype(jnp.int32)
    block_of = jnp.where(inside < half_rows, chosen, 2 * pair_count - 1 - chosen)
    return (block_of * half_rows + inside % half_rows).astype(jnp.int32)

def attend_block(queries, query_places, keys_all, values_all, key_places):
    scaling = HEAD_DIM ** (-0.5)
    raw_scores = low_back(jnp.einsum('qhe,khe->qhk', queries, keys_all, precision=HIGHEST))
    scores = raw_scores * scaling
    allowed = key_places[None, None, :] <= query_places[:, None, None]
    masked = jnp.where(allowed, scores, NEGATIVE)
    row_top = lax.optimization_barrier(jnp.max(masked, axis=2, keepdims=True))
    raised = jnp.where(allowed, jnp.exp(masked - row_top), 0.0)
    weights = raised / lax.optimization_barrier(jnp.sum(raised, axis=2, keepdims=True))
    return jnp.einsum('qhk,khe->qhe', low(weights), values_all, precision=HIGHEST)

def attention(query, key, value, key_places):
    seq_len = query.shape[0]
    block_size = min(512, seq_len)
    block_count = seq_len // block_size
    query_blocks = query.reshape(block_count, block_size, HEADS, HEAD_DIM)
    place_blocks = key_places.reshape(block_count, block_size)
    keys_all = key.reshape(seq_len, HEADS, HEAD_DIM)
    values_all = value.reshape(seq_len, HEADS, HEAD_DIM)
    checked = jax.checkpoint(attend_block)
    attended = lax.map(lambda pieces: checked(pieces[0], pieces[1], keys_all, values_all, key_places), (query_blocks, place_blocks))
    return attended.reshape(seq_len, HEADS * HEAD_DIM)

def forward(inputs, params, key_places):
    gain_one, shift_one, w_qkv, b_qv, w_out, b_out, gain_two, shift_two, w_up, b_up, w_down, b_down = params
    model_width = inputs.shape[1]
    normed_one = low(layer_norm(inputs, gain_one, shift_one))
    projected = jnp.dot(normed_one, w_qkv, precision=HIGHEST)
    query = low(low_back(projected[:, :model_width] + b_qv[:model_width]))
    key = low(low_back(projected[:, model_width:2 * model_width]))
    value = low(low_back(projected[:, 2 * model_width:] + b_qv[model_width:]))
    attended = low(low_back(attention(query, key, value, key_places)))
    residual = inputs + low_back(jnp.dot(attended, w_out, precision=HIGHEST) + b_out)
    normed_two = low(layer_norm(residual, gain_two, shift_two))
    hidden_pre = low_back(jnp.dot(normed_two, w_up, precision=HIGHEST) + b_up)
    active = low(jax.nn.gelu(hidden_pre, approximate=True))
    return residual + low_back(jnp.dot(active, w_down, precision=HIGHEST) + b_down)

def reference(tokens, cotangent, pair_order, first_gain, first_shift, qkv_weight, qv_bias, out_weight, out_bias, second_gain, second_shift, up_weight, up_bias, down_weight, down_bias):
    params = (first_gain.astype(jnp.float32), first_shift.astype(jnp.float32), qkv_weight.astype(jnp.float32), qv_bias.astype(jnp.float32), out_weight.astype(jnp.float32), out_bias.astype(jnp.float32), second_gain.astype(jnp.float32), second_shift.astype(jnp.float32), up_weight.astype(jnp.float32), up_bias.astype(jnp.float32), down_weight.astype(jnp.float32), down_bias.astype(jnp.float32))
    key_places = positions_of(pair_order, TOK_DEV)

    def per_sequence(running, pieces):
        inputs, grad_result = pieces
        result, pullback = jax.vjp(lambda values, weights: forward(values, weights, key_places), inputs, params)
        grad_inputs, grad_params = pullback(grad_result)
        running = jax.tree.map(jnp.add, running, grad_params)
        return (running, (result.astype(jnp.bfloat16), grad_inputs))
    start = jax.tree.map(jnp.zeros_like, params)
    sums, (mixed, tokens_grad) = lax.scan(per_sequence, start, (tokens.astype(jnp.float32), cotangent.astype(jnp.float32)))
    return (mixed, tokens_grad, sums[0], sums[1], sums[2], sums[3], sums[4], sums[5], sums[6], sums[7], sums[8], sums[9], sums[10], sums[11])
```

```python
import jax
import jax.numpy as jnp
from jax import lax
from jax.experimental import pallas as pl
from jax.experimental.pallas import tpu as pltpu
from jax.sharding import PartitionSpec as P

HEADS = 12
DEPTH = 64
WIDTH = 768
HIDDEN = 3072
ROWS = 128
HALF = 64
CTX = 16
FSDP = 8
SEQ = CTX * ROWS
QT = 256
KT = 512
EPSILON = 1e-05
NEGATIVE = -1e30
VMEM_LIMIT = 56 * 1024 * 1024

BF = jnp.bfloat16
F32 = jnp.float32

VECTORS = (
    ("first_gain", 96),
    ("first_shift", 96),
    ("qv_bias", 192),
    ("out_bias", 96),
    ("second_gain", 96),
    ("second_shift", 96),
    ("up_bias", 384),
    ("down_bias", 96),
)
VECTOR_WIDTH = sum(width for _, width in VECTORS)

OUT_AT, UP_AT, DOWN_AT, PACK_ROWS = 0, 96, 480, 864


def dot(left, right):
    return jnp.dot(left, right, preferred_element_type=F32)


def dot_nt(left, right):
    return lax.dot_general(left, right, (((1,), (1,)), ((), ())), preferred_element_type=F32)


def dot_tn(left, right):
    return lax.dot_general(left, right, (((0,), (0,)), ((), ())), preferred_element_type=F32)


def normalise(values):
    center = values - jnp.mean(values, axis=-1, keepdims=True)
    spread = jnp.mean(center * center, axis=-1, keepdims=True)
    inverse = lax.rsqrt(spread + EPSILON)
    return center * inverse, inverse


def norm_back(upstream, hat, inverse, gain):
    scaled = upstream * gain
    mean_one = jnp.mean(scaled, axis=-1, keepdims=True)
    mean_two = jnp.mean(scaled * hat, axis=-1, keepdims=True)
    return (scaled - mean_one - hat * mean_two) * inverse


def block_at(index):
    return pl.ds(pl.multiple_of(index * HALF, HALF), HALF)


def lanes_at(index, size):
    return pl.ds(pl.multiple_of(index * size, size), size)


def vmem_call(kernel, out_shape, scratch, flops, in_vmem, smem_first=False, transcendentals=0):
    specs = [pl.BlockSpec(memory_space=pltpu.VMEM)] * in_vmem
    if smem_first:
        specs = [pl.BlockSpec(memory_space=pltpu.SMEM)] + specs
    return pl.pallas_call(
        kernel,
        out_shape=out_shape,
        in_specs=specs,
        out_specs=[pl.BlockSpec(memory_space=pltpu.VMEM)] * len(out_shape),
        scratch_shapes=scratch,
        compiler_params=pltpu.CompilerParams(vmem_limit_bytes=VMEM_LIMIT),
        cost_estimate=pl.CostEstimate(
            flops=flops, bytes_accessed=8 * 2**20, transcendentals=transcendentals
        ),
    )


def head_forward_kernel(
    order, tok, weight, bias, gain, shift,
    packed, normed, query, key, value, query_t, key_t, out_t, lse,
    value_t,
):
    def project(c, _):
        hat, _inv = normalise(tok[c].astype(F32))
        low = (hat * gain[...] + shift[...]).astype(BF)
        made = (dot(low, weight[...]) + bias[...]).astype(BF)
        place = order[c]
        for part, block in ((0, place), (1, 2 * CTX - 1 - place)):
            rows = slice(part * HALF, (part + 1) * HALF)
            normed[block_at(block), :] = low[rows]
            query[block_at(block), :] = made[rows, 0:DEPTH]
            key[block_at(block), :] = made[rows, DEPTH : 2 * DEPTH]
            value[block_at(block), :] = made[rows, 2 * DEPTH :]
        return 0

    lax.fori_loop(0, CTX, project, 0)

    def turn(t, _):
        rows = lanes_at(t, QT)
        for source, target in ((query, query_t), (key, key_t), (value, value_t)):
            target[:, rows] = source[rows, :].astype(F32).T.astype(BF)
        return 0

    lax.fori_loop(0, SEQ // QT, turn, 0)

    def attend(i, _):
        lanes = lanes_at(i, QT)
        queries = query_t[:, lanes]

        def step(j, carry, masked):
            top, total, acc = carry
            rows = lanes_at(j, KT)
            scores = dot(key[rows, :], queries) * (DEPTH ** -0.5)
            if masked:
                key_place = j * KT + lax.broadcasted_iota(jnp.int32, (KT, QT), 0)
                query_place = i * QT + lax.broadcasted_iota(jnp.int32, (KT, QT), 1)
                scores = jnp.where(key_place <= query_place, scores, NEGATIVE)
            fresh = jnp.maximum(top, jnp.max(scores, axis=0, keepdims=True))
            raised = jnp.exp(scores - fresh)
            fade = jnp.exp(top - fresh)
            total = total * fade + jnp.sum(raised, axis=0, keepdims=True)
            acc = acc * fade + dot(value_t[:, rows], raised.astype(BF))
            return fresh, total, acc

        start = (
            jnp.full((1, QT), NEGATIVE, F32),
            jnp.zeros((1, QT), F32),
            jnp.zeros((DEPTH, QT), F32),
        )
        full = i // 2
        carry = lax.fori_loop(0, full, lambda j, carry: step(j, carry, False), start)
        top, total, acc = step(full, carry, True)
        result = acc / total
        out_t[:, lanes] = result
        lse[pl.ds(i, 1), :] = top + jnp.log(total)
        return 0

    lax.fori_loop(0, SEQ // QT, attend, 0)


def head_forward(order, tok, weight, bias, gain, shift):
    def kernel(
        order, tok, weight, bias, gain, shift,
        packed, normed, query, key, value, query_t, key_t, out_t, lse,
        value_t, out_rows,
    ):
        head_forward_kernel(
            order, tok, weight, bias, gain, shift,
            packed, normed, query, key, value, query_t, key_t, out_t, lse,
            value_t,
        )

        def turn_back(t, _):
            rows = lanes_at(t, QT)
            out_rows[rows, :] = out_t[:, rows].T
            return 0

        lax.fori_loop(0, SEQ // QT, turn_back, 0)

        def pack(c, _):
            place = order[c]
            packed[c] = jnp.concatenate(
                [out_rows[block_at(place), :], out_rows[block_at(2 * CTX - 1 - place), :]], axis=1
            ).astype(BF)
            return 0

        lax.fori_loop(0, CTX, pack, 0)

    shape = jax.ShapeDtypeStruct
    return vmem_call(
        kernel,
        [
            shape((CTX, HALF, 2 * DEPTH), BF),
            shape((SEQ, WIDTH), BF),
            shape((SEQ, DEPTH), BF),
            shape((SEQ, DEPTH), BF),
            shape((SEQ, DEPTH), BF),
            shape((DEPTH, SEQ), BF),
            shape((DEPTH, SEQ), BF),
            shape((DEPTH, SEQ), F32),
            shape((SEQ // QT, QT), F32),
        ],
        [pltpu.VMEM((DEPTH, SEQ), BF), pltpu.VMEM((SEQ, DEPTH), F32)],
        2 * 10**9,
        5,
        smem_first=True,
        transcendentals=3 * 10**6,
    )(order, tok, weight, bias, gain, shift)


def head_backward(order, upstream, normed, query, key, value, query_t, key_t, out_t, lse):
    def kernel(
        order, upstream, normed, query, key, value, query_t, key_t, out_t, lse,
        packed, weight_grad, bias_grad,
        grad_out, grad_out_t, delta, grad_q_t, grad_k, grad_v, rows_low,
    ):
        def unpack(c, _):
            place = order[c]
            grad_out[block_at(place), :] = upstream[c][:, :DEPTH]
            grad_out[block_at(2 * CTX - 1 - place), :] = upstream[c][:, DEPTH:]
            return 0

        lax.fori_loop(0, CTX, unpack, 0)

        def prepare(t, _):
            rows = lanes_at(t, QT)
            turned = grad_out[rows, :].astype(F32).T
            grad_out_t[:, rows] = turned.astype(BF)
            delta[pl.ds(t, 1), :] = jnp.sum(turned * out_t[:, rows], axis=0, keepdims=True)
            grad_q_t[:, rows] = jnp.zeros((DEPTH, QT), F32)
            grad_k[rows, :] = jnp.zeros((QT, DEPTH), F32)
            grad_v[rows, :] = jnp.zeros((QT, DEPTH), F32)
            return 0

        lax.fori_loop(0, SEQ // QT, prepare, 0)

        def one_query_tile(i, _):
            lanes = lanes_at(i, QT)

            def step(j, masked):
                rows = lanes_at(j, KT)
                scores = dot(key[rows, :], query_t[:, lanes]) * (DEPTH ** -0.5)
                probs = jnp.exp(scores - lse[pl.ds(i, 1), :])
                if masked:
                    key_place = j * KT + lax.broadcasted_iota(jnp.int32, (KT, QT), 0)
                    query_place = i * QT + lax.broadcasted_iota(jnp.int32, (KT, QT), 1)
                    probs = jnp.where(key_place <= query_place, probs, 0.0)
                slopes = dot(value[rows, :], grad_out_t[:, lanes])
                grad_scores = (
                    probs * (slopes - delta[pl.ds(i, 1), :]) * (DEPTH ** -0.5)
                ).astype(BF)
                grad_v[rows, :] += dot(probs.astype(BF), grad_out[lanes, :])
                grad_k[rows, :] += dot(grad_scores, query[lanes, :])
                grad_q_t[:, lanes] += dot(key_t[:, rows], grad_scores)

            full = i // 2

            def body(j, _):
                step(j, False)
                return 0

            lax.fori_loop(0, full, body, 0)
            step(full, True)
            return 0

        lax.fori_loop(0, SEQ // QT, one_query_tile, 0)

        def finish(t, sums):
            rows = lanes_at(t, QT)
            low_q = grad_q_t[:, rows].T.astype(BF)
            low_k = grad_k[rows, :].astype(BF)
            low_v = grad_v[rows, :].astype(BF)
            joined = jnp.concatenate(
                [low_q.astype(F32), low_k.astype(F32), low_v.astype(F32)], axis=1
            )
            rows_low[rows, :] = joined
            return sums + jnp.sum(joined, axis=0, keepdims=True)

        sums = lax.fori_loop(0, SEQ // QT, finish, jnp.zeros((1, 3 * DEPTH), F32))
        bias_grad[...] = sums

        weight_grad[...] = (
            dot_tn(normed[...], rows_low[...].astype(BF))
            .astype(BF)
            .reshape(FSDP, WIDTH // FSDP, 3 * DEPTH)
        )

        def pack(c, _):
            place = order[c]
            upper = rows_low[block_at(place), :]
            lower = rows_low[block_at(2 * CTX - 1 - place), :]
            pieces = []
            for part in range(3):
                lanes = slice(part * DEPTH, (part + 1) * DEPTH)
                pieces += [upper[:, lanes], lower[:, lanes]]
            packed[c] = jnp.concatenate(pieces, axis=1).astype(BF)
            return 0

        lax.fori_loop(0, CTX, pack, 0)

    shape = jax.ShapeDtypeStruct
    return vmem_call(
        kernel,
        [
            shape((CTX, HALF, 6 * DEPTH), BF),
            shape((FSDP, WIDTH // FSDP, 3 * DEPTH), BF),
            shape((1, 3 * DEPTH), F32),
        ],
        [
            pltpu.VMEM((SEQ, DEPTH), BF),
            pltpu.VMEM((DEPTH, SEQ), BF),
            pltpu.VMEM((SEQ // QT, QT), F32),
            pltpu.VMEM((DEPTH, SEQ), F32),
            pltpu.VMEM((SEQ, DEPTH), F32),
            pltpu.VMEM((SEQ, DEPTH), F32),
            pltpu.VMEM((SEQ, 3 * DEPTH), F32),
        ],
        4 * 10**9,
        9,
        smem_first=True,
        transcendentals=3 * 10**6,
    )(order, upstream, normed, query, key, value, query_t, key_t, out_t, lse)


def unpack_heads(ref, lanes):
    upper, lower = [], []
    for head in range(HEADS):
        slot = ref[head][:, lanes : lanes + 2 * DEPTH].astype(F32)
        upper.append(slot[:, :DEPTH])
        lower.append(slot[:, DEPTH:])
    return jnp.concatenate(
        [jnp.concatenate(upper, axis=1), jnp.concatenate(lower, axis=1)], axis=0
    ).astype(BF)


def gelu_parts(values):
    slope = 0.7978845608028654
    cubic = 0.044715
    squared = values * values
    bend = jnp.tanh(slope * (values + cubic * squared * values))
    active = 0.5 * values * (1.0 + bend)
    grad = 0.5 * (1.0 + bend) + 0.5 * values * (1.0 - bend * bend) * slope * (
        1.0 + 3.0 * cubic * squared
    )
    return active, grad


def feed_forward(tokens, heads_out, cotangent, pack, out_bias, gain, shift, up_bias, down_bias):
    def kernel(
        tokens, heads_out, cotangent, pack, out_bias, gain, shift, up_bias, down_bias,
        mixed, attended, normed, active, grad_pre, grad_branch, grad_heads, grad_residual,
        vector_sums, up_sums,
    ):
        inputs = tokens[...].astype(F32)
        result_grad = cotangent[...]
        attended_low = unpack_heads(heads_out, 0)
        attended[...] = attended_low
        w_out = pack[:, OUT_AT:UP_AT, :].reshape(WIDTH, WIDTH)
        residual = inputs + dot(attended_low, w_out) + out_bias[...]
        hat, inverse = normalise(residual)
        low = (hat * gain[...] + shift[...]).astype(BF)
        normed[...] = low
        total = residual + down_bias[...]
        grad_normed = jnp.zeros((ROWS, WIDTH), F32)
        for j in range(HIDDEN // WIDTH):
            lanes = slice(j * WIDTH, (j + 1) * WIDTH)
            w_up = pack[:, UP_AT + 96 * j : UP_AT + 96 * (j + 1), :].reshape(WIDTH, WIDTH)
            w_down = pack[2 * j : 2 * j + 2, DOWN_AT:PACK_ROWS, :].reshape(WIDTH, WIDTH)
            hidden = dot(low, w_up) + up_bias[:, lanes]
            acted, slope = gelu_parts(hidden)
            acted = acted.astype(BF)
            active[:, lanes] = acted
            total = total + dot(acted, w_down)
            pre = (dot_nt(result_grad, w_down) * slope).astype(BF)
            grad_pre[:, lanes] = pre
            up_sums[:, lanes] = jnp.sum(pre.astype(F32), axis=0, keepdims=True)
            grad_normed = grad_normed + dot_nt(pre, w_up)
        mixed[...] = total.astype(BF)
        back = result_grad.astype(F32) + norm_back(grad_normed, hat, inverse, gain[...])
        grad_residual[...] = back
        branch = back.astype(BF)
        grad_branch[...] = branch
        vector_sums[0:1, :] = jnp.sum(branch.astype(F32), axis=0, keepdims=True)
        vector_sums[1:2, :] = jnp.sum(grad_normed * hat, axis=0, keepdims=True)
        vector_sums[2:3, :] = jnp.sum(grad_normed, axis=0, keepdims=True)
        vector_sums[3:4, :] = jnp.sum(result_grad.astype(F32), axis=0, keepdims=True)
        grad_attended = dot_nt(branch, w_out)
        for head in range(HEADS):
            lanes = slice(head * DEPTH, (head + 1) * DEPTH)
            grad_heads[head] = jnp.concatenate(
                [grad_attended[:HALF, lanes], grad_attended[HALF:, lanes]], axis=1
            ).astype(BF)
        for head in range(HEADS, CTX):
            grad_heads[head] = jnp.zeros((HALF, 2 * DEPTH), BF)

    shape = jax.ShapeDtypeStruct
    return vmem_call(
        kernel,
        [
            shape((ROWS, WIDTH), BF),
            shape((ROWS, WIDTH), BF),
            shape((ROWS, WIDTH), BF),
            shape((ROWS, HIDDEN), BF),
            shape((ROWS, HIDDEN), BF),
            shape((ROWS, WIDTH), BF),
            shape((CTX, HALF, 2 * DEPTH), BF),
            shape((ROWS, WIDTH), F32),
            shape((4, WIDTH), F32),
            shape((1, HIDDEN), F32),
        ],
        [],
        4 * 10**9,
        9,
    )(tokens, heads_out, cotangent, pack, out_bias, gain, shift, up_bias, down_bias)


def weight_grads(left, right, blocks):
    def kernel(left, right, out):
        for j in range(blocks):
            made = dot_tn(left[...], right[:, j * WIDTH : (j + 1) * WIDTH])
            out[:, 96 * j : 96 * (j + 1), :] = made.astype(BF).reshape(FSDP, 96, WIDTH)

    return vmem_call(
        kernel,
        [jax.ShapeDtypeStruct((FSDP, 96 * blocks, WIDTH), BF)],
        [],
        2 * ROWS * WIDTH * WIDTH * blocks,
        2,
    )(left, right)[0]


def token_gradient(tokens, heads_grad, weight, gain, grad_residual):
    def kernel(tokens, heads_grad, weight, gain, grad_residual, tokens_grad, sums):
        projected = jnp.concatenate(
            [unpack_heads(heads_grad, 2 * DEPTH * part) for part in range(3)], axis=1
        )
        grad_normed = dot_nt(projected, weight[...])
        hat, inverse = normalise(tokens[...].astype(F32))
        tokens_grad[...] = grad_residual[...] + norm_back(grad_normed, hat, inverse, gain[...])
        sums[0:1, :] = jnp.sum(grad_normed * hat, axis=0, keepdims=True)
        sums[1:2, :] = jnp.sum(grad_normed, axis=0, keepdims=True)

    shape = jax.ShapeDtypeStruct
    return vmem_call(
        kernel,
        [shape((ROWS, WIDTH), F32), shape((2, WIDTH), F32)],
        [],
        2 * ROWS * WIDTH * 3 * WIDTH,
        5,
    )(tokens, heads_grad, weight, gain, grad_residual)


def swap(slots, axes):
    return lax.all_to_all(slots, axes, 0, 0, tiled=True)


def spread(piece, axes, count):
    return swap(jnp.broadcast_to(piece[None], (count,) + piece.shape), axes)


def reduce_over_ctx(shard):
    rows = shard.shape[0] // CTX
    parts = swap(shard.reshape(CTX, rows, WIDTH), "ctx")
    mine = jnp.sum(parts.astype(F32), axis=0).astype(BF)
    return spread(mine, "ctx", CTX).reshape(shard.shape).astype(F32)


def local(
    tokens, cotangent, pair_order, first_gain, first_shift, qkv_weight, qv_bias, out_weight,
    out_bias, second_gain, second_shift, up_weight, up_bias, down_weight, down_bias,
):
    my_tokens, my_cotangent = tokens[0], cotangent[0]
    place = lax.axis_index("ctx")
    head = place % HEADS
    shards = dict(
        first_gain=first_gain, first_shift=first_shift, qv_bias=qv_bias, out_bias=out_bias,
        second_gain=second_gain, second_shift=second_shift, up_bias=up_bias, down_bias=down_bias,
    )

    with jax.named_scope("gather_tokens"):
        all_tokens = spread(my_tokens, "ctx", CTX)
    with jax.named_scope("gather_weights"):
        pack = jnp.concatenate(
            [out_weight]
            + [up_weight[:, j * WIDTH : (j + 1) * WIDTH] for j in range(HIDDEN // WIDTH)]
            + [down_weight],
            axis=0,
        )
        pack = lax.all_gather(pack, "fsdp", axis=0, tiled=False)
        w_qkv = lax.all_gather(qkv_weight, "fsdp", axis=0, tiled=True)
    with jax.named_scope("gather_small"):
        head_columns = jnp.concatenate(
            [
                lax.dynamic_slice_in_dim(qkv_weight, part * WIDTH + head * DEPTH, DEPTH, 1)
                for part in range(3)
            ],
            axis=1,
        )
        vectors = jnp.concatenate([shards[name] for name, _ in VECTORS]).reshape(6, 3 * DEPTH)
        small = jnp.concatenate(
            [head_columns, vectors, jnp.zeros((10, 3 * DEPTH), BF)], axis=0
        )
        small = spread(small, "fsdp", FSDP)
        w_head = small[:, :96].reshape(WIDTH, 3 * DEPTH)
        vectors = small[:, 96:102].reshape(FSDP, VECTOR_WIDTH).astype(F32)
        whole, at = {}, 0
        for name, width in VECTORS:
            whole[name] = vectors[:, at : at + width].reshape(1, FSDP * width)
            at += width
        head_bias = jnp.concatenate(
            [
                lax.dynamic_slice_in_dim(whole["qv_bias"], head * DEPTH, DEPTH, 1),
                jnp.zeros((1, DEPTH), F32),
                lax.dynamic_slice_in_dim(whole["qv_bias"], WIDTH + head * DEPTH, DEPTH, 1),
            ],
            axis=1,
        )

    with jax.named_scope("attention"):
        packed, normed, query, key, value, query_t, key_t, out_t, lse = head_forward(
            pair_order, all_tokens, w_head, head_bias, whole["first_gain"], whole["first_shift"]
        )
        heads_out = swap(packed, "ctx")

    with jax.named_scope("feed_forward"):
        (
            mixed, attended, normed_two, active, grad_pre, grad_branch, grad_heads,
            grad_residual, vector_sums, up_sums,
        ) = feed_forward(
            my_tokens, heads_out, my_cotangent, pack, whole["out_bias"], whole["second_gain"],
            whole["second_shift"], whole["up_bias"], whole["down_bias"],
        )
        heads_up = swap(grad_heads, "ctx")

    with jax.named_scope("feed_forward_weights"):
        grad_down = lax.dot_general(
            active, my_cotangent, (((0,), (0,)), ((), ())), preferred_element_type=F32
        ).astype(BF).reshape(FSDP, 384, WIDTH)
        grad_down = lax.psum_scatter(grad_down, "fsdp", scatter_dimension=0, tiled=False)
        grad_up = weight_grads(normed_two, grad_pre, 4)
        grad_up = lax.psum_scatter(grad_up, "fsdp", scatter_dimension=0, tiled=False)
        grad_out = weight_grads(attended, grad_branch, 1)
        grad_out = lax.psum_scatter(grad_out, "fsdp", scatter_dimension=0, tiled=False)

    with jax.named_scope("attention_back"):
        packed_grad, head_weight_grad, head_bias_grad = head_backward(
            pair_order, heads_up, normed, query, key, value, query_t, key_t, out_t, lse
        )
        heads_grad = swap(packed_grad, "ctx")
    with jax.named_scope("head_weights"):
        parts = swap(head_weight_grad, "fsdp")
        mine = jnp.sum(parts.astype(F32), axis=0).astype(BF)
        head_parts = spread(mine, "ctx", CTX)[:HEADS].astype(F32)
        grad_qkv = (
            head_parts.reshape(HEADS, 96, 3, DEPTH).transpose(1, 2, 0, 3).reshape(96, 3 * WIDTH)
        )

    with jax.named_scope("token_gradient"):
        tokens_grad, first_sums = token_gradient(
            my_tokens, heads_grad, w_qkv, whole["first_gain"], grad_residual
        )

    with jax.named_scope("vector_grads"):
        holds = (jnp.arange(HEADS) == place).astype(F32)[:, None]
        bias_sums = jnp.concatenate(
            [
                (holds * head_bias_grad[:, :DEPTH]).reshape(1, WIDTH),
                (holds * head_bias_grad[:, 2 * DEPTH :]).reshape(1, WIDTH),
            ],
            axis=1,
        )
        sums = dict(
            first_gain=first_sums[0:1], first_shift=first_sums[1:2], qv_bias=bias_sums,
            out_bias=vector_sums[0:1], second_gain=vector_sums[1:2],
            second_shift=vector_sums[2:3], up_bias=up_sums, down_bias=vector_sums[3:4],
        )
        sums = jnp.concatenate(
            [sums[name].reshape(FSDP, width) for name, width in VECTORS], axis=1
        ).astype(BF)
        slots = jnp.broadcast_to(
            sums.reshape(1, FSDP, VECTOR_WIDTH // 128, 128), (CTX, FSDP, VECTOR_WIDTH // 128, 128)
        ).reshape(CTX * FSDP, VECTOR_WIDTH // 128, 128)
        mine = jnp.sum(swap(slots, ("ctx", "fsdp")).astype(F32), axis=0).reshape(VECTOR_WIDTH)
        grads, at = {}, 0
        for name, width in VECTORS:
            grads[name] = mine[at : at + width]
            at += width

    with jax.named_scope("sum_over_ctx"):
        grad_down = reduce_over_ctx(grad_down)
        grad_up = reduce_over_ctx(grad_up)
        grad_up = jnp.concatenate(
            [grad_up[96 * j : 96 * (j + 1)] for j in range(HIDDEN // WIDTH)], axis=1
        )
        grad_out = reduce_over_ctx(
            jnp.concatenate([grad_out, jnp.zeros((32, WIDTH), BF)], axis=0)
        )[:96]

    return (
        mixed[None], tokens_grad[None], grads["first_gain"], grads["first_shift"], grad_qkv,
        grads["qv_bias"], grad_out, grads["out_bias"], grads["second_gain"],
        grads["second_shift"], grad_up, grads["up_bias"], grad_down, grads["down_bias"],
    )


def solution(mesh):
    split, vector = P("fsdp", "ctx", None), P("fsdp")
    matrix = P("fsdp", None)
    in_specs = (
        split, split, P(), vector, vector, matrix, vector, matrix, vector, vector, vector,
        matrix, vector, matrix, vector,
    )
    out_specs = (
        split, split, vector, vector, matrix, vector, matrix, vector, vector, vector, matrix,
        vector, matrix, vector,
    )
    return jax.shard_map(local, mesh=mesh, in_specs=in_specs, out_specs=out_specs, check_vma=False)
```

```python
import jax
import jax.numpy as jnp
from jax import lax
from jax.experimental import pallas as pl
from jax.experimental.pallas import tpu as pltpu
from jax.sharding import PartitionSpec as P

HEADS = 12
DEPTH = 64
WIDTH = 768
HIDDEN = 3072
ROWS = 128
HALF = 64
CTX = 16
FSDP = 8
SIDE = 4
SEQ = CTX * ROWS
QT = 512
KT = 512
EPSILON = 1e-05
NEGATIVE = -1e30
VMEM_LIMIT = 56 * 1024 * 1024

BF = jnp.bfloat16
F32 = jnp.float32

VECTORS = (
    ("first_gain", 96),
    ("first_shift", 96),
    ("qv_bias", 192),
    ("out_bias", 96),
    ("second_gain", 96),
    ("second_shift", 96),
    ("up_bias", 384),
    ("down_bias", 96),
)
VECTOR_WIDTH = sum(width for _, width in VECTORS)

OUT_AT, UP_AT, DOWN_AT, PACK_ROWS = 0, 96, 480, 864
CTX_ROWS = PACK_ROWS // CTX
LAST_ROWS = CTX_ROWS + 26


def dot(left, right):
    return jnp.dot(left, right, preferred_element_type=F32)


def dot_nt(left, right):
    return lax.dot_general(left, right, (((1,), (1,)), ((), ())), preferred_element_type=F32)


def dot_tn(left, right):
    return lax.dot_general(left, right, (((0,), (0,)), ((), ())), preferred_element_type=F32)


def normalise(values):
    center = values - jnp.mean(values, axis=-1, keepdims=True)
    spread = jnp.mean(center * center, axis=-1, keepdims=True)
    inverse = lax.rsqrt(spread + EPSILON)
    return center * inverse, inverse


def norm_back(upstream, hat, inverse, gain):
    scaled = upstream * gain
    mean_one = jnp.mean(scaled, axis=-1, keepdims=True)
    mean_two = jnp.mean(scaled * hat, axis=-1, keepdims=True)
    return (scaled - mean_one - hat * mean_two) * inverse


UNROLL = True


def loop(count, body):
    if UNROLL:
        for step in range(count):
            body(step, 0)
    else:
        lax.fori_loop(0, count, body, 0)


def block_at(index):
    return pl.ds(pl.multiple_of(index * HALF, HALF), HALF)


def lanes_at(index, size):
    if isinstance(index, int):
        return pl.ds(index * size, size)
    return pl.ds(pl.multiple_of(index * size, size), size)


def vmem_call(kernel, out_shape, scratch, flops, in_vmem, smem=0, transcendentals=0):
    specs = [pl.BlockSpec(memory_space=pltpu.VMEM)] * in_vmem
    specs = [pl.BlockSpec(memory_space=pltpu.SMEM)] * smem + specs
    return pl.pallas_call(
        kernel,
        out_shape=out_shape,
        in_specs=specs,
        out_specs=[pl.BlockSpec(memory_space=pltpu.VMEM)] * len(out_shape),
        scratch_shapes=scratch,
        compiler_params=pltpu.CompilerParams(vmem_limit_bytes=VMEM_LIMIT),
        cost_estimate=pl.CostEstimate(
            flops=flops, bytes_accessed=8 * 2**20, transcendentals=transcendentals
        ),
    )


def normalised_rows(tokens):
    def kernel(tokens, hat):
        hat[...] = normalise(tokens[...].astype(F32))[0].astype(BF)

    return vmem_call(
        kernel, [jax.ShapeDtypeStruct((ROWS, WIDTH), BF)], [], 10**6, 1
    )(tokens)[0]


def head_forward_kernel(
    order, where, blocks, weight, bias, gain, shift,
    packed, normed, query, key, value, query_t, key_t, out_t, lse,
    value_t,
):
    at_z, at_x = where[0] // SIDE, lax.rem(where[0], SIDE)

    for half, offsets, block in blocks:
        count = len(offsets)
        hat = block[...].reshape(count * HALF, WIDTH).astype(F32)
        low = (hat * gain[...] + shift[...]).astype(BF)
        made = (dot(low, weight[...]) + bias[...]).astype(BF)
        for n, (dz, dx) in enumerate(offsets):
            place = order[lax.rem(at_z + dz, SIDE) * SIDE + lax.rem(at_x + dx, SIDE)]
            to = block_at(place if half == 0 else 2 * CTX - 1 - place)
            rows = slice(n * HALF, (n + 1) * HALF)
            normed[to, :] = low[rows]
            query[to, :] = made[rows, 0:DEPTH]
            key[to, :] = made[rows, DEPTH : 2 * DEPTH]
            value[to, :] = made[rows, 2 * DEPTH :]

    def turn(t, _):
        rows = lanes_at(t, QT)
        for source, target in ((query, query_t), (key, key_t), (value, value_t)):
            target[:, rows] = source[rows, :].astype(F32).T.astype(BF)
        return 0

    lax.fori_loop(0, SEQ // QT, turn, 0)

    def attend(i, _):
        lanes = lanes_at(i, QT)
        queries = query_t[:, lanes]

        def step(j, carry, masked):
            top, total, acc = carry
            rows = lanes_at(j, KT)
            scores = dot(key[rows, :], queries) * (DEPTH ** -0.5)
            if masked:
                key_place = j * KT + lax.broadcasted_iota(jnp.int32, (KT, QT), 0)
                query_place = i * QT + lax.broadcasted_iota(jnp.int32, (KT, QT), 1)
                scores = jnp.where(key_place <= query_place, scores, NEGATIVE)
            fresh = jnp.maximum(top, jnp.max(scores, axis=0, keepdims=True))
            raised = jnp.exp(scores - fresh)
            fade = jnp.exp(top - fresh)
            total = total * fade + jnp.sum(raised, axis=0, keepdims=True)
            acc = acc * fade + dot(value_t[:, rows], raised.astype(BF))
            return fresh, total, acc

        start = (
            jnp.full((1, QT), NEGATIVE, F32),
            jnp.zeros((1, QT), F32),
            jnp.zeros((DEPTH, QT), F32),
        )
        full = i * QT // KT
        if isinstance(i, int):
            carry = start
            for j in range(full):
                carry = step(j, carry, False)
        else:
            carry = lax.fori_loop(0, full, lambda j, carry: step(j, carry, False), start)
        for extra in range(max(1, QT // KT)):
            carry = step(full + extra, carry, True)
        top, total, acc = carry
        result = acc / total
        out_t[:, lanes] = result
        lse[pl.ds(i, 1), :] = top + jnp.log(total)
        return 0

    loop(SEQ // QT, attend)


def head_forward(order, where, blocks, weight, bias, gain, shift):
    layout = [(half, offsets) for half, offsets, _ in blocks]

    def kernel(order, where, *refs):
        block_refs, refs = refs[: len(layout)], refs[len(layout) :]
        (
            weight, bias, gain, shift,
            packed, normed, query, key, value, query_t, key_t, out_t, lse,
            value_t, out_rows,
        ) = refs
        head_forward_kernel(
            order, where,
            [(half, offsets, ref) for (half, offsets), ref in zip(layout, block_refs)],
            weight, bias, gain, shift,
            packed, normed, query, key, value, query_t, key_t, out_t, lse,
            value_t,
        )

        def turn_back(t, _):
            rows = lanes_at(t, QT)
            out_rows[rows, :] = out_t[:, rows].T
            return 0

        lax.fori_loop(0, SEQ // QT, turn_back, 0)

        def pack(c, _):
            place = order[c]
            packed[c] = jnp.concatenate(
                [out_rows[block_at(place), :], out_rows[block_at(2 * CTX - 1 - place), :]], axis=1
            ).astype(BF)
            return 0

        lax.fori_loop(0, CTX, pack, 0)

    shape = jax.ShapeDtypeStruct
    return vmem_call(
        kernel,
        [
            shape((CTX, HALF, 2 * DEPTH), BF),
            shape((SEQ, WIDTH), BF),
            shape((SEQ, DEPTH), BF),
            shape((SEQ, DEPTH), BF),
            shape((SEQ, DEPTH), BF),
            shape((DEPTH, SEQ), BF),
            shape((DEPTH, SEQ), BF),
            shape((DEPTH, SEQ), F32),
            shape((SEQ // QT, QT), F32),
        ],
        [pltpu.VMEM((DEPTH, SEQ), BF), pltpu.VMEM((SEQ, DEPTH), F32)],
        2 * 10**9,
        len(blocks) + 4,
        smem=2,
        transcendentals=3 * 10**6,
    )(order, where, *[block for _, _, block in blocks], weight, bias, gain, shift)


def head_backward(order, upstream, query, key, value, query_t, key_t, out_t, lse):
    def kernel(
        order, upstream, query, key, value, query_t, key_t, out_t, lse,
        packed, low_rows, bias_grad,
        grad_out, grad_out_t, delta, grad_q_t, grad_k, grad_v, rows_low,
    ):
        def unpack(c, _):
            place = order[c]
            grad_out[block_at(place), :] = upstream[c][:, :DEPTH]
            grad_out[block_at(2 * CTX - 1 - place), :] = upstream[c][:, DEPTH:]
            return 0

        lax.fori_loop(0, CTX, unpack, 0)

        def prepare(t, _):
            rows = lanes_at(t, QT)
            turned = grad_out[rows, :].astype(F32).T
            grad_out_t[:, rows] = turned.astype(BF)
            delta[pl.ds(t, 1), :] = jnp.sum(turned * out_t[:, rows], axis=0, keepdims=True)
            grad_q_t[:, rows] = jnp.zeros((DEPTH, QT), F32)
            grad_k[rows, :] = jnp.zeros((QT, DEPTH), F32)
            grad_v[rows, :] = jnp.zeros((QT, DEPTH), F32)
            return 0

        lax.fori_loop(0, SEQ // QT, prepare, 0)

        def one_query_tile(i, _):
            lanes = lanes_at(i, QT)

            def step(j, masked):
                rows = lanes_at(j, KT)
                scores = dot(key[rows, :], query_t[:, lanes]) * (DEPTH ** -0.5)
                probs = jnp.exp(scores - lse[pl.ds(i, 1), :])
                if masked:
                    key_place = j * KT + lax.broadcasted_iota(jnp.int32, (KT, QT), 0)
                    query_place = i * QT + lax.broadcasted_iota(jnp.int32, (KT, QT), 1)
                    probs = jnp.where(key_place <= query_place, probs, 0.0)
                slopes = dot(value[rows, :], grad_out_t[:, lanes])
                grad_scores = (
                    probs * (slopes - delta[pl.ds(i, 1), :]) * (DEPTH ** -0.5)
                ).astype(BF)
                grad_v[rows, :] += dot(probs.astype(BF), grad_out[lanes, :])
                grad_k[rows, :] += dot(grad_scores, query[lanes, :])
                grad_q_t[:, lanes] += dot(key_t[:, rows], grad_scores)

            full = i * QT // KT

            def body(j, _):
                step(j, False)
                return 0

            (loop(full, body) if isinstance(i, int) else lax.fori_loop(0, full, body, 0))
            for extra in range(max(1, QT // KT)):
                step(full + extra, True)
            return 0

        loop(SEQ // QT, one_query_tile)

        def finish(t, sums):
            rows = lanes_at(t, QT)
            low_q = grad_q_t[:, rows].T.astype(BF)
            low_k = grad_k[rows, :].astype(BF)
            low_v = grad_v[rows, :].astype(BF)
            joined = jnp.concatenate(
                [low_q.astype(F32), low_k.astype(F32), low_v.astype(F32)], axis=1
            )
            rows_low[rows, :] = joined
            low_rows[rows, :] = joined.astype(BF)
            return sums + jnp.sum(joined, axis=0, keepdims=True)

        sums = lax.fori_loop(0, SEQ // QT, finish, jnp.zeros((1, 3 * DEPTH), F32))
        bias_grad[...] = sums

        def pack(c, _):
            place = order[c]
            upper = rows_low[block_at(place), :]
            lower = rows_low[block_at(2 * CTX - 1 - place), :]
            pieces = []
            for part in range(3):
                lanes = slice(part * DEPTH, (part + 1) * DEPTH)
                pieces += [upper[:, lanes], lower[:, lanes]]
            packed[c] = jnp.concatenate(pieces, axis=1).astype(BF)
            return 0

        lax.fori_loop(0, CTX, pack, 0)

    shape = jax.ShapeDtypeStruct
    return vmem_call(
        kernel,
        [
            shape((CTX, HALF, 6 * DEPTH), BF),
            shape((SEQ, 3 * DEPTH), BF),
            shape((1, 3 * DEPTH), F32),
        ],
        [
            pltpu.VMEM((SEQ, DEPTH), BF),
            pltpu.VMEM((DEPTH, SEQ), BF),
            pltpu.VMEM((SEQ // QT, QT), F32),
            pltpu.VMEM((DEPTH, SEQ), F32),
            pltpu.VMEM((SEQ, DEPTH), F32),
            pltpu.VMEM((SEQ, DEPTH), F32),
            pltpu.VMEM((SEQ, 3 * DEPTH), F32),
        ],
        4 * 10**9,
        8,
        smem=1,
        transcendentals=3 * 10**6,
    )(order, upstream, query, key, value, query_t, key_t, out_t, lse)


def head_weight_grad(normed, rows):
    def kernel(normed, rows, out):
        out[...] = (
            dot_tn(normed[...], rows[...]).astype(BF).reshape(FSDP, WIDTH // FSDP, 3 * DEPTH)
        )

    return vmem_call(
        kernel,
        [jax.ShapeDtypeStruct((FSDP, WIDTH // FSDP, 3 * DEPTH), BF)],
        [],
        2 * SEQ * WIDTH * 3 * DEPTH,
        2,
    )(normed, rows)[0]


def unpack_heads(ref, lanes):
    upper, lower = [], []
    for head in range(HEADS):
        slot = ref[head][:, lanes : lanes + 2 * DEPTH].astype(F32)
        upper.append(slot[:, :DEPTH])
        lower.append(slot[:, DEPTH:])
    return jnp.concatenate(
        [jnp.concatenate(upper, axis=1), jnp.concatenate(lower, axis=1)], axis=0
    ).astype(BF)


def gelu_parts(values):
    slope = 0.7978845608028654
    cubic = 0.044715
    squared = values * values
    bend = jnp.tanh(slope * (values + cubic * squared * values))
    active = 0.5 * values * (1.0 + bend)
    grad = 0.5 * (1.0 + bend) + 0.5 * values * (1.0 - bend * bend) * slope * (
        1.0 + 3.0 * cubic * squared
    )
    return active, grad


def feed_forward(tokens, heads_out, cotangent, pack, out_bias, gain, shift, up_bias, down_bias):
    def kernel(
        tokens, heads_out, cotangent, pack, out_bias, gain, shift, up_bias, down_bias,
        mixed, pack_grad, grad_heads, grad_residual, vector_sums, up_sums,
    ):
        inputs = tokens[...].astype(F32)
        result_grad = cotangent[...]
        attended_low = unpack_heads(heads_out, 0)
        w_out = pack[:, OUT_AT:UP_AT, :].reshape(WIDTH, WIDTH)
        residual = inputs + dot(attended_low, w_out) + out_bias[...]
        hat, inverse = normalise(residual)
        low = (hat * gain[...] + shift[...]).astype(BF)
        low_t = low.T
        total = residual + down_bias[...]
        grad_normed = jnp.zeros((ROWS, WIDTH), F32)
        for j in range(HIDDEN // WIDTH):
            lanes = slice(j * WIDTH, (j + 1) * WIDTH)
            w_up = pack[:, UP_AT + 96 * j : UP_AT + 96 * (j + 1), :].reshape(WIDTH, WIDTH)
            w_down = pack[2 * j : 2 * j + 2, DOWN_AT:PACK_ROWS, :].reshape(WIDTH, WIDTH)
            hidden = dot(low, w_up) + up_bias[:, lanes]
            acted, slope = gelu_parts(hidden)
            acted = acted.astype(BF)
            pack_grad[2 * j : 2 * j + 2, DOWN_AT:PACK_ROWS, :] = (
                dot(acted.T, result_grad).astype(BF).reshape(2, 384, WIDTH)
            )
            total = total + dot(acted, w_down)
            pre = (dot_nt(result_grad, w_down) * slope).astype(BF)
            pack_grad[:, UP_AT + 96 * j : UP_AT + 96 * (j + 1), :] = (
                dot(low_t, pre).astype(BF).reshape(FSDP, 96, WIDTH)
            )
            up_sums[:, lanes] = jnp.sum(pre.astype(F32), axis=0, keepdims=True)
            grad_normed = grad_normed + dot_nt(pre, w_up)
        mixed[...] = total.astype(BF)
        back = result_grad.astype(F32) + norm_back(grad_normed, hat, inverse, gain[...])
        grad_residual[...] = back
        branch = back.astype(BF)
        pack_grad[:, OUT_AT:UP_AT, :] = (
            dot(attended_low.T, branch).astype(BF).reshape(FSDP, 96, WIDTH)
        )
        vector_sums[0:1, :] = jnp.sum(branch.astype(F32), axis=0, keepdims=True)
        vector_sums[1:2, :] = jnp.sum(grad_normed * hat, axis=0, keepdims=True)
        vector_sums[2:3, :] = jnp.sum(grad_normed, axis=0, keepdims=True)
        vector_sums[3:4, :] = jnp.sum(result_grad.astype(F32), axis=0, keepdims=True)
        grad_attended = dot_nt(branch, w_out)
        for head in range(HEADS):
            lanes = slice(head * DEPTH, (head + 1) * DEPTH)
            grad_heads[head] = jnp.concatenate(
                [grad_attended[:HALF, lanes], grad_attended[HALF:, lanes]], axis=1
            ).astype(BF)
        for head in range(HEADS, CTX):
            grad_heads[head] = jnp.zeros((HALF, 2 * DEPTH), BF)

    shape = jax.ShapeDtypeStruct
    return vmem_call(
        kernel,
        [
            shape((ROWS, WIDTH), BF),
            shape((FSDP, PACK_ROWS, WIDTH), BF),
            shape((CTX, HALF, 2 * DEPTH), BF),
            shape((ROWS, WIDTH), F32),
            shape((4, WIDTH), F32),
            shape((1, HIDDEN), F32),
        ],
        [],
        4 * 10**9,
        9,
    )(tokens, heads_out, cotangent, pack, out_bias, gain, shift, up_bias, down_bias)


def token_gradient(tokens, heads_grad, weight, gain, grad_residual):
    def kernel(tokens, heads_grad, weight, gain, grad_residual, tokens_grad, sums):
        projected = jnp.concatenate(
            [unpack_heads(heads_grad, 2 * DEPTH * part) for part in range(3)], axis=1
        )
        grad_normed = dot_nt(projected, weight[...])
        hat, inverse = normalise(tokens[...].astype(F32))
        tokens_grad[...] = grad_residual[...] + norm_back(grad_normed, hat, inverse, gain[...])
        sums[0:1, :] = jnp.sum(grad_normed * hat, axis=0, keepdims=True)
        sums[1:2, :] = jnp.sum(grad_normed, axis=0, keepdims=True)

    shape = jax.ShapeDtypeStruct
    return vmem_call(
        kernel,
        [shape((ROWS, WIDTH), F32), shape((2, WIDTH), F32)],
        [],
        2 * ROWS * WIDTH * 3 * WIDTH,
        5,
    )(tokens, heads_grad, weight, gain, grad_residual)


def small_slots(place, weight_grad, bias_sums, first_sums, vector_sums, up_sums):
    def kernel(place, weight_grad, bias_sums, first_sums, vector_sums, up_sums, slots):
        slots[:, :96, :] = weight_grad[...]
        tall = jnp.zeros((2, 3 * DEPTH), F32)
        bias_rows = []
        for part in (0, 2):
            piece = bias_sums[:, part * DEPTH : (part + 1) * DEPTH]
            for head in range(HEADS):
                bias_rows.append(jnp.where(place[0] == head, piece, 0.0))
        for owner in range(FSDP):
            lanes = slice(96 * owner, 96 * (owner + 1))
            values = dict(
                first_gain=first_sums[0:1, lanes],
                first_shift=first_sums[1:2, lanes],
                qv_bias=jnp.concatenate(bias_rows[3 * owner : 3 * owner + 3], axis=1),
                out_bias=vector_sums[0:1, lanes],
                second_gain=vector_sums[1:2, lanes],
                second_shift=vector_sums[2:3, lanes],
                up_bias=up_sums[:, 384 * owner : 384 * (owner + 1)],
                down_bias=vector_sums[3:4, lanes],
            )
            line = jnp.concatenate([values[name] for name, _ in VECTORS], axis=1)
            rows = [line[:, 192 * r : 192 * (r + 1)] for r in range(6)]
            slots[owner, 96:104, :] = jnp.concatenate(rows + [tall], axis=0).astype(BF)

    return vmem_call(
        kernel,
        [jax.ShapeDtypeStruct((FSDP, 104, 3 * DEPTH), BF)],
        [],
        10**6,
        5,
        smem=1,
    )(place, weight_grad, bias_sums, first_sums, vector_sums, up_sums)[0]


def last_pieces(parts, smalls):
    def kernel(parts, own, left, right, far, out):
        total = parts[0].astype(F32)
        for source in range(1, CTX):
            total = total + parts[source].astype(F32)
        small = (
            own[...].astype(F32) + left[...].astype(F32) + right[...].astype(F32)
            + far[...].astype(F32)
        )
        wide = jnp.concatenate([small[24 * k : 24 * (k + 1)] for k in range(4)], axis=1)
        line = jnp.concatenate(
            [
                jnp.concatenate([small[96 + r : 97 + r] for r in range(4)], axis=1),
                jnp.concatenate(
                    [small[100:101], small[101:102], jnp.zeros((1, 6 * DEPTH), F32)], axis=1
                ),
            ],
            axis=0,
        )
        joined = jnp.concatenate([total, wide, line], axis=0).astype(BF)
        for target in range(CTX):
            out[target] = joined

    return vmem_call(
        kernel,
        [jax.ShapeDtypeStruct((CTX, LAST_ROWS, WIDTH), BF)],
        [],
        10**6,
        5,
    )(parts, *smalls)[0]


def final_grads(pieces):
    def kernel(pieces, grad_qkv, grad_out, grad_up, grad_down, *vector_refs):
        shard = jnp.concatenate([pieces[n][:CTX_ROWS].astype(F32) for n in range(CTX)], axis=0)
        grad_out[...] = shard[OUT_AT:UP_AT]
        for j in range(HIDDEN // WIDTH):
            grad_up[:, j * WIDTH : (j + 1) * WIDTH] = shard[UP_AT + 96 * j : UP_AT + 96 * (j + 1)]
        grad_down[...] = shard[DOWN_AT:]
        lines = jnp.zeros((2, WIDTH), F32)
        for n in range(CTX):
            lines = lines + pieces[n][CTX_ROWS + 24 : CTX_ROWS + 26].astype(F32)
        line = jnp.concatenate([lines[0:1], lines[1:2]], axis=1)
        at = 0
        for ref, (_, width) in zip(vector_refs, VECTORS):
            ref[...] = line[:, at : at + width]
            at += width
        heads = []
        for head in range(HEADS):
            wide = pieces[head][CTX_ROWS : CTX_ROWS + 24].astype(F32)
            heads.append(
                jnp.concatenate([wide[:, 192 * k : 192 * (k + 1)] for k in range(4)], axis=0)
            )
        for part in range(3):
            grad_qkv[:, part * WIDTH : (part + 1) * WIDTH] = jnp.concatenate(
                [head[:, part * DEPTH : (part + 1) * DEPTH] for head in heads], axis=1
            )

    shape = jax.ShapeDtypeStruct
    return vmem_call(
        kernel,
        [
            shape((96, 3 * WIDTH), F32),
            shape((96, WIDTH), F32),
            shape((96, HIDDEN), F32),
            shape((384, WIDTH), F32),
        ]
        + [shape((1, width), F32) for _, width in VECTORS],
        [],
        10**6,
        1,
    )(pieces)


def swap(slots, axes):
    return lax.all_to_all(slots, axes, 0, 0, tiled=True)


def shift_by(value, z=0, x=0, y=0, core=0):
    pairs = []
    for at_z in range(SIDE):
        for at_x in range(SIDE):
            for at_y in range(SIDE):
                for at_core in range(2):
                    source = (at_z * SIDE + at_x) * FSDP + at_y * 2 + at_core
                    to_ctx = (at_z + z) % SIDE * SIDE + (at_x + x) % SIDE
                    to_fsdp = (at_y + y) % SIDE * 2 + (at_core + core) % 2
                    pairs.append((source, to_ctx * FSDP + to_fsdp))
    return lax.ppermute(value, ("ctx", "fsdp"), pairs)


def gather_rows(hat):
    blocks = []
    steps = (0, SIDE - 1, 1, 2)
    for half, first, second in ((0, "x", "z"), (1, "z", "x")):
        mine = hat[half * HALF : (half + 1) * HALF]
        near = jnp.stack([mine] + [shift_by(mine, **{first: by}) for by in (1, -1, 2)])
        ahead, behind = shift_by(near, **{second: 1}), shift_by(near, **{second: -1})
        far_one = shift_by(ahead[:2], **{second: 1})
        far_two = shift_by(behind[2:], **{second: -1})

        def offsets(across, along):
            return [(across, by) if second == "z" else (by, across) for by in along]

        blocks += [
            (half, offsets(0, steps), near),
            (half, offsets(SIDE - 1, steps), ahead),
            (half, offsets(1, steps), behind),
            (half, offsets(2, steps[:2]), far_one),
            (half, offsets(2, steps[2:]), far_two),
        ]
    return blocks


def gather_small(piece):
    at = lax.axis_index("fsdp")
    at_y, at_core = at // 2, at % 2
    ring = jnp.stack(
        [piece, shift_by(piece, y=-1), shift_by(piece, y=2), shift_by(piece, y=1)]
    )
    other = shift_by(ring, core=1)
    first = jnp.where(at_core == 0, ring, other)
    second = jnp.where(at_core == 0, other, ring)
    both = jnp.stack([first, second], axis=1)
    turned = lax.dynamic_slice_in_dim(
        jnp.concatenate([both, both], axis=0), (SIDE - at_y) % SIDE, SIDE, 0
    )
    return turned.reshape((FSDP,) + piece.shape)


def scatter_small(slots):
    at = lax.axis_index("fsdp")
    at_y, at_core = at // 2, at % 2
    pairs = slots.reshape((SIDE, 2) + slots.shape[1:])
    mine = jnp.where(at_core == 0, pairs[:, 0], pairs[:, 1])
    theirs = jnp.where(at_core == 0, pairs[:, 1], pairs[:, 0])
    both = (mine.astype(F32) + shift_by(theirs, core=1).astype(F32)).astype(BF)

    def slot(by):
        return lax.dynamic_index_in_dim(both, (at_y + by) % SIDE, 0, keepdims=False)

    return [slot(0)] + [shift_by(slot(by), y=by) for by in (1, -1, 2)]


def local(
    tokens, cotangent, pair_order, first_gain, first_shift, qkv_weight, qv_bias, out_weight,
    out_bias, second_gain, second_shift, up_weight, up_bias, down_weight, down_bias,
):
    my_tokens, my_cotangent = tokens[0], cotangent[0]
    place = lax.axis_index("ctx")
    where = place.reshape(1).astype(jnp.int32)
    head = place % HEADS
    shards = dict(
        first_gain=first_gain, first_shift=first_shift, qv_bias=qv_bias, out_bias=out_bias,
        second_gain=second_gain, second_shift=second_shift, up_bias=up_bias, down_bias=down_bias,
    )

    with jax.named_scope("gather_tokens"):
        blocks = gather_rows(normalised_rows(my_tokens))
    with jax.named_scope("gather_weights"):
        pack = jnp.concatenate(
            [out_weight]
            + [up_weight[:, j * WIDTH : (j + 1) * WIDTH] for j in range(HIDDEN // WIDTH)]
            + [down_weight],
            axis=0,
        )
        pack = lax.all_gather(pack, "fsdp", axis=0, tiled=False)
        w_qkv = lax.all_gather(qkv_weight, "fsdp", axis=0, tiled=True)
    with jax.named_scope("gather_small"):
        head_columns = jnp.concatenate(
            [
                lax.dynamic_slice_in_dim(qkv_weight, part * WIDTH + head * DEPTH, DEPTH, 1)
                for part in range(3)
            ],
            axis=1,
        )
        vectors = jnp.concatenate([shards[name] for name, _ in VECTORS]).reshape(6, 3 * DEPTH)
        small = gather_small(
            jnp.concatenate([head_columns, vectors, jnp.zeros((10, 3 * DEPTH), BF)], axis=0)
        )
        w_head = small[:, :96].reshape(WIDTH, 3 * DEPTH)
        vectors = small[:, 96:102].reshape(FSDP, VECTOR_WIDTH).astype(F32)
        whole, at = {}, 0
        for name, width in VECTORS:
            whole[name] = vectors[:, at : at + width].reshape(1, FSDP * width)
            at += width
        head_bias = jnp.concatenate(
            [
                lax.dynamic_slice_in_dim(whole["qv_bias"], head * DEPTH, DEPTH, 1),
                jnp.zeros((1, DEPTH), F32),
                lax.dynamic_slice_in_dim(whole["qv_bias"], WIDTH + head * DEPTH, DEPTH, 1),
            ],
            axis=1,
        )

    with jax.named_scope("attention"):
        packed, normed, query, key, value, query_t, key_t, out_t, lse = head_forward(
            pair_order, where, blocks, w_head, head_bias, whole["first_gain"],
            whole["first_shift"],
        )
        heads_out = swap(packed, "ctx")

    with jax.named_scope("feed_forward"):
        mixed, pack_grad, grad_heads, grad_residual, vector_sums, up_sums = feed_forward(
            my_tokens, heads_out, my_cotangent, pack, whole["out_bias"], whole["second_gain"],
            whole["second_shift"], whole["up_bias"], whole["down_bias"],
        )
        heads_up = swap(grad_heads, "ctx")
        shard_grad = lax.psum_scatter(pack_grad, "fsdp", scatter_dimension=0, tiled=False)

    with jax.named_scope("attention_back"):
        packed_grad, low_rows, bias_sums = head_backward(
            pair_order, heads_up, query, key, value, query_t, key_t, out_t, lse
        )
        heads_grad = swap(packed_grad, "ctx")
        weight_grad = head_weight_grad(normed, low_rows)

    with jax.named_scope("token_gradient"):
        tokens_grad, first_sums = token_gradient(
            my_tokens, heads_grad, w_qkv, whole["first_gain"], grad_residual
        )
        smalls = scatter_small(
            small_slots(where, weight_grad, bias_sums, first_sums, vector_sums, up_sums)
        )

    with jax.named_scope("sum_over_ctx"):
        parts = swap(shard_grad.reshape(CTX, CTX_ROWS, WIDTH), "ctx")
        grad_qkv, grad_out, grad_up, grad_down, *vector_grads = final_grads(
            swap(last_pieces(parts, smalls), "ctx")
        )
        grads = {
            name: grad.reshape(width) for grad, (name, width) in zip(vector_grads, VECTORS)
        }

    return (
        mixed[None], tokens_grad[None], grads["first_gain"], grads["first_shift"], grad_qkv,
        grads["qv_bias"], grad_out, grads["out_bias"], grads["second_gain"],
        grads["second_shift"], grad_up, grads["up_bias"], grad_down, grads["down_bias"],
    )


def solution(mesh):
    split, vector = P("fsdp", "ctx", None), P("fsdp")
    matrix = P("fsdp", None)
    in_specs = (
        split, split, P(), vector, vector, matrix, vector, matrix, vector, vector, vector,
        matrix, vector, matrix, vector,
    )
    out_specs = (
        split, split, vector, vector, matrix, vector, matrix, vector, vector, vector, matrix,
        vector, matrix, vector,
    )
    return jax.shard_map(local, mesh=mesh, in_specs=in_specs, out_specs=out_specs, check_vma=False)
```

```python
import jax
import jax.numpy as jnp
from jax import lax
from jax.experimental import pallas as pl
from jax.experimental.pallas import tpu as pltpu
from jax.sharding import PartitionSpec as P

HEADS = 12
DEPTH = 64
WIDTH = 768
HIDDEN = 3072
ROWS = 128
HALF = 64
CTX = 16
FSDP = 8
SIDE = 4
SEQ = CTX * ROWS
QT = 512
KT = 512
EPSILON = 1e-05
SCALE_LOG2 = DEPTH ** -0.5 * 1.4426950408889634
NEGATIVE = -1e30
VMEM_LIMIT = 56 * 1024 * 1024

BF = jnp.bfloat16
F32 = jnp.float32

VECTORS = (
    ("first_gain", 96),
    ("first_shift", 96),
    ("qv_bias", 192),
    ("out_bias", 96),
    ("second_gain", 96),
    ("second_shift", 96),
    ("up_bias", 384),
    ("down_bias", 96),
)
VECTOR_WIDTH = sum(width for _, width in VECTORS)

OUT_AT, UP_AT, DOWN_AT, PACK_ROWS = 0, 96, 480, 864
SHARE = PACK_ROWS // CTX
EARLY_ROWS = 32


def dot(left, right):
    return jnp.dot(left, right, preferred_element_type=F32)


def dot_nt(left, right):
    return lax.dot_general(left, right, (((1,), (1,)), ((), ())), preferred_element_type=F32)


def dot_tn(left, right):
    return lax.dot_general(left, right, (((0,), (0,)), ((), ())), preferred_element_type=F32)


def normalise(values):
    center = values - jnp.mean(values, axis=-1, keepdims=True)
    spread = jnp.mean(center * center, axis=-1, keepdims=True)
    inverse = lax.rsqrt(spread + EPSILON)
    return center * inverse, inverse


def norm_back(upstream, hat, inverse, gain):
    scaled = upstream * gain
    mean_one = jnp.mean(scaled, axis=-1, keepdims=True)
    mean_two = jnp.mean(scaled * hat, axis=-1, keepdims=True)
    return (scaled - mean_one - hat * mean_two) * inverse


UNROLL = True


def loop(count, body):
    if UNROLL:
        for step in range(count):
            body(step, 0)
    else:
        lax.fori_loop(0, count, body, 0)


def block_at(index):
    return pl.ds(pl.multiple_of(index * HALF, HALF), HALF)


def lanes_at(index, size):
    if isinstance(index, int):
        return pl.ds(index * size, size)
    return pl.ds(pl.multiple_of(index * size, size), size)


def vmem_call(kernel, out_shape, scratch, flops, in_vmem, smem=0, transcendentals=0):
    specs = [pl.BlockSpec(memory_space=pltpu.VMEM)] * in_vmem
    specs = [pl.BlockSpec(memory_space=pltpu.SMEM)] * smem + specs
    return pl.pallas_call(
        kernel,
        out_shape=out_shape,
        in_specs=specs,
        out_specs=[pl.BlockSpec(memory_space=pltpu.VMEM)] * len(out_shape),
        scratch_shapes=scratch,
        compiler_params=pltpu.CompilerParams(vmem_limit_bytes=VMEM_LIMIT),
        cost_estimate=pl.CostEstimate(
            flops=flops, bytes_accessed=8 * 2**20, transcendentals=transcendentals
        ),
    )


def packed_weights(out_weight, up_weight, down_weight):
    def kernel(out_weight, up_weight, down_weight, pack):
        pack[OUT_AT:UP_AT, :] = out_weight[...]
        for j in range(HIDDEN // WIDTH):
            pack[UP_AT + 96 * j : UP_AT + 96 * (j + 1), :] = up_weight[
                :, j * WIDTH : (j + 1) * WIDTH
            ]
        pack[DOWN_AT:PACK_ROWS, :] = down_weight[...]

    return vmem_call(
        kernel, [jax.ShapeDtypeStruct((PACK_ROWS, WIDTH), BF)], [], 10**6, 3
    )(out_weight, up_weight, down_weight)[0]


def normalised_rows(tokens):
    def kernel(tokens, hat):
        hat[...] = normalise(tokens[...].astype(F32))[0].astype(BF)

    return vmem_call(
        kernel, [jax.ShapeDtypeStruct((ROWS, WIDTH), BF)], [], 10**6, 1
    )(tokens)[0]


def head_forward_kernel(
    order, where, blocks, weight, bias, gain, shift,
    packed, hats, query, key, value, query_t, key_t, out_t, lse,
    value_t,
):
    at_z, at_x = where[0] // SIDE, lax.rem(where[0], SIDE)

    for half, offsets, block in blocks:
        count = len(offsets)
        hat_low = block[...].reshape(count * HALF, WIDTH)
        low = (hat_low.astype(F32) * gain[...] + shift[...]).astype(BF)
        made = (dot(low, weight[...]) + bias[...]).astype(BF)
        for n, (dz, dx) in enumerate(offsets):
            place = order[lax.rem(at_z + dz, SIDE) * SIDE + lax.rem(at_x + dx, SIDE)]
            to = block_at(place if half == 0 else 2 * CTX - 1 - place)
            rows = slice(n * HALF, (n + 1) * HALF)
            hats[to, :] = hat_low[rows]
            query[to, :] = made[rows, 0:DEPTH]
            key[to, :] = made[rows, DEPTH : 2 * DEPTH]
            value[to, :] = made[rows, 2 * DEPTH :]

    def turn(t, _):
        rows = lanes_at(t, QT)
        for source, target in ((query, query_t), (key, key_t), (value, value_t)):
            target[:, rows] = source[rows, :].astype(F32).T.astype(BF)
        return 0

    lax.fori_loop(0, SEQ // QT, turn, 0)

    def attend(i, _):
        lanes = lanes_at(i, QT)
        queries = query_t[:, lanes]

        def step(j, carry, masked):
            top, total, acc = carry
            rows = lanes_at(j, KT)
            scores = dot(key[rows, :], queries) * SCALE_LOG2
            if masked:
                key_place = j * KT + lax.broadcasted_iota(jnp.int32, (KT, QT), 0)
                query_place = i * QT + lax.broadcasted_iota(jnp.int32, (KT, QT), 1)
                scores = jnp.where(key_place <= query_place, scores, NEGATIVE)
            fresh = jnp.maximum(top, jnp.max(scores, axis=0, keepdims=True))
            raised = jnp.exp2(scores - fresh)
            fade = jnp.exp2(top - fresh)
            total = total * fade + jnp.sum(raised, axis=0, keepdims=True)
            acc = acc * fade + dot(value_t[:, rows], raised.astype(BF))
            return fresh, total, acc

        start = (
            jnp.full((1, QT), NEGATIVE, F32),
            jnp.zeros((1, QT), F32),
            jnp.zeros((DEPTH, QT), F32),
        )
        full = i * QT // KT
        if isinstance(i, int):
            carry = start
            for j in range(full):
                carry = step(j, carry, False)
        else:
            carry = lax.fori_loop(0, full, lambda j, carry: step(j, carry, False), start)
        for extra in range(max(1, QT // KT)):
            carry = step(full + extra, carry, True)
        top, total, acc = carry
        result = acc / total
        out_t[:, lanes] = result
        lse[pl.ds(i, 1), :] = top + jnp.log2(total)
        return 0

    loop(SEQ // QT, attend)


def head_forward(order, where, blocks, weight, bias, gain, shift):
    layout = [(half, offsets) for half, offsets, _ in blocks]

    def kernel(order, where, *refs):
        block_refs, refs = refs[: len(layout)], refs[len(layout) :]
        (
            weight, bias, gain, shift,
            packed, hats, query, key, value, query_t, key_t, out_t, lse,
            value_t, out_rows,
        ) = refs
        head_forward_kernel(
            order, where,
            [(half, offsets, ref) for (half, offsets), ref in zip(layout, block_refs)],
            weight, bias, gain, shift,
            packed, hats, query, key, value, query_t, key_t, out_t, lse,
            value_t,
        )

        def turn_back(t, _):
            rows = lanes_at(t, QT)
            out_rows[rows, :] = out_t[:, rows].T
            return 0

        lax.fori_loop(0, SEQ // QT, turn_back, 0)

        def pack(c, _):
            place = order[c]
            packed[c] = jnp.concatenate(
                [out_rows[block_at(place), :], out_rows[block_at(2 * CTX - 1 - place), :]], axis=1
            ).astype(BF)
            return 0

        lax.fori_loop(0, CTX, pack, 0)

    shape = jax.ShapeDtypeStruct
    return vmem_call(
        kernel,
        [
            shape((CTX, HALF, 2 * DEPTH), BF),
            shape((SEQ, WIDTH), BF),
            shape((SEQ, DEPTH), BF),
            shape((SEQ, DEPTH), BF),
            shape((SEQ, DEPTH), BF),
            shape((DEPTH, SEQ), BF),
            shape((DEPTH, SEQ), BF),
            shape((DEPTH, SEQ), F32),
            shape((SEQ // QT, QT), F32),
        ],
        [pltpu.VMEM((DEPTH, SEQ), BF), pltpu.VMEM((SEQ, DEPTH), F32)],
        2 * 10**9,
        len(blocks) + 4,
        smem=2,
        transcendentals=3 * 10**6,
    )(order, where, *[block for _, _, block in blocks], weight, bias, gain, shift)


def head_backward(order, upstream, query, key, value, query_t, key_t, out_t, lse):
    def kernel(
        order, upstream, query, key, value, query_t, key_t, out_t, lse,
        packed, low_rows, bias_grad,
        grad_out, grad_out_t, delta, grad_q_t, grad_k, grad_v, rows_low,
    ):
        def unpack(c, _):
            place = order[c]
            grad_out[block_at(place), :] = upstream[c][:, :DEPTH]
            grad_out[block_at(2 * CTX - 1 - place), :] = upstream[c][:, DEPTH:]
            return 0

        lax.fori_loop(0, CTX, unpack, 0)

        def prepare(t, _):
            rows = lanes_at(t, QT)
            turned = grad_out[rows, :].astype(F32).T
            grad_out_t[:, rows] = turned.astype(BF)
            delta[pl.ds(t, 1), :] = jnp.sum(turned * out_t[:, rows], axis=0, keepdims=True)
            grad_q_t[:, rows] = jnp.zeros((DEPTH, QT), F32)
            grad_k[rows, :] = jnp.zeros((QT, DEPTH), F32)
            grad_v[rows, :] = jnp.zeros((QT, DEPTH), F32)
            return 0

        lax.fori_loop(0, SEQ // QT, prepare, 0)

        def one_query_tile(i, _):
            lanes = lanes_at(i, QT)

            def step(j, masked):
                rows = lanes_at(j, KT)
                scores = dot(key[rows, :], query_t[:, lanes]) * SCALE_LOG2
                probs = jnp.exp2(scores - lse[pl.ds(i, 1), :])
                if masked:
                    key_place = j * KT + lax.broadcasted_iota(jnp.int32, (KT, QT), 0)
                    query_place = i * QT + lax.broadcasted_iota(jnp.int32, (KT, QT), 1)
                    probs = jnp.where(key_place <= query_place, probs, 0.0)
                slopes = dot(value[rows, :], grad_out_t[:, lanes])
                grad_scores = (probs * (slopes - delta[pl.ds(i, 1), :])).astype(BF)
                grad_v[rows, :] += dot(probs.astype(BF), grad_out[lanes, :])
                grad_k[rows, :] += dot(grad_scores, query[lanes, :])
                grad_q_t[:, lanes] += dot(key_t[:, rows], grad_scores)

            full = i * QT // KT

            def body(j, _):
                step(j, False)
                return 0

            (loop(full, body) if isinstance(i, int) else lax.fori_loop(0, full, body, 0))
            for extra in range(max(1, QT // KT)):
                step(full + extra, True)
            return 0

        loop(SEQ // QT, one_query_tile)

        def finish(t, sums):
            rows = lanes_at(t, QT)
            low_q = (grad_q_t[:, rows].T * (DEPTH ** -0.5)).astype(BF)
            low_k = (grad_k[rows, :] * (DEPTH ** -0.5)).astype(BF)
            low_v = grad_v[rows, :].astype(BF)
            joined = jnp.concatenate(
                [low_q.astype(F32), low_k.astype(F32), low_v.astype(F32)], axis=1
            )
            rows_low[rows, :] = joined
            low_rows[rows, :] = joined.astype(BF)
            return sums + jnp.sum(joined, axis=0, keepdims=True)

        sums = lax.fori_loop(0, SEQ // QT, finish, jnp.zeros((1, 3 * DEPTH), F32))
        bias_grad[...] = sums

        def pack(c, _):
            place = order[c]
            upper = rows_low[block_at(place), :]
            lower = rows_low[block_at(2 * CTX - 1 - place), :]
            pieces = []
            for part in range(3):
                lanes = slice(part * DEPTH, (part + 1) * DEPTH)
                pieces += [upper[:, lanes], lower[:, lanes]]
            packed[c] = jnp.concatenate(pieces, axis=1).astype(BF)
            return 0

        lax.fori_loop(0, CTX, pack, 0)

    shape = jax.ShapeDtypeStruct
    return vmem_call(
        kernel,
        [
            shape((CTX, HALF, 6 * DEPTH), BF),
            shape((SEQ, 3 * DEPTH), BF),
            shape((1, 3 * DEPTH), F32),
        ],
        [
            pltpu.VMEM((SEQ, DEPTH), BF),
            pltpu.VMEM((DEPTH, SEQ), BF),
            pltpu.VMEM((SEQ // QT, QT), F32),
            pltpu.VMEM((DEPTH, SEQ), F32),
            pltpu.VMEM((SEQ, DEPTH), F32),
            pltpu.VMEM((SEQ, DEPTH), F32),
            pltpu.VMEM((SEQ, 3 * DEPTH), F32),
        ],
        4 * 10**9,
        8,
        smem=1,
        transcendentals=3 * 10**6,
    )(order, upstream, query, key, value, query_t, key_t, out_t, lse)


def unpack_heads(ref, lanes):
    upper, lower = [], []
    for head in range(HEADS):
        slot = ref[head][:, lanes : lanes + 2 * DEPTH].astype(F32)
        upper.append(slot[:, :DEPTH])
        lower.append(slot[:, DEPTH:])
    return jnp.concatenate(
        [jnp.concatenate(upper, axis=1), jnp.concatenate(lower, axis=1)], axis=0
    ).astype(BF)


def gelu_parts(values):
    slope = 0.7978845608028654
    cubic = 0.044715
    squared = values * values
    bend = jnp.tanh(slope * (values + cubic * squared * values))
    active = 0.5 * values * (1.0 + bend)
    grad = 0.5 * (1.0 + bend) + 0.5 * values * (1.0 - bend * bend) * slope * (
        1.0 + 3.0 * cubic * squared
    )
    return active, grad


def pack_piece(source, held, sems, index):
    if index == 0:
        rows = (slice(0, FSDP), pl.ds(OUT_AT, 96))
    elif index <= 4:
        rows = (slice(0, FSDP), pl.ds(UP_AT + 96 * (index - 1), 96))
    else:
        rows = (pl.ds(2 * (index - 5), 2), pl.ds(DOWN_AT, 384))
    return pltpu.make_async_copy(source.at[rows], held.at[rows], sems.at[index])


def feed_forward(pack, tokens, heads_out, cotangent, out_bias, gain, shift, up_bias, down_bias):
    def kernel(
        source, tokens, heads_out, cotangent, out_bias, gain, shift, up_bias, down_bias,
        mixed, mix_grad, grad_heads, grad_residual, vector_sums, up_sums,
        pack, sems,
    ):
        order = [0] + [index for j in range(4) for index in (1 + j, 5 + j)]
        copies = {index: pack_piece(source, pack, sems, index) for index in order}
        for index in order:
            copies[index].start()
        inputs = tokens[...].astype(F32)
        result_grad = cotangent[...]
        attended_low = unpack_heads(heads_out, 0)
        copies[0].wait()
        w_out = pack[:, OUT_AT:UP_AT, :].reshape(WIDTH, WIDTH)
        residual = inputs + dot(attended_low, w_out) + out_bias[...]
        hat, inverse = normalise(residual)
        low = (hat * gain[...] + shift[...]).astype(BF)
        low_t = low.T
        total = residual + down_bias[...]
        grad_normed = jnp.zeros((ROWS, WIDTH), F32)
        for j in range(HIDDEN // WIDTH):
            lanes = slice(j * WIDTH, (j + 1) * WIDTH)
            copies[1 + j].wait()
            w_up = pack[:, UP_AT + 96 * j : UP_AT + 96 * (j + 1), :].reshape(WIDTH, WIDTH)
            hidden = dot(low, w_up) + up_bias[:, lanes]
            copies[5 + j].wait()
            w_down = pack[2 * j : 2 * j + 2, DOWN_AT:PACK_ROWS, :].reshape(WIDTH, WIDTH)
            upstream = dot_nt(result_grad, w_down)
            acted, slope = gelu_parts(hidden)
            acted = acted.astype(BF)
            mix_grad[2 * j : 2 * j + 2, DOWN_AT:, :] = (
                dot(acted.T, result_grad).astype(BF).reshape(2, 384, WIDTH)
            )
            total = total + dot(acted, w_down)
            pre = (upstream * slope).astype(BF)
            mix_grad[:, UP_AT + 96 * j : UP_AT + 96 * (j + 1), :] = (
                dot(low_t, pre).astype(BF).reshape(FSDP, 96, WIDTH)
            )
            up_sums[:, lanes] = jnp.sum(pre.astype(F32), axis=0, keepdims=True)
            grad_normed = grad_normed + dot_nt(pre, w_up)
        mixed[...] = total.astype(BF)
        back = result_grad.astype(F32) + norm_back(grad_normed, hat, inverse, gain[...])
        grad_residual[...] = back
        branch = back.astype(BF)
        grad_attended = dot_nt(branch, w_out)
        for head in range(HEADS):
            lanes = slice(head * DEPTH, (head + 1) * DEPTH)
            grad_heads[head] = jnp.concatenate(
                [grad_attended[:HALF, lanes], grad_attended[HALF:, lanes]], axis=1
            ).astype(BF)
        for head in range(HEADS, CTX):
            grad_heads[head] = jnp.zeros((HALF, 2 * DEPTH), BF)
        mix_grad[:, OUT_AT:UP_AT, :] = (
            dot(attended_low.T, branch).astype(BF).reshape(FSDP, 96, WIDTH)
        )
        vector_sums[0:1, :] = jnp.sum(branch.astype(F32), axis=0, keepdims=True)
        vector_sums[1:2, :] = jnp.sum(grad_normed * hat, axis=0, keepdims=True)
        vector_sums[2:3, :] = jnp.sum(grad_normed, axis=0, keepdims=True)
        vector_sums[3:4, :] = jnp.sum(result_grad.astype(F32), axis=0, keepdims=True)

    shape = jax.ShapeDtypeStruct
    outs = [
        shape((ROWS, WIDTH), BF),
        shape((FSDP, PACK_ROWS, WIDTH), BF),
        shape((CTX, HALF, 2 * DEPTH), BF),
        shape((ROWS, WIDTH), F32),
        shape((4, WIDTH), F32),
        shape((1, HIDDEN), F32),
    ]
    return pl.pallas_call(
        kernel,
        out_shape=outs,
        in_specs=[pl.BlockSpec(memory_space=pl.ANY)]
        + [pl.BlockSpec(memory_space=pltpu.VMEM)] * 8,
        out_specs=[pl.BlockSpec(memory_space=pltpu.VMEM)] * len(outs),
        scratch_shapes=[
            pltpu.VMEM((FSDP, PACK_ROWS, WIDTH), BF),
            pltpu.SemaphoreType.DMA((9,)),
        ],
        compiler_params=pltpu.CompilerParams(vmem_limit_bytes=VMEM_LIMIT),
        cost_estimate=pl.CostEstimate(
            flops=4 * 10**9, bytes_accessed=24 * 2**20, transcendentals=4 * 10**5
        ),
    )(pack, tokens, heads_out, cotangent, out_bias, gain, shift, up_bias, down_bias)


def token_gradient(weight, tokens, heads_grad, gain, grad_residual):
    def kernel(weight, tokens, heads_grad, gain, grad_residual, tokens_grad):
        hat, inverse = normalise(tokens[...].astype(F32))
        projected = jnp.concatenate(
            [unpack_heads(heads_grad, 2 * DEPTH * part) for part in range(3)], axis=1
        )
        grad_normed = dot_nt(projected, weight[...])
        tokens_grad[...] = grad_residual[...] + norm_back(grad_normed, hat, inverse, gain[...])

    return vmem_call(
        kernel,
        [jax.ShapeDtypeStruct((ROWS, WIDTH), F32)],
        [],
        2 * ROWS * WIDTH * 3 * WIDTH,
        5,
    )(weight, tokens, heads_grad, gain, grad_residual)[0]


def early_slots(where, hats, rows, weight, gain, shift, bias_sums, vector_sums, up_sums):
    def kernel(where, hats, rows, weight, gain, shift, bias_sums, vector_sums, up_sums, slots):
        place = where[0]

        made = dot_tn(rows[...], hats[...])
        column = jnp.broadcast_to(bias_sums[...], (8, 3 * DEPTH)).T[:, :1]
        weight_t = weight[...].astype(F32).T
        first_gain = jnp.sum(weight_t * made, axis=0, keepdims=True)
        first_shift = jnp.sum(weight_t * column, axis=0, keepdims=True)
        weight_grad = (made * gain[...] + column * shift[...]).T
        for owner in range(FSDP):
            slots[owner, :96, :] = weight_grad[96 * owner : 96 * (owner + 1)].astype(BF)

        tall = jnp.zeros((2, 3 * DEPTH), F32)
        bias_rows = []
        for part in (0, 2):
            piece = bias_sums[:, part * DEPTH : (part + 1) * DEPTH]
            for head in range(HEADS):
                bias_rows.append(jnp.where(place == head, piece, 0.0))
        for owner in range(FSDP):
            lanes = slice(96 * owner, 96 * (owner + 1))
            values = dict(
                first_gain=first_gain[:, lanes],
                first_shift=first_shift[:, lanes],
                qv_bias=jnp.concatenate(bias_rows[3 * owner : 3 * owner + 3], axis=1),
                out_bias=vector_sums[0:1, lanes],
                second_gain=vector_sums[1:2, lanes],
                second_shift=vector_sums[2:3, lanes],
                up_bias=up_sums[:, 384 * owner : 384 * (owner + 1)],
                down_bias=vector_sums[3:4, lanes],
            )
            line = jnp.concatenate([values[name] for name, _ in VECTORS], axis=1)
            pieces = [line[:, 192 * r : 192 * (r + 1)] for r in range(6)] + [tall]
            slots[owner, 96:, :] = jnp.concatenate(pieces, axis=0).astype(BF)

    return vmem_call(
        kernel,
        [jax.ShapeDtypeStruct((FSDP, 104, 3 * DEPTH), BF)],
        [],
        2 * SEQ * WIDTH * 3 * DEPTH,
        8,
        smem=1,
    )(where, hats, rows, weight, gain, shift, bias_sums, vector_sums, up_sums)[0]


def early_sums(parts):
    def kernel(own, left, right, far, out):
        total = (
            own[...].astype(F32) + left[...].astype(F32) + right[...].astype(F32)
            + far[...].astype(F32)
        )
        head = jnp.concatenate([total[24 * k : 24 * (k + 1)] for k in range(4)], axis=1)
        line = jnp.concatenate([total[96:104], jnp.zeros((8, 9 * DEPTH), F32)], axis=1)
        out[...] = jnp.concatenate([head, line], axis=0).astype(BF)

    return vmem_call(kernel, [jax.ShapeDtypeStruct((EARLY_ROWS, WIDTH), BF)], [], 10**6, 4)(*parts)[0]


def early_grads(pieces):
    def kernel(pieces, grad_qkv, *vector_refs):
        lines = jnp.zeros((8, 3 * DEPTH), F32)
        heads = []
        for n in range(CTX):
            piece = pieces[n].astype(F32)
            lines = lines + piece[24:, : 3 * DEPTH]
            if n < HEADS:
                heads.append(
                    jnp.concatenate(
                        [piece[:24, 192 * k : 192 * (k + 1)] for k in range(4)], axis=0
                    )
                )
        line = jnp.concatenate([lines[r : r + 1] for r in range(6)], axis=1)
        at = 0
        for ref, (_, width) in zip(vector_refs, VECTORS):
            ref[...] = line[:, at : at + width]
            at += width
        for part in range(3):
            grad_qkv[:, part * WIDTH : (part + 1) * WIDTH] = jnp.concatenate(
                [head[:, part * DEPTH : (part + 1) * DEPTH] for head in heads], axis=1
            )

    shape = jax.ShapeDtypeStruct
    return vmem_call(
        kernel,
        [shape((96, 3 * WIDTH), F32)] + [shape((1, width), F32) for _, width in VECTORS],
        [],
        10**6,
        1,
    )(pieces)


def last_pieces(parts):
    def kernel(parts, out):
        total = parts[0].astype(F32)
        for source in range(1, CTX):
            total = total + parts[source].astype(F32)
        total = total.astype(BF)
        for target in range(CTX):
            out[target] = total

    return vmem_call(
        kernel, [jax.ShapeDtypeStruct((CTX, SHARE, WIDTH), BF)], [], 10**6, 1
    )(parts)[0]


def last_grads(pieces):
    def kernel(pieces, grad_out, grad_up, grad_down):
        shard = jnp.concatenate([pieces[n].astype(F32) for n in range(CTX)], axis=0)
        grad_out[...] = shard[OUT_AT:UP_AT]
        for j in range(HIDDEN // WIDTH):
            grad_up[:, j * WIDTH : (j + 1) * WIDTH] = shard[UP_AT + 96 * j : UP_AT + 96 * (j + 1)]
        grad_down[...] = shard[DOWN_AT:]

    shape = jax.ShapeDtypeStruct
    return vmem_call(
        kernel,
        [shape((96, WIDTH), F32), shape((96, HIDDEN), F32), shape((384, WIDTH), F32)],
        [],
        10**6,
        1,
    )(pieces)


def swap(slots, axes):
    return lax.all_to_all(slots, axes, 0, 0, tiled=True)


def spread(piece, axes, count):
    return swap(jnp.broadcast_to(piece[None], (count,) + piece.shape), axes)


def shift_by(value, z=0, x=0, y=0, core=0):
    pairs = []
    for at_z in range(SIDE):
        for at_x in range(SIDE):
            for at_y in range(SIDE):
                for at_core in range(2):
                    source = (at_z * SIDE + at_x) * FSDP + at_y * 2 + at_core
                    to_ctx = (at_z + z) % SIDE * SIDE + (at_x + x) % SIDE
                    to_fsdp = (at_y + y) % SIDE * 2 + (at_core + core) % 2
                    pairs.append((source, to_ctx * FSDP + to_fsdp))
    return lax.ppermute(value, ("ctx", "fsdp"), pairs)


def gather_rows(values):
    blocks = []
    steps = (0, SIDE - 1, 1, 2)
    for half, first, second in ((0, "x", "z"), (1, "z", "x")):
        mine = values[half * HALF : (half + 1) * HALF]
        near = jnp.stack([mine] + [shift_by(mine, **{first: by}) for by in (1, -1, 2)])
        ahead, behind = shift_by(near, **{second: 1}), shift_by(near, **{second: -1})
        far_one = shift_by(ahead[:2], **{second: 1})
        far_two = shift_by(behind[2:], **{second: -1})

        def offsets(across, along):
            return [(across, by) if second == "z" else (by, across) for by in along]

        blocks += [
            (half, offsets(0, steps), near),
            (half, offsets(SIDE - 1, steps), ahead),
            (half, offsets(1, steps), behind),
            (half, offsets(2, steps[:2]), far_one),
            (half, offsets(2, steps[2:]), far_two),
        ]
    return blocks


def gather_small(piece):
    at = lax.axis_index("fsdp")
    at_y, at_core = at // 2, at % 2
    ring = jnp.stack(
        [piece, shift_by(piece, y=-1), shift_by(piece, y=2), shift_by(piece, y=1)]
    )
    other = shift_by(ring, core=1)
    first = jnp.where(at_core == 0, ring, other)
    second = jnp.where(at_core == 0, other, ring)
    both = jnp.stack([first, second], axis=1)
    turned = lax.dynamic_slice_in_dim(
        jnp.concatenate([both, both], axis=0), (SIDE - at_y) % SIDE, SIDE, 0
    )
    return turned.reshape((FSDP,) + piece.shape)


def scatter_small(slots):
    at = lax.axis_index("fsdp")
    at_y, at_core = at // 2, at % 2
    pairs = slots.reshape((SIDE, 2) + slots.shape[1:])
    mine = jnp.where(at_core == 0, pairs[:, 0], pairs[:, 1])
    theirs = jnp.where(at_core == 0, pairs[:, 1], pairs[:, 0])
    both = (mine.astype(F32) + shift_by(theirs, core=1).astype(F32)).astype(BF)

    def slot(by):
        return lax.dynamic_index_in_dim(both, (at_y + by) % SIDE, 0, keepdims=False)

    return [slot(0)] + [shift_by(slot(by), y=by) for by in (1, -1, 2)]


def local(
    tokens, cotangent, pair_order, first_gain, first_shift, qkv_weight, qv_bias, out_weight,
    out_bias, second_gain, second_shift, up_weight, up_bias, down_weight, down_bias,
):
    my_tokens, my_cotangent = tokens[0], cotangent[0]
    place = lax.axis_index("ctx")
    where = place.reshape(1).astype(jnp.int32)
    head = place % HEADS
    shards = dict(
        first_gain=first_gain, first_shift=first_shift, qv_bias=qv_bias, out_bias=out_bias,
        second_gain=second_gain, second_shift=second_shift, up_bias=up_bias, down_bias=down_bias,
    )

    with jax.named_scope("gather_tokens"):
        blocks = gather_rows(normalised_rows(my_tokens))
    with jax.named_scope("gather_weights"):
        pack = packed_weights(out_weight, up_weight, down_weight)
        pack = lax.all_gather(pack, "fsdp", axis=0, tiled=False)
    with jax.named_scope("gather_small"):
        head_columns = jnp.concatenate(
            [
                lax.dynamic_slice_in_dim(qkv_weight, part * WIDTH + head * DEPTH, DEPTH, 1)
                for part in range(3)
            ],
            axis=1,
        )
        vectors = jnp.concatenate([shards[name] for name, _ in VECTORS]).reshape(6, 3 * DEPTH)
        small = gather_small(
            jnp.concatenate([head_columns, vectors, jnp.zeros((10, 3 * DEPTH), BF)], axis=0)
        )
        w_head = small[:, :96].reshape(WIDTH, 3 * DEPTH)
        vectors = small[:, 96:102].reshape(FSDP, VECTOR_WIDTH).astype(F32)
        whole, at = {}, 0
        for name, width in VECTORS:
            whole[name] = vectors[:, at : at + width].reshape(1, FSDP * width)
            at += width
        head_bias = jnp.concatenate(
            [
                lax.dynamic_slice_in_dim(whole["qv_bias"], head * DEPTH, DEPTH, 1),
                jnp.zeros((1, DEPTH), F32),
                lax.dynamic_slice_in_dim(whole["qv_bias"], WIDTH + head * DEPTH, DEPTH, 1),
            ],
            axis=1,
        )

    with jax.named_scope("attention"):
        packed, hats, query, key, value, query_t, key_t, out_t, lse = head_forward(
            pair_order, where, blocks, w_head, head_bias, whole["first_gain"],
            whole["first_shift"],
        )
        heads_out = swap(packed, "ctx")

    with jax.named_scope("feed_forward"):
        mixed, mix_grad, grad_heads, grad_residual, vector_sums, up_sums = feed_forward(
            pack, my_tokens, heads_out, my_cotangent, whole["out_bias"], whole["second_gain"],
            whole["second_shift"], whole["up_bias"], whole["down_bias"],
        )
        mix_shard = lax.psum_scatter(mix_grad, "fsdp", scatter_dimension=0, tiled=False)
        heads_up = swap(grad_heads, "ctx")

    with jax.named_scope("attention_back"):
        packed_grad, low_rows, bias_sums = head_backward(
            pair_order, heads_up, query, key, value, query_t, key_t, out_t, lse
        )
        heads_grad = swap(packed_grad, "ctx")

    with jax.named_scope("early_grads"):
        early = early_sums(
            scatter_small(
                early_slots(
                    where, hats, low_rows, w_head, whole["first_gain"], whole["first_shift"],
                    bias_sums, vector_sums, up_sums,
                )
            )
        )
        early, heads_grad = lax.optimization_barrier((early, heads_grad))
        early = spread(early, "ctx", CTX)

    with jax.named_scope("sum_over_ctx"):
        mix_shard, early = lax.optimization_barrier((mix_shard, early))
        parts = swap(mix_shard.reshape(CTX, SHARE, WIDTH), "ctx")
        shares, early = lax.optimization_barrier((last_pieces(parts), early))
        grad_out, grad_up, grad_down = last_grads(swap(shares, "ctx"))
        grad_qkv, *vector_grads = early_grads(early)
        grads = {
            name: grad.reshape(width) for grad, (name, width) in zip(vector_grads, VECTORS)
        }

    with jax.named_scope("token_gradient"):
        late_weight, heads_grad = lax.optimization_barrier((qkv_weight, heads_grad))
        w_qkv = lax.all_gather(late_weight, "fsdp", axis=0, tiled=True)
        tokens_grad = token_gradient(
            w_qkv, my_tokens, heads_grad, whole["first_gain"], grad_residual
        )

    return (
        mixed[None], tokens_grad[None], grads["first_gain"], grads["first_shift"], grad_qkv,
        grads["qv_bias"], grad_out, grads["out_bias"], grads["second_gain"],
        grads["second_shift"], grad_up, grads["up_bias"], grad_down, grads["down_bias"],
    )


def solution(mesh):
    split, vector = P("fsdp", "ctx", None), P("fsdp")
    matrix = P("fsdp", None)
    in_specs = (
        split, split, P(), vector, vector, matrix, vector, matrix, vector, vector, vector,
        matrix, vector, matrix, vector,
    )
    out_specs = (
        split, split, vector, vector, matrix, vector, matrix, vector, vector, vector, matrix,
        vector, matrix, vector,
    )
    return jax.shard_map(local, mesh=mesh, in_specs=in_specs, out_specs=out_specs, check_vma=False)
```

```python
import jax
import jax.numpy as jnp
from jax import lax
from jax.experimental import pallas as pl
from jax.experimental.pallas import tpu as pltpu
from jax.sharding import PartitionSpec as P

HEADS = 12
DEPTH = 64
WIDTH = 768
HIDDEN = 3072
ROWS = 128
HALF = 64
CTX = 16
FSDP = 8
SIDE = 4
SEQ = CTX * ROWS
QT = 512
KT = 512
EPSILON = 1e-05
SCALE_LOG2 = DEPTH ** -0.5 * 1.4426950408889634
NEGATIVE = -1e30
VMEM_LIMIT = 56 * 1024 * 1024

BF = jnp.bfloat16
F32 = jnp.float32

VECTORS = (
    ("first_gain", 96),
    ("first_shift", 96),
    ("qv_bias", 192),
    ("out_bias", 96),
    ("second_gain", 96),
    ("second_shift", 96),
    ("up_bias", 384),
    ("down_bias", 96),
)
VECTOR_WIDTH = sum(width for _, width in VECTORS)

OUT_AT, UP_AT, DOWN_AT, PACK_ROWS = 0, 96, 480, 864
SHARE = PACK_ROWS // CTX
EARLY_ROWS = 32


def dot(left, right):
    return jnp.dot(left, right, preferred_element_type=F32)


def dot_nt(left, right):
    return lax.dot_general(left, right, (((1,), (1,)), ((), ())), preferred_element_type=F32)


def dot_tn(left, right):
    return lax.dot_general(left, right, (((0,), (0,)), ((), ())), preferred_element_type=F32)


def normalise(values):
    center = values - jnp.mean(values, axis=-1, keepdims=True)
    spread = jnp.mean(center * center, axis=-1, keepdims=True)
    inverse = lax.rsqrt(spread + EPSILON)
    return center * inverse, inverse


def norm_back(upstream, hat, inverse, gain):
    scaled = upstream * gain
    mean_one = jnp.mean(scaled, axis=-1, keepdims=True)
    mean_two = jnp.mean(scaled * hat, axis=-1, keepdims=True)
    return (scaled - mean_one - hat * mean_two) * inverse


UNROLL = True


def loop(count, body):
    if UNROLL:
        for step in range(count):
            body(step, 0)
    else:
        lax.fori_loop(0, count, body, 0)


def block_at(index):
    return pl.ds(pl.multiple_of(index * HALF, HALF), HALF)


def lanes_at(index, size):
    if isinstance(index, int):
        return pl.ds(index * size, size)
    return pl.ds(pl.multiple_of(index * size, size), size)


def vmem_call(kernel, out_shape, scratch, flops, in_vmem, smem=0, transcendentals=0):
    specs = [pl.BlockSpec(memory_space=pltpu.VMEM)] * in_vmem
    specs = [pl.BlockSpec(memory_space=pltpu.SMEM)] * smem + specs
    return pl.pallas_call(
        kernel,
        out_shape=out_shape,
        in_specs=specs,
        out_specs=[pl.BlockSpec(memory_space=pltpu.VMEM)] * len(out_shape),
        scratch_shapes=scratch,
        compiler_params=pltpu.CompilerParams(vmem_limit_bytes=VMEM_LIMIT),
        cost_estimate=pl.CostEstimate(
            flops=flops, bytes_accessed=8 * 2**20, transcendentals=transcendentals
        ),
    )


def packed_weights(out_weight, up_weight, down_weight):
    def kernel(out_weight, up_weight, down_weight, pack):
        pack[OUT_AT:UP_AT, :] = out_weight[...]
        for j in range(HIDDEN // WIDTH):
            pack[UP_AT + 96 * j : UP_AT + 96 * (j + 1), :] = up_weight[
                :, j * WIDTH : (j + 1) * WIDTH
            ]
        pack[DOWN_AT:PACK_ROWS, :] = down_weight[...]

    return vmem_call(
        kernel, [jax.ShapeDtypeStruct((PACK_ROWS, WIDTH), BF)], [], 10**6, 3
    )(out_weight, up_weight, down_weight)[0]


def normalised_rows(tokens):
    def kernel(tokens, hat):
        hat[...] = normalise(tokens[...].astype(F32))[0].astype(BF)

    return vmem_call(
        kernel, [jax.ShapeDtypeStruct((ROWS, WIDTH), BF)], [], 10**6, 1
    )(tokens)[0]


def head_forward_kernel(
    order, where, blocks, weight, bias, gain, shift,
    packed, hats, query, key, value, query_t, key_t, out_t, lse,
    value_t,
):
    at_z, at_x = where[0] // SIDE, lax.rem(where[0], SIDE)

    for half, offsets, block in blocks:
        count = len(offsets)
        hat_low = block[...].reshape(count * HALF, WIDTH)
        low = (hat_low.astype(F32) * gain[...] + shift[...]).astype(BF)
        made = (dot(low, weight[...]) + bias[...]).astype(BF)
        for n, (dz, dx) in enumerate(offsets):
            place = order[lax.rem(at_z + dz, SIDE) * SIDE + lax.rem(at_x + dx, SIDE)]
            to = block_at(place if half == 0 else 2 * CTX - 1 - place)
            rows = slice(n * HALF, (n + 1) * HALF)
            hats[to, :] = hat_low[rows]
            query[to, :] = made[rows, 0:DEPTH]
            key[to, :] = made[rows, DEPTH : 2 * DEPTH]
            value[to, :] = made[rows, 2 * DEPTH :]

    def turn(t, _):
        rows = lanes_at(t, QT)
        for source, target in ((query, query_t), (key, key_t), (value, value_t)):
            target[:, rows] = source[rows, :].astype(F32).T.astype(BF)
        return 0

    lax.fori_loop(0, SEQ // QT, turn, 0)

    def attend(i, _):
        lanes = lanes_at(i, QT)
        queries = query_t[:, lanes]

        def step(j, carry, masked):
            top, total, acc = carry
            rows = lanes_at(j, KT)
            scores = dot(key[rows, :], queries) * SCALE_LOG2
            if masked:
                key_place = j * KT + lax.broadcasted_iota(jnp.int32, (KT, QT), 0)
                query_place = i * QT + lax.broadcasted_iota(jnp.int32, (KT, QT), 1)
                scores = jnp.where(key_place <= query_place, scores, NEGATIVE)
            fresh = jnp.maximum(top, jnp.max(scores, axis=0, keepdims=True))
            raised = jnp.exp2(scores - fresh)
            fade = jnp.exp2(top - fresh)
            total = total * fade + jnp.sum(raised, axis=0, keepdims=True)
            acc = acc * fade + dot(value_t[:, rows], raised.astype(BF))
            return fresh, total, acc

        start = (
            jnp.full((1, QT), NEGATIVE, F32),
            jnp.zeros((1, QT), F32),
            jnp.zeros((DEPTH, QT), F32),
        )
        full = i * QT // KT
        if isinstance(i, int):
            carry = start
            for j in range(full):
                carry = step(j, carry, False)
        else:
            carry = lax.fori_loop(0, full, lambda j, carry: step(j, carry, False), start)
        for extra in range(max(1, QT // KT)):
            carry = step(full + extra, carry, True)
        top, total, acc = carry
        result = acc / total
        out_t[:, lanes] = result
        lse[pl.ds(i, 1), :] = top + jnp.log2(total)
        return 0

    loop(SEQ // QT, attend)


def head_forward(order, where, blocks, weight, bias, gain, shift):
    layout = [(half, offsets) for half, offsets, _ in blocks]

    def kernel(order, where, *refs):
        block_refs, refs = refs[: len(layout)], refs[len(layout) :]
        (
            weight, bias, gain, shift,
            packed, hats, query, key, value, query_t, key_t, out_t, lse,
            value_t, out_rows,
        ) = refs
        head_forward_kernel(
            order, where,
            [(half, offsets, ref) for (half, offsets), ref in zip(layout, block_refs)],
            weight, bias, gain, shift,
            packed, hats, query, key, value, query_t, key_t, out_t, lse,
            value_t,
        )

        def turn_back(t, _):
            rows = lanes_at(t, QT)
            out_rows[rows, :] = out_t[:, rows].T
            return 0

        lax.fori_loop(0, SEQ // QT, turn_back, 0)

        def pack(c, _):
            place = order[c]
            packed[c] = jnp.concatenate(
                [out_rows[block_at(place), :], out_rows[block_at(2 * CTX - 1 - place), :]], axis=1
            ).astype(BF)
            return 0

        lax.fori_loop(0, CTX, pack, 0)

    shape = jax.ShapeDtypeStruct
    return vmem_call(
        kernel,
        [
            shape((CTX, HALF, 2 * DEPTH), BF),
            shape((SEQ, WIDTH), BF),
            shape((SEQ, DEPTH), BF),
            shape((SEQ, DEPTH), BF),
            shape((SEQ, DEPTH), BF),
            shape((DEPTH, SEQ), BF),
            shape((DEPTH, SEQ), BF),
            shape((DEPTH, SEQ), F32),
            shape((SEQ // QT, QT), F32),
        ],
        [pltpu.VMEM((DEPTH, SEQ), BF), pltpu.VMEM((SEQ, DEPTH), F32)],
        2 * 10**9,
        len(blocks) + 4,
        smem=2,
        transcendentals=3 * 10**6,
    )(order, where, *[block for _, _, block in blocks], weight, bias, gain, shift)


def head_backward(order, upstream, query, key, value, query_t, key_t, out_t, lse):
    def kernel(
        order, upstream, query, key, value, query_t, key_t, out_t, lse,
        packed, low_rows, bias_grad,
        grad_out, grad_out_t, delta, grad_q_t, grad_k, grad_v, rows_low,
    ):
        def unpack(c, _):
            place = order[c]
            grad_out[block_at(place), :] = upstream[c][:, :DEPTH]
            grad_out[block_at(2 * CTX - 1 - place), :] = upstream[c][:, DEPTH:]
            return 0

        lax.fori_loop(0, CTX, unpack, 0)

        def prepare(t, _):
            rows = lanes_at(t, QT)
            turned = grad_out[rows, :].astype(F32).T
            grad_out_t[:, rows] = turned.astype(BF)
            delta[pl.ds(t, 1), :] = jnp.sum(turned * out_t[:, rows], axis=0, keepdims=True)
            grad_q_t[:, rows] = jnp.zeros((DEPTH, QT), F32)
            grad_k[rows, :] = jnp.zeros((QT, DEPTH), F32)
            grad_v[rows, :] = jnp.zeros((QT, DEPTH), F32)
            return 0

        lax.fori_loop(0, SEQ // QT, prepare, 0)

        def one_query_tile(i, _):
            lanes = lanes_at(i, QT)

            def step(j, masked):
                rows = lanes_at(j, KT)
                scores = dot(key[rows, :], query_t[:, lanes]) * SCALE_LOG2
                probs = jnp.exp2(scores - lse[pl.ds(i, 1), :])
                if masked:
                    key_place = j * KT + lax.broadcasted_iota(jnp.int32, (KT, QT), 0)
                    query_place = i * QT + lax.broadcasted_iota(jnp.int32, (KT, QT), 1)
                    probs = jnp.where(key_place <= query_place, probs, 0.0)
                slopes = dot(value[rows, :], grad_out_t[:, lanes])
                grad_scores = (probs * (slopes - delta[pl.ds(i, 1), :])).astype(BF)
                grad_v[rows, :] += dot(probs.astype(BF), grad_out[lanes, :])
                grad_k[rows, :] += dot(grad_scores, query[lanes, :])
                grad_q_t[:, lanes] += dot(key_t[:, rows], grad_scores)

            full = i * QT // KT

            def body(j, _):
                step(j, False)
                return 0

            (loop(full, body) if isinstance(i, int) else lax.fori_loop(0, full, body, 0))
            for extra in range(max(1, QT // KT)):
                step(full + extra, True)
            return 0

        loop(SEQ // QT, one_query_tile)

        def finish(t, sums):
            rows = lanes_at(t, QT)
            low_q = (grad_q_t[:, rows].T * (DEPTH ** -0.5)).astype(BF)
            low_k = (grad_k[rows, :] * (DEPTH ** -0.5)).astype(BF)
            low_v = grad_v[rows, :].astype(BF)
            joined = jnp.concatenate(
                [low_q.astype(F32), low_k.astype(F32), low_v.astype(F32)], axis=1
            )
            rows_low[rows, :] = joined
            low_rows[rows, :] = joined.astype(BF)
            return sums + jnp.sum(joined, axis=0, keepdims=True)

        sums = lax.fori_loop(0, SEQ // QT, finish, jnp.zeros((1, 3 * DEPTH), F32))
        bias_grad[...] = sums

        def pack(c, _):
            place = order[c]
            upper = rows_low[block_at(place), :]
            lower = rows_low[block_at(2 * CTX - 1 - place), :]
            pieces = []
            for part in range(3):
                lanes = slice(part * DEPTH, (part + 1) * DEPTH)
                pieces += [upper[:, lanes], lower[:, lanes]]
            packed[c] = jnp.concatenate(pieces, axis=1).astype(BF)
            return 0

        lax.fori_loop(0, CTX, pack, 0)

    shape = jax.ShapeDtypeStruct
    return vmem_call(
        kernel,
        [
            shape((CTX, HALF, 6 * DEPTH), BF),
            shape((SEQ, 3 * DEPTH), BF),
            shape((1, 3 * DEPTH), F32),
        ],
        [
            pltpu.VMEM((SEQ, DEPTH), BF),
            pltpu.VMEM((DEPTH, SEQ), BF),
            pltpu.VMEM((SEQ // QT, QT), F32),
            pltpu.VMEM((DEPTH, SEQ), F32),
            pltpu.VMEM((SEQ, DEPTH), F32),
            pltpu.VMEM((SEQ, DEPTH), F32),
            pltpu.VMEM((SEQ, 3 * DEPTH), F32),
        ],
        4 * 10**9,
        8,
        smem=1,
        transcendentals=3 * 10**6,
    )(order, upstream, query, key, value, query_t, key_t, out_t, lse)


def unpack_heads(ref, lanes):
    upper, lower = [], []
    for head in range(HEADS):
        slot = ref[head][:, lanes : lanes + 2 * DEPTH].astype(F32)
        upper.append(slot[:, :DEPTH])
        lower.append(slot[:, DEPTH:])
    return jnp.concatenate(
        [jnp.concatenate(upper, axis=1), jnp.concatenate(lower, axis=1)], axis=0
    ).astype(BF)


def gelu_parts(values):
    slope = 0.7978845608028654
    cubic = 0.044715
    squared = values * values
    bend = jnp.tanh(slope * (values + cubic * squared * values))
    active = 0.5 * values * (1.0 + bend)
    grad = 0.5 * (1.0 + bend) + 0.5 * values * (1.0 - bend * bend) * slope * (
        1.0 + 3.0 * cubic * squared
    )
    return active, grad


def pack_piece(source, held, sems, index):
    if index == 0:
        rows = (slice(0, FSDP), pl.ds(OUT_AT, 96))
    elif index <= 4:
        rows = (slice(0, FSDP), pl.ds(UP_AT + 96 * (index - 1), 96))
    else:
        rows = (pl.ds(2 * (index - 5), 2), pl.ds(DOWN_AT, 384))
    return pltpu.make_async_copy(source.at[rows], held.at[rows], sems.at[index])


def feed_forward(pack, tokens, heads_out, cotangent, out_bias, gain, shift, up_bias, down_bias):
    def kernel(
        source, tokens, heads_out, cotangent, out_bias, gain, shift, up_bias, down_bias,
        mixed, grads_out, grad_heads, grad_residual, vector_sums, up_sums,
        pack, sems, mix_grad, out_sems,
    ):
        order = [0] + [index for j in range(4) for index in (1 + j, 5 + j)]
        copies = {index: pack_piece(source, pack, sems, index) for index in order}
        for index in order:
            copies[index].start()

        def send(index):
            copy = pack_piece(mix_grad, grads_out, out_sems, index)
            copy.start()
            return copy

        sent = []
        inputs = tokens[...].astype(F32)
        result_grad = cotangent[...]
        attended_low = unpack_heads(heads_out, 0)
        copies[0].wait()
        w_out = pack[:, OUT_AT:UP_AT, :].reshape(WIDTH, WIDTH)
        residual = inputs + dot(attended_low, w_out) + out_bias[...]
        hat, inverse = normalise(residual)
        low = (hat * gain[...] + shift[...]).astype(BF)
        low_t = low.T
        total = residual + down_bias[...]
        grad_normed = jnp.zeros((ROWS, WIDTH), F32)
        for j in range(HIDDEN // WIDTH):
            lanes = slice(j * WIDTH, (j + 1) * WIDTH)
            copies[1 + j].wait()
            w_up = pack[:, UP_AT + 96 * j : UP_AT + 96 * (j + 1), :].reshape(WIDTH, WIDTH)
            hidden = dot(low, w_up) + up_bias[:, lanes]
            copies[5 + j].wait()
            w_down = pack[2 * j : 2 * j + 2, DOWN_AT:PACK_ROWS, :].reshape(WIDTH, WIDTH)
            upstream = dot_nt(result_grad, w_down)
            acted, slope = gelu_parts(hidden)
            acted = acted.astype(BF)
            mix_grad[2 * j : 2 * j + 2, DOWN_AT:, :] = (
                dot(acted.T, result_grad).astype(BF).reshape(2, 384, WIDTH)
            )
            sent.append(send(5 + j))
            total = total + dot(acted, w_down)
            pre = (upstream * slope).astype(BF)
            mix_grad[:, UP_AT + 96 * j : UP_AT + 96 * (j + 1), :] = (
                dot(low_t, pre).astype(BF).reshape(FSDP, 96, WIDTH)
            )
            sent.append(send(1 + j))
            up_sums[:, lanes] = jnp.sum(pre.astype(F32), axis=0, keepdims=True)
            grad_normed = grad_normed + dot_nt(pre, w_up)
        mixed[...] = total.astype(BF)
        back = result_grad.astype(F32) + norm_back(grad_normed, hat, inverse, gain[...])
        grad_residual[...] = back
        branch = back.astype(BF)
        grad_attended = dot_nt(branch, w_out)
        for head in range(HEADS):
            lanes = slice(head * DEPTH, (head + 1) * DEPTH)
            grad_heads[head] = jnp.concatenate(
                [grad_attended[:HALF, lanes], grad_attended[HALF:, lanes]], axis=1
            ).astype(BF)
        for head in range(HEADS, CTX):
            grad_heads[head] = jnp.zeros((HALF, 2 * DEPTH), BF)
        mix_grad[:, OUT_AT:UP_AT, :] = (
            dot(attended_low.T, branch).astype(BF).reshape(FSDP, 96, WIDTH)
        )
        sent.append(send(0))
        vector_sums[0:1, :] = jnp.sum(branch.astype(F32), axis=0, keepdims=True)
        vector_sums[1:2, :] = jnp.sum(grad_normed * hat, axis=0, keepdims=True)
        vector_sums[2:3, :] = jnp.sum(grad_normed, axis=0, keepdims=True)
        vector_sums[3:4, :] = jnp.sum(result_grad.astype(F32), axis=0, keepdims=True)
        for copy in sent:
            copy.wait()

    shape = jax.ShapeDtypeStruct
    outs = [
        shape((ROWS, WIDTH), BF),
        shape((FSDP, PACK_ROWS, WIDTH), BF),
        shape((CTX, HALF, 2 * DEPTH), BF),
        shape((ROWS, WIDTH), F32),
        shape((4, WIDTH), F32),
        shape((1, HIDDEN), F32),
    ]
    return pl.pallas_call(
        kernel,
        out_shape=outs,
        in_specs=[pl.BlockSpec(memory_space=pl.ANY)]
        + [pl.BlockSpec(memory_space=pltpu.VMEM)] * 8,
        out_specs=[
            pl.BlockSpec(memory_space=pl.ANY if index == 1 else pltpu.VMEM)
            for index in range(len(outs))
        ],
        scratch_shapes=[
            pltpu.VMEM((FSDP, PACK_ROWS, WIDTH), BF),
            pltpu.SemaphoreType.DMA((9,)),
            pltpu.VMEM((FSDP, PACK_ROWS, WIDTH), BF),
            pltpu.SemaphoreType.DMA((9,)),
        ],
        compiler_params=pltpu.CompilerParams(vmem_limit_bytes=VMEM_LIMIT),
        cost_estimate=pl.CostEstimate(
            flops=4 * 10**9, bytes_accessed=24 * 2**20, transcendentals=4 * 10**5
        ),
    )(pack, tokens, heads_out, cotangent, out_bias, gain, shift, up_bias, down_bias)


def token_gradient(weight, tokens, heads_grad, gain, grad_residual):
    def kernel(weight, tokens, heads_grad, gain, grad_residual, tokens_grad):
        hat, inverse = normalise(tokens[...].astype(F32))
        projected = jnp.concatenate(
            [unpack_heads(heads_grad, 2 * DEPTH * part) for part in range(3)], axis=1
        )
        grad_normed = dot_nt(projected, weight[...])
        tokens_grad[...] = grad_residual[...] + norm_back(grad_normed, hat, inverse, gain[...])

    return vmem_call(
        kernel,
        [jax.ShapeDtypeStruct((ROWS, WIDTH), F32)],
        [],
        2 * ROWS * WIDTH * 3 * WIDTH,
        5,
    )(weight, tokens, heads_grad, gain, grad_residual)[0]


def early_slots(where, hats, rows, weight, gain, shift, bias_sums, vector_sums, up_sums):
    def kernel(where, hats, rows, weight, gain, shift, bias_sums, vector_sums, up_sums, slots):
        place = where[0]

        made = dot_tn(rows[...], hats[...])
        column = jnp.broadcast_to(bias_sums[...], (8, 3 * DEPTH)).T[:, :1]
        weight_t = weight[...].astype(F32).T
        first_gain = jnp.sum(weight_t * made, axis=0, keepdims=True)
        first_shift = jnp.sum(weight_t * column, axis=0, keepdims=True)
        weight_grad = (made * gain[...] + column * shift[...]).T
        for owner in range(FSDP):
            slots[owner, :96, :] = weight_grad[96 * owner : 96 * (owner + 1)].astype(BF)

        tall = jnp.zeros((2, 3 * DEPTH), F32)
        bias_rows = []
        for part in (0, 2):
            piece = bias_sums[:, part * DEPTH : (part + 1) * DEPTH]
            for head in range(HEADS):
                bias_rows.append(jnp.where(place == head, piece, 0.0))
        for owner in range(FSDP):
            lanes = slice(96 * owner, 96 * (owner + 1))
            values = dict(
                first_gain=first_gain[:, lanes],
                first_shift=first_shift[:, lanes],
                qv_bias=jnp.concatenate(bias_rows[3 * owner : 3 * owner + 3], axis=1),
                out_bias=vector_sums[0:1, lanes],
                second_gain=vector_sums[1:2, lanes],
                second_shift=vector_sums[2:3, lanes],
                up_bias=up_sums[:, 384 * owner : 384 * (owner + 1)],
                down_bias=vector_sums[3:4, lanes],
            )
            line = jnp.concatenate([values[name] for name, _ in VECTORS], axis=1)
            pieces = [line[:, 192 * r : 192 * (r + 1)] for r in range(6)] + [tall]
            slots[owner, 96:, :] = jnp.concatenate(pieces, axis=0).astype(BF)

    return vmem_call(
        kernel,
        [jax.ShapeDtypeStruct((FSDP, 104, 3 * DEPTH), BF)],
        [],
        2 * SEQ * WIDTH * 3 * DEPTH,
        8,
        smem=1,
    )(where, hats, rows, weight, gain, shift, bias_sums, vector_sums, up_sums)[0]


def early_sums(parts):
    def kernel(own, left, right, far, out):
        total = (
            own[...].astype(F32) + left[...].astype(F32) + right[...].astype(F32)
            + far[...].astype(F32)
        )
        head = jnp.concatenate([total[24 * k : 24 * (k + 1)] for k in range(4)], axis=1)
        line = jnp.concatenate([total[96:104], jnp.zeros((8, 9 * DEPTH), F32)], axis=1)
        out[...] = jnp.concatenate([head, line], axis=0).astype(BF)

    return vmem_call(kernel, [jax.ShapeDtypeStruct((EARLY_ROWS, WIDTH), BF)], [], 10**6, 4)(*parts)[0]


def early_grads(pieces):
    def kernel(pieces, grad_qkv, *vector_refs):
        lines = jnp.zeros((8, 3 * DEPTH), F32)
        heads = []
        for n in range(CTX):
            piece = pieces[n].astype(F32)
            lines = lines + piece[24:, : 3 * DEPTH]
            if n < HEADS:
                heads.append(
                    jnp.concatenate(
                        [piece[:24, 192 * k : 192 * (k + 1)] for k in range(4)], axis=0
                    )
                )
        line = jnp.concatenate([lines[r : r + 1] for r in range(6)], axis=1)
        at = 0
        for ref, (_, width) in zip(vector_refs, VECTORS):
            ref[...] = line[:, at : at + width]
            at += width
        for part in range(3):
            grad_qkv[:, part * WIDTH : (part + 1) * WIDTH] = jnp.concatenate(
                [head[:, part * DEPTH : (part + 1) * DEPTH] for head in heads], axis=1
            )

    shape = jax.ShapeDtypeStruct
    return vmem_call(
        kernel,
        [shape((96, 3 * WIDTH), F32)] + [shape((1, width), F32) for _, width in VECTORS],
        [],
        10**6,
        1,
    )(pieces)


def last_pieces(parts):
    def kernel(parts, out):
        total = parts[0].astype(F32)
        for source in range(1, CTX):
            total = total + parts[source].astype(F32)
        total = total.astype(BF)
        for target in range(CTX):
            out[target] = total

    return vmem_call(
        kernel, [jax.ShapeDtypeStruct((CTX, SHARE, WIDTH), BF)], [], 10**6, 1
    )(parts)[0]


def last_grads(pieces):
    def kernel(pieces, grad_out, grad_up, grad_down):
        shard = jnp.concatenate([pieces[n].astype(F32) for n in range(CTX)], axis=0)
        grad_out[...] = shard[OUT_AT:UP_AT]
        for j in range(HIDDEN // WIDTH):
            grad_up[:, j * WIDTH : (j + 1) * WIDTH] = shard[UP_AT + 96 * j : UP_AT + 96 * (j + 1)]
        grad_down[...] = shard[DOWN_AT:]

    shape = jax.ShapeDtypeStruct
    return vmem_call(
        kernel,
        [shape((96, WIDTH), F32), shape((96, HIDDEN), F32), shape((384, WIDTH), F32)],
        [],
        10**6,
        1,
    )(pieces)


def swap(slots, axes):
    return lax.all_to_all(slots, axes, 0, 0, tiled=True)


def spread(piece, axes, count):
    return swap(jnp.broadcast_to(piece[None], (count,) + piece.shape), axes)


def shift_by(value, z=0, x=0, y=0, core=0):
    pairs = []
    for at_z in range(SIDE):
        for at_x in range(SIDE):
            for at_y in range(SIDE):
                for at_core in range(2):
                    source = (at_z * SIDE + at_x) * FSDP + at_y * 2 + at_core
                    to_ctx = (at_z + z) % SIDE * SIDE + (at_x + x) % SIDE
                    to_fsdp = (at_y + y) % SIDE * 2 + (at_core + core) % 2
                    pairs.append((source, to_ctx * FSDP + to_fsdp))
    return lax.ppermute(value, ("ctx", "fsdp"), pairs)


def gather_rows(values):
    blocks = []
    steps = (0, SIDE - 1, 1, 2)
    for half, first, second in ((0, "x", "z"), (1, "z", "x")):
        mine = values[half * HALF : (half + 1) * HALF]
        near = jnp.stack([mine] + [shift_by(mine, **{first: by}) for by in (1, -1, 2)])
        ahead, behind = shift_by(near, **{second: 1}), shift_by(near, **{second: -1})
        far_one = shift_by(ahead[:2], **{second: 1})
        far_two = shift_by(behind[2:], **{second: -1})

        def offsets(across, along):
            return [(across, by) if second == "z" else (by, across) for by in along]

        blocks += [
            (half, offsets(0, steps), near),
            (half, offsets(SIDE - 1, steps), ahead),
            (half, offsets(1, steps), behind),
            (half, offsets(2, steps[:2]), far_one),
            (half, offsets(2, steps[2:]), far_two),
        ]
    return blocks


def gather_small(piece):
    at = lax.axis_index("fsdp")
    at_y, at_core = at // 2, at % 2
    ring = jnp.stack(
        [piece, shift_by(piece, y=-1), shift_by(piece, y=2), shift_by(piece, y=1)]
    )
    other = shift_by(ring, core=1)
    first = jnp.where(at_core == 0, ring, other)
    second = jnp.where(at_core == 0, other, ring)
    both = jnp.stack([first, second], axis=1)
    turned = lax.dynamic_slice_in_dim(
        jnp.concatenate([both, both], axis=0), (SIDE - at_y) % SIDE, SIDE, 0
    )
    return turned.reshape((FSDP,) + piece.shape)


def scatter_small(slots):
    at = lax.axis_index("fsdp")
    at_y, at_core = at // 2, at % 2
    pairs = slots.reshape((SIDE, 2) + slots.shape[1:])
    mine = jnp.where(at_core == 0, pairs[:, 0], pairs[:, 1])
    theirs = jnp.where(at_core == 0, pairs[:, 1], pairs[:, 0])
    both = (mine.astype(F32) + shift_by(theirs, core=1).astype(F32)).astype(BF)

    def slot(by):
        return lax.dynamic_index_in_dim(both, (at_y + by) % SIDE, 0, keepdims=False)

    return [slot(0)] + [shift_by(slot(by), y=by) for by in (1, -1, 2)]


def local(
    tokens, cotangent, pair_order, first_gain, first_shift, qkv_weight, qv_bias, out_weight,
    out_bias, second_gain, second_shift, up_weight, up_bias, down_weight, down_bias,
):
    my_tokens, my_cotangent = tokens[0], cotangent[0]
    place = lax.axis_index("ctx")
    where = place.reshape(1).astype(jnp.int32)
    head = place % HEADS
    shards = dict(
        first_gain=first_gain, first_shift=first_shift, qv_bias=qv_bias, out_bias=out_bias,
        second_gain=second_gain, second_shift=second_shift, up_bias=up_bias, down_bias=down_bias,
    )

    with jax.named_scope("gather_tokens"):
        hat = normalised_rows(my_tokens)
        blocks = gather_rows(hat)
    with jax.named_scope("gather_weights"):
        out_weight, up_weight, down_weight, _ = lax.optimization_barrier(
            (out_weight, up_weight, down_weight, hat)
        )
        pack = packed_weights(out_weight, up_weight, down_weight)
        pack = lax.all_gather(pack, "fsdp", axis=0, tiled=False)
    with jax.named_scope("gather_small"):
        head_columns = jnp.concatenate(
            [
                lax.dynamic_slice_in_dim(qkv_weight, part * WIDTH + head * DEPTH, DEPTH, 1)
                for part in range(3)
            ],
            axis=1,
        )
        vectors = jnp.concatenate([shards[name] for name, _ in VECTORS]).reshape(6, 3 * DEPTH)
        small = gather_small(
            jnp.concatenate([head_columns, vectors, jnp.zeros((10, 3 * DEPTH), BF)], axis=0)
        )
        w_head = small[:, :96].reshape(WIDTH, 3 * DEPTH)
        vectors = small[:, 96:102].reshape(FSDP, VECTOR_WIDTH).astype(F32)
        whole, at = {}, 0
        for name, width in VECTORS:
            whole[name] = vectors[:, at : at + width].reshape(1, FSDP * width)
            at += width
        head_bias = jnp.concatenate(
            [
                lax.dynamic_slice_in_dim(whole["qv_bias"], head * DEPTH, DEPTH, 1),
                jnp.zeros((1, DEPTH), F32),
                lax.dynamic_slice_in_dim(whole["qv_bias"], WIDTH + head * DEPTH, DEPTH, 1),
            ],
            axis=1,
        )

    with jax.named_scope("attention"):
        packed, hats, query, key, value, query_t, key_t, out_t, lse = head_forward(
            pair_order, where, blocks, w_head, head_bias, whole["first_gain"],
            whole["first_shift"],
        )
        heads_out = swap(packed, "ctx")

    with jax.named_scope("feed_forward"):
        mixed, mix_grad, grad_heads, grad_residual, vector_sums, up_sums = feed_forward(
            pack, my_tokens, heads_out, my_cotangent, whole["out_bias"], whole["second_gain"],
            whole["second_shift"], whole["up_bias"], whole["down_bias"],
        )
        mix_shard = lax.psum_scatter(mix_grad, "fsdp", scatter_dimension=0, tiled=False)
        heads_up = swap(grad_heads, "ctx")

    with jax.named_scope("attention_back"):
        packed_grad, low_rows, bias_sums = head_backward(
            pair_order, heads_up, query, key, value, query_t, key_t, out_t, lse
        )
        heads_grad = swap(packed_grad, "ctx")

    with jax.named_scope("early_grads"):
        early = early_sums(
            scatter_small(
                early_slots(
                    where, hats, low_rows, w_head, whole["first_gain"], whole["first_shift"],
                    bias_sums, vector_sums, up_sums,
                )
            )
        )
        early, heads_grad = lax.optimization_barrier((early, heads_grad))
        early = spread(early, "ctx", CTX)

    with jax.named_scope("sum_over_ctx"):
        mix_shard, early = lax.optimization_barrier((mix_shard, early))
        parts = swap(mix_shard.reshape(CTX, SHARE, WIDTH), "ctx")
        shares, early = lax.optimization_barrier((last_pieces(parts), early))
        grad_out, grad_up, grad_down = last_grads(swap(shares, "ctx"))
        grad_qkv, *vector_grads = early_grads(early)
        grads = {
            name: grad.reshape(width) for grad, (name, width) in zip(vector_grads, VECTORS)
        }

    with jax.named_scope("token_gradient"):
        late_weight, heads_grad = lax.optimization_barrier((qkv_weight, heads_grad))
        w_qkv = lax.all_gather(late_weight, "fsdp", axis=0, tiled=True)
        tokens_grad = token_gradient(
            w_qkv, my_tokens, heads_grad, whole["first_gain"], grad_residual
        )

    return (
        mixed[None], tokens_grad[None], grads["first_gain"], grads["first_shift"], grad_qkv,
        grads["qv_bias"], grad_out, grads["out_bias"], grads["second_gain"],
        grads["second_shift"], grad_up, grads["up_bias"], grad_down, grads["down_bias"],
    )


def solution(mesh):
    split, vector = P("fsdp", "ctx", None), P("fsdp")
    matrix = P("fsdp", None)
    in_specs = (
        split, split, P(), vector, vector, matrix, vector, matrix, vector, vector, vector,
        matrix, vector, matrix, vector,
    )
    out_specs = (
        split, split, vector, vector, matrix, vector, matrix, vector, vector, vector, matrix,
        vector, matrix, vector,
    )
    return jax.shard_map(local, mesh=mesh, in_specs=in_specs, out_specs=out_specs, check_vma=False)
```

```python
import jax
import jax.numpy as jnp
from jax import lax
from jax.experimental import pallas as pl
from jax.experimental.pallas import tpu as pltpu
from jax.sharding import PartitionSpec as P

HEADS = 12
DEPTH = 64
WIDTH = 768
HIDDEN = 3072
ROWS = 128
HALF = 64
CTX = 16
FSDP = 8
SIDE = 4
SEQ = CTX * ROWS
QT = 512
KT = 512
EPSILON = 1e-05
SCALE_LOG2 = DEPTH ** -0.5 * 1.4426950408889634
NEGATIVE = -1e30
VMEM_LIMIT = 56 * 1024 * 1024

BF = jnp.bfloat16
F32 = jnp.float32

VECTORS = (
    ("first_gain", 96),
    ("first_shift", 96),
    ("qv_bias", 192),
    ("out_bias", 96),
    ("second_gain", 96),
    ("second_shift", 96),
    ("up_bias", 384),
    ("down_bias", 96),
)
VECTOR_WIDTH = sum(width for _, width in VECTORS)

OUT_AT, UP_AT, DOWN_AT, PACK_ROWS = 0, 96, 480, 864
SHARE = PACK_ROWS // CTX
EARLY_ROWS = 32


def dot(left, right):
    return jnp.dot(left, right, preferred_element_type=F32)


def dot_nt(left, right):
    return lax.dot_general(left, right, (((1,), (1,)), ((), ())), preferred_element_type=F32)


def dot_tn(left, right):
    return lax.dot_general(left, right, (((0,), (0,)), ((), ())), preferred_element_type=F32)


def normalise(values):
    center = values - jnp.mean(values, axis=-1, keepdims=True)
    spread = jnp.mean(center * center, axis=-1, keepdims=True)
    inverse = lax.rsqrt(spread + EPSILON)
    return center * inverse, inverse


def norm_back(upstream, hat, inverse, gain):
    scaled = upstream * gain
    mean_one = jnp.mean(scaled, axis=-1, keepdims=True)
    mean_two = jnp.mean(scaled * hat, axis=-1, keepdims=True)
    return (scaled - mean_one - hat * mean_two) * inverse


UNROLL = True


def loop(count, body):
    if UNROLL:
        for step in range(count):
            body(step, 0)
    else:
        lax.fori_loop(0, count, body, 0)


def block_at(index):
    return pl.ds(pl.multiple_of(index * HALF, HALF), HALF)


def lanes_at(index, size):
    if isinstance(index, int):
        return pl.ds(index * size, size)
    return pl.ds(pl.multiple_of(index * size, size), size)


def vmem_call(
    kernel, out_shape, scratch, flops, in_vmem, smem=0, transcendentals=0, far_outs=()
):
    specs = [pl.BlockSpec(memory_space=pltpu.VMEM)] * in_vmem
    specs = [pl.BlockSpec(memory_space=pltpu.SMEM)] * smem + specs
    return pl.pallas_call(
        kernel,
        out_shape=out_shape,
        in_specs=specs,
        out_specs=[
            pl.BlockSpec(memory_space=pl.ANY if index in far_outs else pltpu.VMEM)
            for index in range(len(out_shape))
        ],
        scratch_shapes=scratch,
        compiler_params=pltpu.CompilerParams(vmem_limit_bytes=VMEM_LIMIT),
        cost_estimate=pl.CostEstimate(
            flops=flops, bytes_accessed=8 * 2**20, transcendentals=transcendentals
        ),
    )


def packed_weights(out_weight, up_weight, down_weight):
    def kernel(out_weight, up_weight, down_weight, pack):
        pack[OUT_AT:UP_AT, :] = out_weight[...]
        for j in range(HIDDEN // WIDTH):
            pack[UP_AT + 96 * j : UP_AT + 96 * (j + 1), :] = up_weight[
                :, j * WIDTH : (j + 1) * WIDTH
            ]
        pack[DOWN_AT:PACK_ROWS, :] = down_weight[...]

    return vmem_call(
        kernel, [jax.ShapeDtypeStruct((PACK_ROWS, WIDTH), BF)], [], 10**6, 3
    )(out_weight, up_weight, down_weight)[0]


def normalised_rows(tokens):
    def kernel(tokens, hat):
        hat[...] = normalise(tokens[...].astype(F32))[0].astype(BF)

    return vmem_call(
        kernel, [jax.ShapeDtypeStruct((ROWS, WIDTH), BF)], [], 10**6, 1
    )(tokens)[0]


def head_forward_kernel(
    order, where, blocks, weight, bias, gain, shift,
    packed, hats, query, key, value, query_t, key_t, out_t, lse,
    value_t, projected,
):
    at_z, at_x = where[0] // SIDE, lax.rem(where[0], SIDE)

    for half, offsets, block in blocks:
        count = len(offsets)
        hat_low = block[...].reshape(count * HALF, WIDTH)
        low = (hat_low.astype(F32) * gain[...] + shift[...]).astype(BF)
        made = (dot(low, weight[...]) + bias[...]).astype(BF)
        for n, (dz, dx) in enumerate(offsets):
            place = order[lax.rem(at_z + dz, SIDE) * SIDE + lax.rem(at_x + dx, SIDE)]
            to = block_at(place if half == 0 else 2 * CTX - 1 - place)
            rows = slice(n * HALF, (n + 1) * HALF)
            hats[to, :] = hat_low[rows]
            query[to, :] = made[rows, 0:DEPTH]
            key[to, :] = made[rows, DEPTH : 2 * DEPTH]
            value[to, :] = made[rows, 2 * DEPTH :]

    projected()

    def turn(t, _):
        rows = lanes_at(t, QT)
        for source, target in ((query, query_t), (key, key_t), (value, value_t)):
            target[:, rows] = source[rows, :].astype(F32).T.astype(BF)
        return 0

    lax.fori_loop(0, SEQ // QT, turn, 0)

    def attend(i, _):
        lanes = lanes_at(i, QT)
        queries = query_t[:, lanes]

        def step(j, carry, masked):
            top, total, acc = carry
            rows = lanes_at(j, KT)
            scores = dot(key[rows, :], queries) * SCALE_LOG2
            if masked:
                key_place = j * KT + lax.broadcasted_iota(jnp.int32, (KT, QT), 0)
                query_place = i * QT + lax.broadcasted_iota(jnp.int32, (KT, QT), 1)
                scores = jnp.where(key_place <= query_place, scores, NEGATIVE)
            fresh = jnp.maximum(top, jnp.max(scores, axis=0, keepdims=True))
            raised = jnp.exp2(scores - fresh)
            fade = jnp.exp2(top - fresh)
            total = total * fade + jnp.sum(raised, axis=0, keepdims=True)
            acc = acc * fade + dot(value_t[:, rows], raised.astype(BF))
            return fresh, total, acc

        start = (
            jnp.full((1, QT), NEGATIVE, F32),
            jnp.zeros((1, QT), F32),
            jnp.zeros((DEPTH, QT), F32),
        )
        full = i * QT // KT
        if isinstance(i, int):
            carry = start
            for j in range(full):
                carry = step(j, carry, False)
        else:
            carry = lax.fori_loop(0, full, lambda j, carry: step(j, carry, False), start)
        for extra in range(max(1, QT // KT)):
            carry = step(full + extra, carry, True)
        top, total, acc = carry
        result = acc / total
        out_t[:, lanes] = result
        lse[pl.ds(i, 1), :] = top + jnp.log2(total)
        return 0

    loop(SEQ // QT, attend)


def head_forward(order, where, blocks, weight, bias, gain, shift):
    layout = [(half, offsets) for half, offsets, _ in blocks]

    def kernel(order, where, *refs):
        block_refs, refs = refs[: len(layout)], refs[len(layout) :]
        (
            weight, bias, gain, shift,
            packed, hats_out, query, key, value, query_t, key_t, out_t, lse,
            value_t, out_rows, hats, sem,
        ) = refs
        leave = pltpu.make_async_copy(hats, hats_out, sem.at[0])
        head_forward_kernel(
            order, where,
            [(half, offsets, ref) for (half, offsets), ref in zip(layout, block_refs)],
            weight, bias, gain, shift,
            packed, hats, query, key, value, query_t, key_t, out_t, lse,
            value_t, leave.start,
        )

        def turn_back(t, _):
            rows = lanes_at(t, QT)
            out_rows[rows, :] = out_t[:, rows].T
            return 0

        lax.fori_loop(0, SEQ // QT, turn_back, 0)

        def pack(c, _):
            place = order[c]
            packed[c] = jnp.concatenate(
                [out_rows[block_at(place), :], out_rows[block_at(2 * CTX - 1 - place), :]], axis=1
            ).astype(BF)
            return 0

        lax.fori_loop(0, CTX, pack, 0)
        leave.wait()

    shape = jax.ShapeDtypeStruct
    return vmem_call(
        kernel,
        [
            shape((CTX, HALF, 2 * DEPTH), BF),
            shape((SEQ, WIDTH), BF),
            shape((SEQ, DEPTH), BF),
            shape((SEQ, DEPTH), BF),
            shape((SEQ, DEPTH), BF),
            shape((DEPTH, SEQ), BF),
            shape((DEPTH, SEQ), BF),
            shape((DEPTH, SEQ), F32),
            shape((SEQ // QT, QT), F32),
        ],
        [
            pltpu.VMEM((DEPTH, SEQ), BF),
            pltpu.VMEM((SEQ, DEPTH), F32),
            pltpu.VMEM((SEQ, WIDTH), BF),
            pltpu.SemaphoreType.DMA((1,)),
        ],
        2 * 10**9,
        len(blocks) + 4,
        smem=2,
        transcendentals=3 * 10**6,
        far_outs=(1,),
    )(order, where, *[block for _, _, block in blocks], weight, bias, gain, shift)


def head_backward(order, upstream, query, key, value, query_t, key_t, out_t, lse):
    def kernel(
        order, upstream, query, key, value, query_t, key_t, out_t, lse,
        packed, low_rows, bias_grad,
        grad_out, grad_out_t, delta, grad_q_t, grad_k, grad_v, rows_low,
    ):
        def unpack(c, _):
            place = order[c]
            grad_out[block_at(place), :] = upstream[c][:, :DEPTH]
            grad_out[block_at(2 * CTX - 1 - place), :] = upstream[c][:, DEPTH:]
            return 0

        lax.fori_loop(0, CTX, unpack, 0)

        def prepare(t, _):
            rows = lanes_at(t, QT)
            turned = grad_out[rows, :].astype(F32).T
            grad_out_t[:, rows] = turned.astype(BF)
            delta[pl.ds(t, 1), :] = jnp.sum(turned * out_t[:, rows], axis=0, keepdims=True)
            grad_q_t[:, rows] = jnp.zeros((DEPTH, QT), F32)
            grad_k[rows, :] = jnp.zeros((QT, DEPTH), F32)
            grad_v[rows, :] = jnp.zeros((QT, DEPTH), F32)
            return 0

        lax.fori_loop(0, SEQ // QT, prepare, 0)

        def one_query_tile(i, _):
            lanes = lanes_at(i, QT)

            def step(j, masked):
                rows = lanes_at(j, KT)
                scores = dot(key[rows, :], query_t[:, lanes]) * SCALE_LOG2
                probs = jnp.exp2(scores - lse[pl.ds(i, 1), :])
                if masked:
                    key_place = j * KT + lax.broadcasted_iota(jnp.int32, (KT, QT), 0)
                    query_place = i * QT + lax.broadcasted_iota(jnp.int32, (KT, QT), 1)
                    probs = jnp.where(key_place <= query_place, probs, 0.0)
                slopes = dot(value[rows, :], grad_out_t[:, lanes])
                grad_scores = (probs * (slopes - delta[pl.ds(i, 1), :])).astype(BF)
                grad_v[rows, :] += dot(probs.astype(BF), grad_out[lanes, :])
                grad_k[rows, :] += dot(grad_scores, query[lanes, :])
                grad_q_t[:, lanes] += dot(key_t[:, rows], grad_scores)

            full = i * QT // KT

            def body(j, _):
                step(j, False)
                return 0

            (loop(full, body) if isinstance(i, int) else lax.fori_loop(0, full, body, 0))
            for extra in range(max(1, QT // KT)):
                step(full + extra, True)
            return 0

        loop(SEQ // QT, one_query_tile)

        def finish(t, sums):
            rows = lanes_at(t, QT)
            low_q = (grad_q_t[:, rows].T * (DEPTH ** -0.5)).astype(BF)
            low_k = (grad_k[rows, :] * (DEPTH ** -0.5)).astype(BF)
            low_v = grad_v[rows, :].astype(BF)
            joined = jnp.concatenate(
                [low_q.astype(F32), low_k.astype(F32), low_v.astype(F32)], axis=1
            )
            rows_low[rows, :] = joined
            low_rows[rows, :] = joined.astype(BF)
            return sums + jnp.sum(joined, axis=0, keepdims=True)

        sums = lax.fori_loop(0, SEQ // QT, finish, jnp.zeros((1, 3 * DEPTH), F32))
        bias_grad[...] = sums

        def pack(c, _):
            place = order[c]
            upper = rows_low[block_at(place), :]
            lower = rows_low[block_at(2 * CTX - 1 - place), :]
            pieces = []
            for part in range(3):
                lanes = slice(part * DEPTH, (part + 1) * DEPTH)
                pieces += [upper[:, lanes], lower[:, lanes]]
            packed[c] = jnp.concatenate(pieces, axis=1).astype(BF)
            return 0

        lax.fori_loop(0, CTX, pack, 0)

    shape = jax.ShapeDtypeStruct
    return vmem_call(
        kernel,
        [
            shape((CTX, HALF, 6 * DEPTH), BF),
            shape((SEQ, 3 * DEPTH), BF),
            shape((1, 3 * DEPTH), F32),
        ],
        [
            pltpu.VMEM((SEQ, DEPTH), BF),
            pltpu.VMEM((DEPTH, SEQ), BF),
            pltpu.VMEM((SEQ // QT, QT), F32),
            pltpu.VMEM((DEPTH, SEQ), F32),
            pltpu.VMEM((SEQ, DEPTH), F32),
            pltpu.VMEM((SEQ, DEPTH), F32),
            pltpu.VMEM((SEQ, 3 * DEPTH), F32),
        ],
        4 * 10**9,
        8,
        smem=1,
        transcendentals=3 * 10**6,
    )(order, upstream, query, key, value, query_t, key_t, out_t, lse)


def unpack_heads(ref, lanes):
    upper, lower = [], []
    for head in range(HEADS):
        slot = ref[head][:, lanes : lanes + 2 * DEPTH].astype(F32)
        upper.append(slot[:, :DEPTH])
        lower.append(slot[:, DEPTH:])
    return jnp.concatenate(
        [jnp.concatenate(upper, axis=1), jnp.concatenate(lower, axis=1)], axis=0
    ).astype(BF)


def gelu_parts(values):
    slope = 0.7978845608028654
    cubic = 0.044715
    squared = values * values
    bend = jnp.tanh(slope * (values + cubic * squared * values))
    active = 0.5 * values * (1.0 + bend)
    grad = 0.5 * (1.0 + bend) + 0.5 * values * (1.0 - bend * bend) * slope * (
        1.0 + 3.0 * cubic * squared
    )
    return active, grad


def pack_piece(source, held, sems, index):
    if index == 0:
        rows = (slice(0, FSDP), pl.ds(OUT_AT, 96))
    elif index <= 4:
        rows = (slice(0, FSDP), pl.ds(UP_AT + 96 * (index - 1), 96))
    else:
        rows = (pl.ds(2 * (index - 5), 2), pl.ds(DOWN_AT, 384))
    return pltpu.make_async_copy(source.at[rows], held.at[rows], sems.at[index])


def feed_forward(pack, tokens, heads_out, cotangent, out_bias, gain, shift, up_bias, down_bias):
    def kernel(
        source, tokens, heads_out, cotangent, out_bias, gain, shift, up_bias, down_bias,
        mixed, grads_out, grad_heads, grad_residual, vector_sums, up_sums,
        pack, sems, mix_grad, out_sems,
    ):
        order = [0] + [index for j in range(4) for index in (1 + j, 5 + j)]
        copies = {index: pack_piece(source, pack, sems, index) for index in order}
        for index in order:
            copies[index].start()

        def send(index):
            copy = pack_piece(mix_grad, grads_out, out_sems, index)
            copy.start()
            return copy

        sent = []
        inputs = tokens[...].astype(F32)
        result_grad = cotangent[...]
        attended_low = unpack_heads(heads_out, 0)
        copies[0].wait()
        w_out = pack[:, OUT_AT:UP_AT, :].reshape(WIDTH, WIDTH)
        residual = inputs + dot(attended_low, w_out) + out_bias[...]
        hat, inverse = normalise(residual)
        low = (hat * gain[...] + shift[...]).astype(BF)
        low_t = low.T
        total = residual + down_bias[...]
        grad_normed = jnp.zeros((ROWS, WIDTH), F32)
        for j in range(HIDDEN // WIDTH):
            lanes = slice(j * WIDTH, (j + 1) * WIDTH)
            copies[1 + j].wait()
            w_up = pack[:, UP_AT + 96 * j : UP_AT + 96 * (j + 1), :].reshape(WIDTH, WIDTH)
            hidden = dot(low, w_up) + up_bias[:, lanes]
            copies[5 + j].wait()
            w_down = pack[2 * j : 2 * j + 2, DOWN_AT:PACK_ROWS, :].reshape(WIDTH, WIDTH)
            upstream = dot_nt(result_grad, w_down)
            acted, slope = gelu_parts(hidden)
            acted = acted.astype(BF)
            mix_grad[2 * j : 2 * j + 2, DOWN_AT:, :] = (
                dot(acted.T, result_grad).astype(BF).reshape(2, 384, WIDTH)
            )
            sent.append(send(5 + j))
            total = total + dot(acted, w_down)
            pre = (upstream * slope).astype(BF)
            mix_grad[:, UP_AT + 96 * j : UP_AT + 96 * (j + 1), :] = (
                dot(low_t, pre).astype(BF).reshape(FSDP, 96, WIDTH)
            )
            sent.append(send(1 + j))
            up_sums[:, lanes] = jnp.sum(pre.astype(F32), axis=0, keepdims=True)
            grad_normed = grad_normed + dot_nt(pre, w_up)
        mixed[...] = total.astype(BF)
        back = result_grad.astype(F32) + norm_back(grad_normed, hat, inverse, gain[...])
        grad_residual[...] = back
        branch = back.astype(BF)
        mix_grad[:, OUT_AT:UP_AT, :] = (
            dot(attended_low.T, branch).astype(BF).reshape(FSDP, 96, WIDTH)
        )
        sent.append(send(0))
        grad_attended = dot_nt(branch, w_out)
        for head in range(HEADS):
            lanes = slice(head * DEPTH, (head + 1) * DEPTH)
            grad_heads[head] = jnp.concatenate(
                [grad_attended[:HALF, lanes], grad_attended[HALF:, lanes]], axis=1
            ).astype(BF)
        for head in range(HEADS, CTX):
            grad_heads[head] = jnp.zeros((HALF, 2 * DEPTH), BF)
        vector_sums[0:1, :] = jnp.sum(branch.astype(F32), axis=0, keepdims=True)
        vector_sums[1:2, :] = jnp.sum(grad_normed * hat, axis=0, keepdims=True)
        vector_sums[2:3, :] = jnp.sum(grad_normed, axis=0, keepdims=True)
        vector_sums[3:4, :] = jnp.sum(result_grad.astype(F32), axis=0, keepdims=True)
        for copy in sent:
            copy.wait()

    shape = jax.ShapeDtypeStruct
    outs = [
        shape((ROWS, WIDTH), BF),
        shape((FSDP, PACK_ROWS, WIDTH), BF),
        shape((CTX, HALF, 2 * DEPTH), BF),
        shape((ROWS, WIDTH), F32),
        shape((4, WIDTH), F32),
        shape((1, HIDDEN), F32),
    ]
    return pl.pallas_call(
        kernel,
        out_shape=outs,
        in_specs=[pl.BlockSpec(memory_space=pl.ANY)]
        + [pl.BlockSpec(memory_space=pltpu.VMEM)] * 8,
        out_specs=[
            pl.BlockSpec(memory_space=pl.ANY if index == 1 else pltpu.VMEM)
            for index in range(len(outs))
        ],
        scratch_shapes=[
            pltpu.VMEM((FSDP, PACK_ROWS, WIDTH), BF),
            pltpu.SemaphoreType.DMA((9,)),
            pltpu.VMEM((FSDP, PACK_ROWS, WIDTH), BF),
            pltpu.SemaphoreType.DMA((9,)),
        ],
        compiler_params=pltpu.CompilerParams(vmem_limit_bytes=VMEM_LIMIT),
        cost_estimate=pl.CostEstimate(
            flops=4 * 10**9, bytes_accessed=24 * 2**20, transcendentals=4 * 10**5
        ),
    )(pack, tokens, heads_out, cotangent, out_bias, gain, shift, up_bias, down_bias)


def token_gradient(weight, tokens, heads_grad, gain, grad_residual):
    def kernel(weight, tokens, heads_grad, gain, grad_residual, tokens_grad):
        hat, inverse = normalise(tokens[...].astype(F32))
        projected = jnp.concatenate(
            [unpack_heads(heads_grad, 2 * DEPTH * part) for part in range(3)], axis=1
        )
        grad_normed = dot_nt(projected, weight[...])
        tokens_grad[...] = grad_residual[...] + norm_back(grad_normed, hat, inverse, gain[...])

    return vmem_call(
        kernel,
        [jax.ShapeDtypeStruct((ROWS, WIDTH), F32)],
        [],
        2 * ROWS * WIDTH * 3 * WIDTH,
        5,
    )(weight, tokens, heads_grad, gain, grad_residual)[0]


def early_slots(where, hats, rows, weight, gain, shift, bias_sums, vector_sums, up_sums):
    def kernel(where, hats, rows, weight, gain, shift, bias_sums, vector_sums, up_sums, slots):
        place = where[0]

        made = dot_tn(rows[...], hats[...])
        column = jnp.broadcast_to(bias_sums[...], (8, 3 * DEPTH)).T[:, :1]
        weight_t = weight[...].astype(F32).T
        first_gain = jnp.sum(weight_t * made, axis=0, keepdims=True)
        first_shift = jnp.sum(weight_t * column, axis=0, keepdims=True)
        weight_grad = (made * gain[...] + column * shift[...]).T
        for owner in range(FSDP):
            slots[owner, :96, :] = weight_grad[96 * owner : 96 * (owner + 1)].astype(BF)

        tall = jnp.zeros((2, 3 * DEPTH), F32)
        bias_rows = []
        for part in (0, 2):
            piece = bias_sums[:, part * DEPTH : (part + 1) * DEPTH]
            for head in range(HEADS):
                bias_rows.append(jnp.where(place == head, piece, 0.0))
        for owner in range(FSDP):
            lanes = slice(96 * owner, 96 * (owner + 1))
            values = dict(
                first_gain=first_gain[:, lanes],
                first_shift=first_shift[:, lanes],
                qv_bias=jnp.concatenate(bias_rows[3 * owner : 3 * owner + 3], axis=1),
                out_bias=vector_sums[0:1, lanes],
                second_gain=vector_sums[1:2, lanes],
                second_shift=vector_sums[2:3, lanes],
                up_bias=up_sums[:, 384 * owner : 384 * (owner + 1)],
                down_bias=vector_sums[3:4, lanes],
            )
            line = jnp.concatenate([values[name] for name, _ in VECTORS], axis=1)
            pieces = [line[:, 192 * r : 192 * (r + 1)] for r in range(6)] + [tall]
            slots[owner, 96:, :] = jnp.concatenate(pieces, axis=0).astype(BF)

    return vmem_call(
        kernel,
        [jax.ShapeDtypeStruct((FSDP, 104, 3 * DEPTH), BF)],
        [],
        2 * SEQ * WIDTH * 3 * DEPTH,
        8,
        smem=1,
    )(where, hats, rows, weight, gain, shift, bias_sums, vector_sums, up_sums)[0]


def early_sums(parts):
    def kernel(own, left, right, far, out):
        total = (
            own[...].astype(F32) + left[...].astype(F32) + right[...].astype(F32)
            + far[...].astype(F32)
        )
        head = jnp.concatenate([total[24 * k : 24 * (k + 1)] for k in range(4)], axis=1)
        line = jnp.concatenate([total[96:104], jnp.zeros((8, 9 * DEPTH), F32)], axis=1)
        joined = jnp.concatenate([head, line], axis=0).astype(BF)
        for target in range(CTX):
            out[target] = joined

    return vmem_call(kernel, [jax.ShapeDtypeStruct((CTX, EARLY_ROWS, WIDTH), BF)], [], 10**6, 4)(*parts)[0]


def early_grads(pieces):
    def kernel(pieces, grad_qkv, *vector_refs):
        lines = jnp.zeros((8, 3 * DEPTH), F32)
        heads = []
        for n in range(CTX):
            piece = pieces[n].astype(F32)
            lines = lines + piece[24:, : 3 * DEPTH]
            if n < HEADS:
                heads.append(
                    jnp.concatenate(
                        [piece[:24, 192 * k : 192 * (k + 1)] for k in range(4)], axis=0
                    )
                )
        line = jnp.concatenate([lines[r : r + 1] for r in range(6)], axis=1)
        at = 0
        for ref, (_, width) in zip(vector_refs, VECTORS):
            ref[...] = line[:, at : at + width]
            at += width
        for part in range(3):
            grad_qkv[:, part * WIDTH : (part + 1) * WIDTH] = jnp.concatenate(
                [head[:, part * DEPTH : (part + 1) * DEPTH] for head in heads], axis=1
            )

    shape = jax.ShapeDtypeStruct
    return vmem_call(
        kernel,
        [shape((96, 3 * WIDTH), F32)] + [shape((1, width), F32) for _, width in VECTORS],
        [],
        10**6,
        1,
    )(pieces)


def last_pieces(parts):
    def kernel(parts, out):
        total = parts[0].astype(F32)
        for source in range(1, CTX):
            total = total + parts[source].astype(F32)
        total = total.astype(BF)
        for target in range(CTX):
            out[target] = total

    return vmem_call(
        kernel, [jax.ShapeDtypeStruct((CTX, SHARE, WIDTH), BF)], [], 10**6, 1
    )(parts)[0]


def last_grads(pieces):
    def kernel(pieces, grad_out, grad_up, grad_down):
        shard = jnp.concatenate([pieces[n].astype(F32) for n in range(CTX)], axis=0)
        grad_out[...] = shard[OUT_AT:UP_AT]
        for j in range(HIDDEN // WIDTH):
            grad_up[:, j * WIDTH : (j + 1) * WIDTH] = shard[UP_AT + 96 * j : UP_AT + 96 * (j + 1)]
        grad_down[...] = shard[DOWN_AT:]

    shape = jax.ShapeDtypeStruct
    return vmem_call(
        kernel,
        [shape((96, WIDTH), F32), shape((96, HIDDEN), F32), shape((384, WIDTH), F32)],
        [],
        10**6,
        1,
    )(pieces)


def swap(slots, axes):
    return lax.all_to_all(slots, axes, 0, 0, tiled=True)


def shift_by(value, z=0, x=0, y=0, core=0):
    pairs = []
    for at_z in range(SIDE):
        for at_x in range(SIDE):
            for at_y in range(SIDE):
                for at_core in range(2):
                    source = (at_z * SIDE + at_x) * FSDP + at_y * 2 + at_core
                    to_ctx = (at_z + z) % SIDE * SIDE + (at_x + x) % SIDE
                    to_fsdp = (at_y + y) % SIDE * 2 + (at_core + core) % 2
                    pairs.append((source, to_ctx * FSDP + to_fsdp))
    return lax.ppermute(value, ("ctx", "fsdp"), pairs)


def gather_rows(values):
    blocks = []
    steps = (0, SIDE - 1, 1, 2)
    for half, first, second in ((0, "x", "z"), (1, "z", "x")):
        mine = values[half * HALF : (half + 1) * HALF]
        near = jnp.stack([mine] + [shift_by(mine, **{first: by}) for by in (1, -1, 2)])
        ahead, behind = shift_by(near, **{second: 1}), shift_by(near, **{second: -1})
        far_one = shift_by(ahead[:2], **{second: 1})
        far_two = shift_by(behind[2:], **{second: -1})

        def offsets(across, along):
            return [(across, by) if second == "z" else (by, across) for by in along]

        blocks += [
            (half, offsets(0, steps), near),
            (half, offsets(SIDE - 1, steps), ahead),
            (half, offsets(1, steps), behind),
            (half, offsets(2, steps[:2]), far_one),
            (half, offsets(2, steps[2:]), far_two),
        ]
    return blocks


def gather_small(piece):
    at = lax.axis_index("fsdp")
    at_y, at_core = at // 2, at % 2
    ring = jnp.stack(
        [piece, shift_by(piece, y=-1), shift_by(piece, y=2), shift_by(piece, y=1)]
    )
    other = shift_by(ring, core=1)
    first = jnp.where(at_core == 0, ring, other)
    second = jnp.where(at_core == 0, other, ring)
    both = jnp.stack([first, second], axis=1)
    turned = lax.dynamic_slice_in_dim(
        jnp.concatenate([both, both], axis=0), (SIDE - at_y) % SIDE, SIDE, 0
    )
    return turned.reshape((FSDP,) + piece.shape)


def scatter_small(slots):
    at = lax.axis_index("fsdp")
    at_y, at_core = at // 2, at % 2
    pairs = slots.reshape((SIDE, 2) + slots.shape[1:])
    mine = jnp.where(at_core == 0, pairs[:, 0], pairs[:, 1])
    theirs = jnp.where(at_core == 0, pairs[:, 1], pairs[:, 0])
    both = (mine.astype(F32) + shift_by(theirs, core=1).astype(F32)).astype(BF)

    def slot(by):
        return lax.dynamic_index_in_dim(both, (at_y + by) % SIDE, 0, keepdims=False)

    return [slot(0)] + [shift_by(slot(by), y=by) for by in (1, -1, 2)]


def local(
    tokens, cotangent, pair_order, first_gain, first_shift, qkv_weight, qv_bias, out_weight,
    out_bias, second_gain, second_shift, up_weight, up_bias, down_weight, down_bias,
):
    my_tokens, my_cotangent = tokens[0], cotangent[0]
    place = lax.axis_index("ctx")
    where = place.reshape(1).astype(jnp.int32)
    head = place % HEADS
    shards = dict(
        first_gain=first_gain, first_shift=first_shift, qv_bias=qv_bias, out_bias=out_bias,
        second_gain=second_gain, second_shift=second_shift, up_bias=up_bias, down_bias=down_bias,
    )

    with jax.named_scope("gather_tokens"):
        hat = normalised_rows(my_tokens)
        blocks = gather_rows(hat)
    with jax.named_scope("gather_weights"):
        out_weight, up_weight, down_weight, _ = lax.optimization_barrier(
            (out_weight, up_weight, down_weight, hat)
        )
        pack = packed_weights(out_weight, up_weight, down_weight)
        pack = lax.all_gather(pack, "fsdp", axis=0, tiled=False)
    with jax.named_scope("gather_small"):
        head_columns = jnp.concatenate(
            [
                lax.dynamic_slice_in_dim(qkv_weight, part * WIDTH + head * DEPTH, DEPTH, 1)
                for part in range(3)
            ],
            axis=1,
        )
        vectors = jnp.concatenate([shards[name] for name, _ in VECTORS]).reshape(6, 3 * DEPTH)
        small = gather_small(
            jnp.concatenate([head_columns, vectors, jnp.zeros((10, 3 * DEPTH), BF)], axis=0)
        )
        w_head = small[:, :96].reshape(WIDTH, 3 * DEPTH)
        vectors = small[:, 96:102].reshape(FSDP, VECTOR_WIDTH).astype(F32)
        whole, at = {}, 0
        for name, width in VECTORS:
            whole[name] = vectors[:, at : at + width].reshape(1, FSDP * width)
            at += width
        head_bias = jnp.concatenate(
            [
                lax.dynamic_slice_in_dim(whole["qv_bias"], head * DEPTH, DEPTH, 1),
                jnp.zeros((1, DEPTH), F32),
                lax.dynamic_slice_in_dim(whole["qv_bias"], WIDTH + head * DEPTH, DEPTH, 1),
            ],
            axis=1,
        )

    with jax.named_scope("attention"):
        packed, hats, query, key, value, query_t, key_t, out_t, lse = head_forward(
            pair_order, where, blocks, w_head, head_bias, whole["first_gain"],
            whole["first_shift"],
        )
        heads_out = swap(packed, "ctx")

    with jax.named_scope("feed_forward"):
        mixed, mix_grad, grad_heads, grad_residual, vector_sums, up_sums = feed_forward(
            pack, my_tokens, heads_out, my_cotangent, whole["out_bias"], whole["second_gain"],
            whole["second_shift"], whole["up_bias"], whole["down_bias"],
        )
        mix_shard = lax.psum_scatter(mix_grad, "fsdp", scatter_dimension=0, tiled=False)
        heads_up = swap(grad_heads, "ctx")

    with jax.named_scope("attention_back"):
        packed_grad, low_rows, bias_sums = head_backward(
            pair_order, heads_up, query, key, value, query_t, key_t, out_t, lse
        )
        heads_grad = swap(packed_grad, "ctx")

    with jax.named_scope("early_grads"):
        early = early_sums(
            scatter_small(
                early_slots(
                    where, hats, low_rows, w_head, whole["first_gain"], whole["first_shift"],
                    bias_sums, vector_sums, up_sums,
                )
            )
        )
        early, heads_grad = lax.optimization_barrier((early, heads_grad))
        early = swap(early, "ctx")

    with jax.named_scope("sum_over_ctx"):
        slots = mix_shard.reshape(CTX, SHARE, WIDTH)
        slots, early = lax.optimization_barrier((slots, early))
        parts = swap(slots, "ctx")
        shares, early = lax.optimization_barrier((last_pieces(parts), early))
        grad_out, grad_up, grad_down = last_grads(swap(shares, "ctx"))
        grad_qkv, *vector_grads = early_grads(early)
        grads = {
            name: grad.reshape(width) for grad, (name, width) in zip(vector_grads, VECTORS)
        }

    with jax.named_scope("token_gradient"):
        late_weight, heads_grad = lax.optimization_barrier((qkv_weight, heads_grad))
        w_qkv = lax.all_gather(late_weight, "fsdp", axis=0, tiled=True)
        tokens_grad = token_gradient(
            w_qkv, my_tokens, heads_grad, whole["first_gain"], grad_residual
        )

    return (
        mixed[None], tokens_grad[None], grads["first_gain"], grads["first_shift"], grad_qkv,
        grads["qv_bias"], grad_out, grads["out_bias"], grads["second_gain"],
        grads["second_shift"], grad_up, grads["up_bias"], grad_down, grads["down_bias"],
    )


def solution(mesh):
    split, vector = P("fsdp", "ctx", None), P("fsdp")
    matrix = P("fsdp", None)
    in_specs = (
        split, split, P(), vector, vector, matrix, vector, matrix, vector, vector, vector,
        matrix, vector, matrix, vector,
    )
    out_specs = (
        split, split, vector, vector, matrix, vector, matrix, vector, vector, vector, matrix,
        vector, matrix, vector,
    )
    return jax.shard_map(local, mesh=mesh, in_specs=in_specs, out_specs=out_specs, check_vma=False)
```

```python
import jax
import jax.numpy as jnp
from jax import lax
from jax.experimental import pallas as pl
from jax.experimental.pallas import tpu as pltpu
from jax.sharding import PartitionSpec as P

HEADS = 12
DEPTH = 64
WIDTH = 768
HIDDEN = 3072
ROWS = 128
HALF = 64
CTX = 16
FSDP = 8
SIDE = 4
SEQ = CTX * ROWS
QT = 512
KT = 512
EPSILON = 1e-05
SCALE_LOG2 = DEPTH ** -0.5 * 1.4426950408889634
NEGATIVE = -1e30
MIB = 1024 * 1024

BF = jnp.bfloat16
F32 = jnp.float32

VECTORS = (
    ("first_gain", 96),
    ("first_shift", 96),
    ("qv_bias", 192),
    ("out_bias", 96),
    ("second_gain", 96),
    ("second_shift", 96),
    ("up_bias", 384),
    ("down_bias", 96),
)
VECTOR_WIDTH = sum(width for _, width in VECTORS)

OUT_AT, UP_AT, DOWN_AT, PACK_ROWS = 0, 96, 480, 864
SHARE = PACK_ROWS // CTX
EARLY_ROWS = 32


def dot(left, right):
    return jnp.dot(left, right, preferred_element_type=F32)


def dot_nt(left, right):
    return lax.dot_general(left, right, (((1,), (1,)), ((), ())), preferred_element_type=F32)


def dot_tn(left, right):
    return lax.dot_general(left, right, (((0,), (0,)), ((), ())), preferred_element_type=F32)


def normalise(values):
    center = values - jnp.mean(values, axis=-1, keepdims=True)
    spread = jnp.mean(center * center, axis=-1, keepdims=True)
    inverse = lax.rsqrt(spread + EPSILON)
    return center * inverse, inverse


def norm_back(upstream, hat, inverse, gain):
    scaled = upstream * gain
    mean_one = jnp.mean(scaled, axis=-1, keepdims=True)
    mean_two = jnp.mean(scaled * hat, axis=-1, keepdims=True)
    return (scaled - mean_one - hat * mean_two) * inverse


UNROLL = True


def loop(count, body):
    if UNROLL:
        for step in range(count):
            body(step, 0)
    else:
        lax.fori_loop(0, count, body, 0)


def block_at(index):
    return pl.ds(pl.multiple_of(index * HALF, HALF), HALF)


def lanes_at(index, size):
    if isinstance(index, int):
        return pl.ds(index * size, size)
    return pl.ds(pl.multiple_of(index * size, size), size)


def vmem_call(
    kernel, out_shape, scratch, flops, in_vmem, smem=0, transcendentals=0, far_outs=(),
    limit=16,
):
    specs = [pl.BlockSpec(memory_space=pltpu.VMEM)] * in_vmem
    specs = [pl.BlockSpec(memory_space=pltpu.SMEM)] * smem + specs
    return pl.pallas_call(
        kernel,
        out_shape=out_shape,
        in_specs=specs,
        out_specs=[
            pl.BlockSpec(memory_space=pl.ANY if index in far_outs else pltpu.VMEM)
            for index in range(len(out_shape))
        ],
        scratch_shapes=scratch,
        compiler_params=pltpu.CompilerParams(vmem_limit_bytes=limit * MIB),
        cost_estimate=pl.CostEstimate(
            flops=flops, bytes_accessed=8 * 2**20, transcendentals=transcendentals
        ),
    )


def packed_weights(out_weight, up_weight, down_weight):
    def kernel(out_weight, up_weight, down_weight, pack):
        pack[OUT_AT:UP_AT, :] = out_weight[...]
        for j in range(HIDDEN // WIDTH):
            pack[UP_AT + 96 * j : UP_AT + 96 * (j + 1), :] = up_weight[
                :, j * WIDTH : (j + 1) * WIDTH
            ]
        pack[DOWN_AT:PACK_ROWS, :] = down_weight[...]

    return vmem_call(
        kernel, [jax.ShapeDtypeStruct((PACK_ROWS, WIDTH), BF)], [], 10**6, 3, limit=56
    )(out_weight, up_weight, down_weight)[0]


def normalised_rows(tokens):
    def kernel(tokens, hat):
        hat[...] = normalise(tokens[...].astype(F32))[0].astype(BF)

    return vmem_call(
        kernel, [jax.ShapeDtypeStruct((ROWS, WIDTH), BF)], [], 10**6, 1, limit=56
    )(tokens)[0]


def head_forward_kernel(
    order, where, blocks, weight, bias, gain, shift,
    packed, hats, query, key, value, query_t, key_t, out_t, lse,
    value_t, projected,
):
    at_z, at_x = where[0] // SIDE, lax.rem(where[0], SIDE)

    for half, offsets, block in blocks:
        count = len(offsets)
        hat_low = block[...].reshape(count * HALF, WIDTH)
        low = (hat_low.astype(F32) * gain[...] + shift[...]).astype(BF)
        made = (dot(low, weight[...]) + bias[...]).astype(BF)
        for n, (dz, dx) in enumerate(offsets):
            place = order[lax.rem(at_z + dz, SIDE) * SIDE + lax.rem(at_x + dx, SIDE)]
            to = block_at(place if half == 0 else 2 * CTX - 1 - place)
            rows = slice(n * HALF, (n + 1) * HALF)
            hats[to, :] = hat_low[rows]
            query[to, :] = made[rows, 0:DEPTH]
            key[to, :] = made[rows, DEPTH : 2 * DEPTH]
            value[to, :] = made[rows, 2 * DEPTH :]

    projected()

    def turn(t, _):
        rows = lanes_at(t, QT)
        for source, target in ((query, query_t), (key, key_t), (value, value_t)):
            target[:, rows] = source[rows, :].astype(F32).T.astype(BF)
        return 0

    lax.fori_loop(0, SEQ // QT, turn, 0)

    def attend(i, _):
        lanes = lanes_at(i, QT)
        queries = query_t[:, lanes]

        def step(j, carry, masked):
            top, total, acc = carry
            rows = lanes_at(j, KT)
            scores = dot(key[rows, :], queries) * SCALE_LOG2
            if masked:
                key_place = j * KT + lax.broadcasted_iota(jnp.int32, (KT, QT), 0)
                query_place = i * QT + lax.broadcasted_iota(jnp.int32, (KT, QT), 1)
                scores = jnp.where(key_place <= query_place, scores, NEGATIVE)
            fresh = jnp.maximum(top, jnp.max(scores, axis=0, keepdims=True))
            raised = jnp.exp2(scores - fresh)
            fade = jnp.exp2(top - fresh)
            total = total * fade + jnp.sum(raised, axis=0, keepdims=True)
            acc = acc * fade + dot(value_t[:, rows], raised.astype(BF))
            return fresh, total, acc

        start = (
            jnp.full((1, QT), NEGATIVE, F32),
            jnp.zeros((1, QT), F32),
            jnp.zeros((DEPTH, QT), F32),
        )
        full = i * QT // KT
        if isinstance(i, int):
            carry = start
            for j in range(full):
                carry = step(j, carry, False)
        else:
            carry = lax.fori_loop(0, full, lambda j, carry: step(j, carry, False), start)
        for extra in range(max(1, QT // KT)):
            carry = step(full + extra, carry, True)
        top, total, acc = carry
        result = acc / total
        out_t[:, lanes] = result
        lse[pl.ds(i, 1), :] = top + jnp.log2(total)
        return 0

    loop(SEQ // QT, attend)


def head_forward(order, where, blocks, weight, bias, gain, shift):
    layout = [(half, offsets) for half, offsets, _ in blocks]

    def kernel(order, where, *refs):
        block_refs, refs = refs[: len(layout)], refs[len(layout) :]
        (
            weight, bias, gain, shift,
            packed, hats_out, query, key, value, query_t, key_t, out_t, lse,
            value_t, out_rows, hats, sem,
        ) = refs
        leave = pltpu.make_async_copy(hats, hats_out, sem.at[0])
        head_forward_kernel(
            order, where,
            [(half, offsets, ref) for (half, offsets), ref in zip(layout, block_refs)],
            weight, bias, gain, shift,
            packed, hats, query, key, value, query_t, key_t, out_t, lse,
            value_t, leave.start,
        )

        def turn_back(t, _):
            rows = lanes_at(t, QT)
            out_rows[rows, :] = out_t[:, rows].T
            return 0

        lax.fori_loop(0, SEQ // QT, turn_back, 0)

        def pack(c, _):
            place = order[c]
            packed[c] = jnp.concatenate(
                [out_rows[block_at(place), :], out_rows[block_at(2 * CTX - 1 - place), :]], axis=1
            ).astype(BF)
            return 0

        lax.fori_loop(0, CTX, pack, 0)
        leave.wait()

    shape = jax.ShapeDtypeStruct
    return vmem_call(
        kernel,
        [
            shape((CTX, HALF, 2 * DEPTH), BF),
            shape((SEQ, WIDTH), BF),
            shape((SEQ, DEPTH), BF),
            shape((SEQ, DEPTH), BF),
            shape((SEQ, DEPTH), BF),
            shape((DEPTH, SEQ), BF),
            shape((DEPTH, SEQ), BF),
            shape((DEPTH, SEQ), F32),
            shape((SEQ // QT, QT), F32),
        ],
        [
            pltpu.VMEM((DEPTH, SEQ), BF),
            pltpu.VMEM((SEQ, DEPTH), F32),
            pltpu.VMEM((SEQ, WIDTH), BF),
            pltpu.SemaphoreType.DMA((1,)),
        ],
        2 * 10**9,
        len(blocks) + 4,
        smem=2,
        transcendentals=3 * 10**6,
        far_outs=(1,),
        limit=56,
    )(order, where, *[block for _, _, block in blocks], weight, bias, gain, shift)


def head_backward(order, upstream, query, key, value, query_t, key_t, out_t, lse):
    def kernel(
        order, upstream, query, key, value, query_t, key_t, out_t, lse,
        packed, low_rows, bias_grad,
        grad_out, grad_out_t, delta, grad_q_t, grad_k, grad_v, rows_low,
    ):
        def unpack(c, _):
            place = order[c]
            grad_out[block_at(place), :] = upstream[c][:, :DEPTH]
            grad_out[block_at(2 * CTX - 1 - place), :] = upstream[c][:, DEPTH:]
            return 0

        lax.fori_loop(0, CTX, unpack, 0)

        def prepare(t, _):
            rows = lanes_at(t, QT)
            turned = grad_out[rows, :].astype(F32).T
            grad_out_t[:, rows] = turned.astype(BF)
            delta[pl.ds(t, 1), :] = jnp.sum(turned * out_t[:, rows], axis=0, keepdims=True)
            grad_q_t[:, rows] = jnp.zeros((DEPTH, QT), F32)
            grad_k[rows, :] = jnp.zeros((QT, DEPTH), F32)
            grad_v[rows, :] = jnp.zeros((QT, DEPTH), F32)
            return 0

        lax.fori_loop(0, SEQ // QT, prepare, 0)

        def one_query_tile(i, _):
            lanes = lanes_at(i, QT)

            def step(j, masked):
                rows = lanes_at(j, KT)
                scores = dot(key[rows, :], query_t[:, lanes]) * SCALE_LOG2
                probs = jnp.exp2(scores - lse[pl.ds(i, 1), :])
                if masked:
                    key_place = j * KT + lax.broadcasted_iota(jnp.int32, (KT, QT), 0)
                    query_place = i * QT + lax.broadcasted_iota(jnp.int32, (KT, QT), 1)
                    probs = jnp.where(key_place <= query_place, probs, 0.0)
                slopes = dot(value[rows, :], grad_out_t[:, lanes])
                grad_scores = (probs * (slopes - delta[pl.ds(i, 1), :])).astype(BF)
                grad_v[rows, :] += dot(probs.astype(BF), grad_out[lanes, :])
                grad_k[rows, :] += dot(grad_scores, query[lanes, :])
                grad_q_t[:, lanes] += dot(key_t[:, rows], grad_scores)

            full = i * QT // KT

            def body(j, _):
                step(j, False)
                return 0

            (loop(full, body) if isinstance(i, int) else lax.fori_loop(0, full, body, 0))
            for extra in range(max(1, QT // KT)):
                step(full + extra, True)
            return 0

        loop(SEQ // QT, one_query_tile)

        def finish(t, sums):
            rows = lanes_at(t, QT)
            low_q = (grad_q_t[:, rows].T * (DEPTH ** -0.5)).astype(BF)
            low_k = (grad_k[rows, :] * (DEPTH ** -0.5)).astype(BF)
            low_v = grad_v[rows, :].astype(BF)
            joined = jnp.concatenate(
                [low_q.astype(F32), low_k.astype(F32), low_v.astype(F32)], axis=1
            )
            rows_low[rows, :] = joined
            low_rows[rows, :] = joined.astype(BF)
            return sums + jnp.sum(joined, axis=0, keepdims=True)

        sums = lax.fori_loop(0, SEQ // QT, finish, jnp.zeros((1, 3 * DEPTH), F32))
        bias_grad[...] = sums

        def pack(c, _):
            place = order[c]
            upper = rows_low[block_at(place), :]
            lower = rows_low[block_at(2 * CTX - 1 - place), :]
            pieces = []
            for part in range(3):
                lanes = slice(part * DEPTH, (part + 1) * DEPTH)
                pieces += [upper[:, lanes], lower[:, lanes]]
            packed[c] = jnp.concatenate(pieces, axis=1).astype(BF)
            return 0

        lax.fori_loop(0, CTX, pack, 0)

    shape = jax.ShapeDtypeStruct
    return vmem_call(
        kernel,
        [
            shape((CTX, HALF, 6 * DEPTH), BF),
            shape((SEQ, 3 * DEPTH), BF),
            shape((1, 3 * DEPTH), F32),
        ],
        [
            pltpu.VMEM((SEQ, DEPTH), BF),
            pltpu.VMEM((DEPTH, SEQ), BF),
            pltpu.VMEM((SEQ // QT, QT), F32),
            pltpu.VMEM((DEPTH, SEQ), F32),
            pltpu.VMEM((SEQ, DEPTH), F32),
            pltpu.VMEM((SEQ, DEPTH), F32),
            pltpu.VMEM((SEQ, 3 * DEPTH), F32),
        ],
        4 * 10**9,
        8,
        smem=1,
        transcendentals=3 * 10**6,
        limit=56,
    )(order, upstream, query, key, value, query_t, key_t, out_t, lse)


def unpack_heads(ref, lanes):
    upper, lower = [], []
    for head in range(HEADS):
        slot = ref[head][:, lanes : lanes + 2 * DEPTH].astype(F32)
        upper.append(slot[:, :DEPTH])
        lower.append(slot[:, DEPTH:])
    return jnp.concatenate(
        [jnp.concatenate(upper, axis=1), jnp.concatenate(lower, axis=1)], axis=0
    ).astype(BF)


def gelu_parts(values):
    slope = 0.7978845608028654
    cubic = 0.044715
    squared = values * values
    bend = jnp.tanh(slope * (values + cubic * squared * values))
    active = 0.5 * values * (1.0 + bend)
    grad = 0.5 * (1.0 + bend) + 0.5 * values * (1.0 - bend * bend) * slope * (
        1.0 + 3.0 * cubic * squared
    )
    return active, grad


def pack_piece(source, held, sems, index):
    if index == 0:
        rows = (slice(0, FSDP), pl.ds(OUT_AT, 96))
    elif index <= 4:
        rows = (slice(0, FSDP), pl.ds(UP_AT + 96 * (index - 1), 96))
    else:
        rows = (pl.ds(2 * (index - 5), 2), pl.ds(DOWN_AT, 384))
    return pltpu.make_async_copy(source.at[rows], held.at[rows], sems.at[index])


def feed_forward(pack, tokens, heads_out, cotangent, out_bias, gain, shift, up_bias, down_bias):
    def kernel(
        source, tokens, heads_out, cotangent, out_bias, gain, shift, up_bias, down_bias,
        mixed, grads_out, grad_heads, grad_residual, vector_sums, up_sums,
        pack, sems, mix_grad, out_sems,
    ):
        order = [0] + [index for j in range(4) for index in (1 + j, 5 + j)]
        copies = {index: pack_piece(source, pack, sems, index) for index in order}
        for index in order:
            copies[index].start()

        def send(index):
            copy = pack_piece(mix_grad, grads_out, out_sems, index)
            copy.start()
            return copy

        sent = []
        inputs = tokens[...].astype(F32)
        result_grad = cotangent[...]
        attended_low = unpack_heads(heads_out, 0)
        copies[0].wait()
        w_out = pack[:, OUT_AT:UP_AT, :].reshape(WIDTH, WIDTH)
        residual = inputs + dot(attended_low, w_out) + out_bias[...]
        hat, inverse = normalise(residual)
        low = (hat * gain[...] + shift[...]).astype(BF)
        low_t = low.T
        total = residual + down_bias[...]
        grad_normed = jnp.zeros((ROWS, WIDTH), F32)
        for j in range(HIDDEN // WIDTH):
            lanes = slice(j * WIDTH, (j + 1) * WIDTH)
            copies[1 + j].wait()
            w_up = pack[:, UP_AT + 96 * j : UP_AT + 96 * (j + 1), :].reshape(WIDTH, WIDTH)
            hidden = dot(low, w_up) + up_bias[:, lanes]
            copies[5 + j].wait()
            w_down = pack[2 * j : 2 * j + 2, DOWN_AT:PACK_ROWS, :].reshape(WIDTH, WIDTH)
            upstream = dot_nt(result_grad, w_down)
            acted, slope = gelu_parts(hidden)
            acted = acted.astype(BF)
            mix_grad[2 * j : 2 * j + 2, DOWN_AT:, :] = (
                dot(acted.T, result_grad).astype(BF).reshape(2, 384, WIDTH)
            )
            sent.append(send(5 + j))
            total = total + dot(acted, w_down)
            pre = (upstream * slope).astype(BF)
            mix_grad[:, UP_AT + 96 * j : UP_AT + 96 * (j + 1), :] = (
                dot(low_t, pre).astype(BF).reshape(FSDP, 96, WIDTH)
            )
            sent.append(send(1 + j))
            up_sums[:, lanes] = jnp.sum(pre.astype(F32), axis=0, keepdims=True)
            grad_normed = grad_normed + dot_nt(pre, w_up)
        mixed[...] = total.astype(BF)
        back = result_grad.astype(F32) + norm_back(grad_normed, hat, inverse, gain[...])
        grad_residual[...] = back
        branch = back.astype(BF)
        mix_grad[:, OUT_AT:UP_AT, :] = (
            dot(attended_low.T, branch).astype(BF).reshape(FSDP, 96, WIDTH)
        )
        sent.append(send(0))
        grad_attended = dot_nt(branch, w_out)
        for head in range(HEADS):
            lanes = slice(head * DEPTH, (head + 1) * DEPTH)
            grad_heads[head] = jnp.concatenate(
                [grad_attended[:HALF, lanes], grad_attended[HALF:, lanes]], axis=1
            ).astype(BF)
        for head in range(HEADS, CTX):
            grad_heads[head] = jnp.zeros((HALF, 2 * DEPTH), BF)
        vector_sums[0:1, :] = jnp.sum(branch.astype(F32), axis=0, keepdims=True)
        vector_sums[1:2, :] = jnp.sum(grad_normed * hat, axis=0, keepdims=True)
        vector_sums[2:3, :] = jnp.sum(grad_normed, axis=0, keepdims=True)
        vector_sums[3:4, :] = jnp.sum(result_grad.astype(F32), axis=0, keepdims=True)
        for copy in sent:
            copy.wait()

    shape = jax.ShapeDtypeStruct
    outs = [
        shape((ROWS, WIDTH), BF),
        shape((FSDP, PACK_ROWS, WIDTH), BF),
        shape((CTX, HALF, 2 * DEPTH), BF),
        shape((ROWS, WIDTH), F32),
        shape((4, WIDTH), F32),
        shape((1, HIDDEN), F32),
    ]
    return pl.pallas_call(
        kernel,
        out_shape=outs,
        in_specs=[pl.BlockSpec(memory_space=pl.ANY)]
        + [pl.BlockSpec(memory_space=pltpu.VMEM)] * 8,
        out_specs=[
            pl.BlockSpec(memory_space=pl.ANY if index == 1 else pltpu.VMEM)
            for index in range(len(outs))
        ],
        scratch_shapes=[
            pltpu.VMEM((FSDP, PACK_ROWS, WIDTH), BF),
            pltpu.SemaphoreType.DMA((9,)),
            pltpu.VMEM((FSDP, PACK_ROWS, WIDTH), BF),
            pltpu.SemaphoreType.DMA((9,)),
        ],
        compiler_params=pltpu.CompilerParams(vmem_limit_bytes=56 * MIB),
        cost_estimate=pl.CostEstimate(
            flops=4 * 10**9, bytes_accessed=24 * 2**20, transcendentals=4 * 10**5
        ),
    )(pack, tokens, heads_out, cotangent, out_bias, gain, shift, up_bias, down_bias)


def token_gradient(weight, tokens, heads_grad, gain, grad_residual):
    def kernel(weight, tokens, heads_grad, gain, grad_residual, tokens_grad):
        hat, inverse = normalise(tokens[...].astype(F32))
        projected = jnp.concatenate(
            [unpack_heads(heads_grad, 2 * DEPTH * part) for part in range(3)], axis=1
        )
        grad_normed = dot_nt(projected, weight[...])
        tokens_grad[...] = grad_residual[...] + norm_back(grad_normed, hat, inverse, gain[...])

    return vmem_call(
        kernel,
        [jax.ShapeDtypeStruct((ROWS, WIDTH), F32)],
        [],
        2 * ROWS * WIDTH * 3 * WIDTH,
        5,
    )(weight, tokens, heads_grad, gain, grad_residual)[0]


def early_slots(where, hats, rows, weight, gain, shift, bias_sums, vector_sums, up_sums):
    def kernel(where, hats, rows, weight, gain, shift, bias_sums, vector_sums, up_sums, slots):
        place = where[0]

        made = dot_tn(rows[...], hats[...])
        column = jnp.broadcast_to(bias_sums[...], (8, 3 * DEPTH)).T[:, :1]
        weight_t = weight[...].astype(F32).T
        first_gain = jnp.sum(weight_t * made, axis=0, keepdims=True)
        first_shift = jnp.sum(weight_t * column, axis=0, keepdims=True)
        weight_grad = (made * gain[...] + column * shift[...]).T
        for owner in range(FSDP):
            slots[owner, :96, :] = weight_grad[96 * owner : 96 * (owner + 1)].astype(BF)

        tall = jnp.zeros((2, 3 * DEPTH), F32)
        bias_rows = []
        for part in (0, 2):
            piece = bias_sums[:, part * DEPTH : (part + 1) * DEPTH]
            for head in range(HEADS):
                bias_rows.append(jnp.where(place == head, piece, 0.0))
        for owner in range(FSDP):
            lanes = slice(96 * owner, 96 * (owner + 1))
            values = dict(
                first_gain=first_gain[:, lanes],
                first_shift=first_shift[:, lanes],
                qv_bias=jnp.concatenate(bias_rows[3 * owner : 3 * owner + 3], axis=1),
                out_bias=vector_sums[0:1, lanes],
                second_gain=vector_sums[1:2, lanes],
                second_shift=vector_sums[2:3, lanes],
                up_bias=up_sums[:, 384 * owner : 384 * (owner + 1)],
                down_bias=vector_sums[3:4, lanes],
            )
            line = jnp.concatenate([values[name] for name, _ in VECTORS], axis=1)
            pieces = [line[:, 192 * r : 192 * (r + 1)] for r in range(6)] + [tall]
            slots[owner, 96:, :] = jnp.concatenate(pieces, axis=0).astype(BF)

    return vmem_call(
        kernel,
        [jax.ShapeDtypeStruct((FSDP, 104, 3 * DEPTH), BF)],
        [],
        2 * SEQ * WIDTH * 3 * DEPTH,
        8,
        smem=1,
    )(where, hats, rows, weight, gain, shift, bias_sums, vector_sums, up_sums)[0]


def early_sums(parts):
    def kernel(own, left, right, far, out):
        total = (
            own[...].astype(F32) + left[...].astype(F32) + right[...].astype(F32)
            + far[...].astype(F32)
        )
        head = jnp.concatenate([total[24 * k : 24 * (k + 1)] for k in range(4)], axis=1)
        line = jnp.concatenate([total[96:104], jnp.zeros((8, 9 * DEPTH), F32)], axis=1)
        joined = jnp.concatenate([head, line], axis=0).astype(BF)
        for target in range(CTX):
            out[target] = joined

    return vmem_call(kernel, [jax.ShapeDtypeStruct((CTX, EARLY_ROWS, WIDTH), BF)], [], 10**6, 4)(*parts)[0]


def early_grads(pieces):
    def kernel(pieces, grad_qkv, *vector_refs):
        lines = jnp.zeros((8, 3 * DEPTH), F32)
        heads = []
        for n in range(CTX):
            piece = pieces[n].astype(F32)
            lines = lines + piece[24:, : 3 * DEPTH]
            if n < HEADS:
                heads.append(
                    jnp.concatenate(
                        [piece[:24, 192 * k : 192 * (k + 1)] for k in range(4)], axis=0
                    )
                )
        line = jnp.concatenate([lines[r : r + 1] for r in range(6)], axis=1)
        at = 0
        for ref, (_, width) in zip(vector_refs, VECTORS):
            ref[...] = line[:, at : at + width]
            at += width
        for part in range(3):
            grad_qkv[:, part * WIDTH : (part + 1) * WIDTH] = jnp.concatenate(
                [head[:, part * DEPTH : (part + 1) * DEPTH] for head in heads], axis=1
            )

    shape = jax.ShapeDtypeStruct
    return vmem_call(
        kernel,
        [shape((96, 3 * WIDTH), F32)] + [shape((1, width), F32) for _, width in VECTORS],
        [],
        10**6,
        1,
    )(pieces)


def last_pieces(parts):
    def kernel(parts, out):
        total = parts[0].astype(F32)
        for source in range(1, CTX):
            total = total + parts[source].astype(F32)
        total = total.astype(BF)
        for target in range(CTX):
            out[target] = total

    return vmem_call(
        kernel, [jax.ShapeDtypeStruct((CTX, SHARE, WIDTH), BF)], [], 10**6, 1
    )(parts)[0]


def last_grads(pieces):
    def kernel(pieces, grad_out, grad_up, grad_down):
        shard = jnp.concatenate([pieces[n].astype(F32) for n in range(CTX)], axis=0)
        grad_out[...] = shard[OUT_AT:UP_AT]
        for j in range(HIDDEN // WIDTH):
            grad_up[:, j * WIDTH : (j + 1) * WIDTH] = shard[UP_AT + 96 * j : UP_AT + 96 * (j + 1)]
        grad_down[...] = shard[DOWN_AT:]

    shape = jax.ShapeDtypeStruct
    return vmem_call(
        kernel,
        [shape((96, WIDTH), F32), shape((96, HIDDEN), F32), shape((384, WIDTH), F32)],
        [],
        10**6,
        1,
    )(pieces)


def swap(slots, axes):
    return lax.all_to_all(slots, axes, 0, 0, tiled=True)


def shift_by(value, z=0, x=0, y=0, core=0):
    pairs = []
    for at_z in range(SIDE):
        for at_x in range(SIDE):
            for at_y in range(SIDE):
                for at_core in range(2):
                    source = (at_z * SIDE + at_x) * FSDP + at_y * 2 + at_core
                    to_ctx = (at_z + z) % SIDE * SIDE + (at_x + x) % SIDE
                    to_fsdp = (at_y + y) % SIDE * 2 + (at_core + core) % 2
                    pairs.append((source, to_ctx * FSDP + to_fsdp))
    return lax.ppermute(value, ("ctx", "fsdp"), pairs)


def gather_rows(values):
    blocks = []
    steps = (0, SIDE - 1, 1, 2)
    for half, first, second in ((0, "x", "z"), (1, "z", "x")):
        mine = values[half * HALF : (half + 1) * HALF]
        near = jnp.stack([mine] + [shift_by(mine, **{first: by}) for by in (1, -1, 2)])
        ahead, behind = shift_by(near, **{second: 1}), shift_by(near, **{second: -1})
        far_one = shift_by(ahead[:2], **{second: 1})
        far_two = shift_by(behind[2:], **{second: -1})

        def offsets(across, along):
            return [(across, by) if second == "z" else (by, across) for by in along]

        blocks += [
            (half, offsets(0, steps), near),
            (half, offsets(SIDE - 1, steps), ahead),
            (half, offsets(1, steps), behind),
            (half, offsets(2, steps[:2]), far_one),
            (half, offsets(2, steps[2:]), far_two),
        ]
    return blocks


def gather_small(piece):
    at = lax.axis_index("fsdp")
    at_y, at_core = at // 2, at % 2
    ring = jnp.stack(
        [piece, shift_by(piece, y=-1), shift_by(piece, y=2), shift_by(piece, y=1)]
    )
    other = shift_by(ring, core=1)
    first = jnp.where(at_core == 0, ring, other)
    second = jnp.where(at_core == 0, other, ring)
    both = jnp.stack([first, second], axis=1)
    turned = lax.dynamic_slice_in_dim(
        jnp.concatenate([both, both], axis=0), (SIDE - at_y) % SIDE, SIDE, 0
    )
    return turned.reshape((FSDP,) + piece.shape)


def scatter_small(slots):
    at = lax.axis_index("fsdp")
    at_y, at_core = at // 2, at % 2
    pairs = slots.reshape((SIDE, 2) + slots.shape[1:])
    mine = jnp.where(at_core == 0, pairs[:, 0], pairs[:, 1])
    theirs = jnp.where(at_core == 0, pairs[:, 1], pairs[:, 0])
    both = (mine.astype(F32) + shift_by(theirs, core=1).astype(F32)).astype(BF)

    def slot(by):
        return lax.dynamic_index_in_dim(both, (at_y + by) % SIDE, 0, keepdims=False)

    return [slot(0)] + [shift_by(slot(by), y=by) for by in (1, -1, 2)]


def local(
    tokens, cotangent, pair_order, first_gain, first_shift, qkv_weight, qv_bias, out_weight,
    out_bias, second_gain, second_shift, up_weight, up_bias, down_weight, down_bias,
):
    my_tokens, my_cotangent = tokens[0], cotangent[0]
    place = lax.axis_index("ctx")
    where = place.reshape(1).astype(jnp.int32)
    head = place % HEADS
    shards = dict(
        first_gain=first_gain, first_shift=first_shift, qv_bias=qv_bias, out_bias=out_bias,
        second_gain=second_gain, second_shift=second_shift, up_bias=up_bias, down_bias=down_bias,
    )

    with jax.named_scope("gather_tokens"):
        hat = normalised_rows(my_tokens)
        blocks = gather_rows(hat)
    with jax.named_scope("gather_weights"):
        out_weight, up_weight, down_weight, _ = lax.optimization_barrier(
            (out_weight, up_weight, down_weight, hat)
        )
        pack = packed_weights(out_weight, up_weight, down_weight)
        pack = lax.all_gather(pack, "fsdp", axis=0, tiled=False)
    with jax.named_scope("gather_small"):
        head_columns = jnp.concatenate(
            [
                lax.dynamic_slice_in_dim(qkv_weight, part * WIDTH + head * DEPTH, DEPTH, 1)
                for part in range(3)
            ],
            axis=1,
        )
        vectors = jnp.concatenate([shards[name] for name, _ in VECTORS]).reshape(6, 3 * DEPTH)
        small = gather_small(
            jnp.concatenate([head_columns, vectors, jnp.zeros((10, 3 * DEPTH), BF)], axis=0)
        )
        w_head = small[:, :96].reshape(WIDTH, 3 * DEPTH)
        vectors = small[:, 96:102].reshape(FSDP, VECTOR_WIDTH).astype(F32)
        whole, at = {}, 0
        for name, width in VECTORS:
            whole[name] = vectors[:, at : at + width].reshape(1, FSDP * width)
            at += width
        head_bias = jnp.concatenate(
            [
                lax.dynamic_slice_in_dim(whole["qv_bias"], head * DEPTH, DEPTH, 1),
                jnp.zeros((1, DEPTH), F32),
                lax.dynamic_slice_in_dim(whole["qv_bias"], WIDTH + head * DEPTH, DEPTH, 1),
            ],
            axis=1,
        )

    with jax.named_scope("attention"):
        packed, hats, query, key, value, query_t, key_t, out_t, lse = head_forward(
            pair_order, where, blocks, w_head, head_bias, whole["first_gain"],
            whole["first_shift"],
        )
        heads_out = swap(packed, "ctx")

    with jax.named_scope("feed_forward"):
        mixed, mix_grad, grad_heads, grad_residual, vector_sums, up_sums = feed_forward(
            pack, my_tokens, heads_out, my_cotangent, whole["out_bias"], whole["second_gain"],
            whole["second_shift"], whole["up_bias"], whole["down_bias"],
        )
        mix_shard = lax.psum_scatter(mix_grad, "fsdp", scatter_dimension=0, tiled=False)
        heads_up = swap(grad_heads, "ctx")

    with jax.named_scope("attention_back"):
        packed_grad, low_rows, bias_sums = head_backward(
            pair_order, heads_up, query, key, value, query_t, key_t, out_t, lse
        )
        heads_grad = swap(packed_grad, "ctx")

    with jax.named_scope("early_grads"):
        early = early_sums(
            scatter_small(
                early_slots(
                    where, hats, low_rows, w_head, whole["first_gain"], whole["first_shift"],
                    bias_sums, vector_sums, up_sums,
                )
            )
        )
        early, heads_grad = lax.optimization_barrier((early, heads_grad))
        early = swap(early, "ctx")

    with jax.named_scope("sum_over_ctx"):
        slots = mix_shard.reshape(CTX, SHARE, WIDTH)
        slots, early = lax.optimization_barrier((slots, early))
        parts = swap(slots, "ctx")
        shares, early = lax.optimization_barrier((last_pieces(parts), early))
        grad_out, grad_up, grad_down = last_grads(swap(shares, "ctx"))
        grad_qkv, *vector_grads = early_grads(early)
        grads = {
            name: grad.reshape(width) for grad, (name, width) in zip(vector_grads, VECTORS)
        }

    with jax.named_scope("token_gradient"):
        late_weight, heads_grad = lax.optimization_barrier((qkv_weight, heads_grad))
        w_qkv = lax.all_gather(late_weight, "fsdp", axis=0, tiled=True)
        tokens_grad = token_gradient(
            w_qkv, my_tokens, heads_grad, whole["first_gain"], grad_residual
        )

    return (
        mixed[None], tokens_grad[None], grads["first_gain"], grads["first_shift"], grad_qkv,
        grads["qv_bias"], grad_out, grads["out_bias"], grads["second_gain"],
        grads["second_shift"], grad_up, grads["up_bias"], grad_down, grads["down_bias"],
    )


def solution(mesh):
    split, vector = P("fsdp", "ctx", None), P("fsdp")
    matrix = P("fsdp", None)
    in_specs = (
        split, split, P(), vector, vector, matrix, vector, matrix, vector, vector, vector,
        matrix, vector, matrix, vector,
    )
    out_specs = (
        split, split, vector, vector, matrix, vector, matrix, vector, vector, vector, matrix,
        vector, matrix, vector,
    )
    return jax.shard_map(local, mesh=mesh, in_specs=in_specs, out_specs=out_specs, check_vma=False)
```
